32 devices in a mesh: dp: 16 (over z, x, core), mp: 2 (over y).
Axes of the slice: x: 2, y: 2, z: 4, core: 2. Of those that a mesh axis runs over, the one named last changes fastest.
Arguments:
- tokens: bfloat16 [64, 512, 512], P(('dp', 'mp')), may hold values from -6 to 6
- memory: bfloat16 [64, 512, 512], P('dp'), may hold values from -6 to 6
- neighbours: bfloat16 [64, 512, 4, 512], P(('dp', 'mp')), may hold values from -6 to 6
- neighbour_ids: int32 [64, 512, 4], P(('dp', 'mp')), may hold values from 0 to 267734
- doc_starts: int32 [64], P('dp'), may hold values 0 or 1
- bin_edges: int32 [129], replicated, may hold values from 0 to 267735, as said below
- w_query: bfloat16 [512, 512], P(None, 'mp'), may hold values from -0.25 to 0.25
- w_key: bfloat16 [512, 512], P(None, 'mp'), may hold values from -0.25 to 0.25
- w_value: bfloat16 [512, 512], P(None, 'mp'), may hold values from -0.25 to 0.25
- w_out: bfloat16 [512, 512], P('mp'), may hold values from -4 to 4
- w_up: bfloat16 [512, 2048], P(None, 'mp'), may hold values from -0.25 to 0.25
- w_down: bfloat16 [2048, 512], P('mp'), may hold values from -0.125 to 0.125
- gain_attn: float32 [512], replicated, may hold values from 0.5 to 1.5
- gain_ffn: float32 [512], replicated, may hold values from 0.5 to 1.5
- w_gate: float32 [512], replicated, may hold values from -0.25 to 0.25
- cotangent: bfloat16 [64, 512, 512], P(('dp', 'mp')), may hold values from -6 to 6
Outputs:
- result: bfloat16 [64, 512, 512], P(('dp', 'mp'))
- grad_input: bfloat16 [64, 512, 512], P(('dp', 'mp'))
- grad_w_query: float32 [512, 512], P(None, 'mp')
- grad_w_key: float32 [512, 512], P(None, 'mp')
- grad_w_value: float32 [512, 512], P(None, 'mp')
- grad_w_out: float32 [512, 512], P('mp')
- grad_w_up: float32 [512, 2048], P(None, 'mp')
- grad_w_down: float32 [2048, 512], P('mp')
- grad_gain_attn: float32 [512], replicated
- grad_gain_ffn: float32 [512], replicated
- grad_w_gate: float32 [512], replicated
- gate_mean: float32 [], replicated
- gate_hist: float32 [128], replicated
The draws below stay inside these ranges and needn't reach their ends.
Inputs may be any that keep to these rules, and one draw needn't show every extreme that they name: bin_edges[0] is 0, bin_edges[128] is 267735, strictly increasing.
All inputs are finite; a program needn't handle non-finite values. No bound on the sum of `doc_starts` on one device may be relied on, other than what follows from the above.
Results may differ from the reference program's by a relative error of at most 0.015.
The reference program's roundings to bfloat16 on the way count: a program that leaves them out, or rounds other values in their place, can miss the bound.
Values may be sent and summed in bfloat16 or wider, within the bound.
No kernel may reach another device: no remote copies, remote signals or barrier semaphores. Data moves between devices by JAX's collectives and lax.ppermute only.
A program may use at most 192 MiB of HBM per device.

```python
import math
import jax
import jax.numpy as jnp
import numpy as np
from jax import lax

D = 512
HEADS = 8
HEAD = 64
FF = 2048
VOCAB = 267735
SEG = 512
NEIGH = 4
BINS = 128
ROWS = 64


def draw_bin_edges(key, part):
    key = jax.random.fold_in(key, 7)
    stride = VOCAB // (BINS * BINS)
    inner = jnp.arange(1, BINS, dtype=jnp.int32)
    jitter = jax.random.randint(key, (BINS - 1,), 0, stride, dtype=jnp.int32)
    middle = inner * inner * stride + jitter
    return jnp.concatenate([jnp.zeros((1,), jnp.int32), middle, jnp.full((1,), VOCAB, jnp.int32)])


def with_ends(array, rng, least, largest):
    shape = array.shape
    spot = [jax.random.randint(jax.random.fold_in(rng, axis), (), 0, shape[axis]) for axis in range(len(shape))]
    array = array.at[tuple(spot)].set(least)
    longest = shape.index(max(shape))
    spot[longest] = (spot[longest] + 1) % shape[longest]
    return array.at[tuple(spot)].set(largest)


def steps_of(stream_key, extent, shards, smallest, top_value):
    level = 1.0
    for axis_at, shards_of in shards:
        draws = jax.random.uniform(jax.random.fold_in(jax.random.fold_in(stream_key, 6), axis_at), (shards_of,), jnp.float32, smallest / len(shards), top_value / len(shards))
        level = level * jnp.repeat(jnp.exp(draws), extent[axis_at] // shards_of).reshape((-1,) + (1,) * (len(extent) - 1 - axis_at))
    return level


def skewed_wide(rng, dims, amount, slope):
    loads = [min(1 << octave, amount + 1 - (1 << octave)) * (1 << 20) // math.isqrt((1 << octave) ** slope) + 1 for octave in range((amount + 1).bit_length()) if 1 << octave <= amount]
    scale = 1 + sum(loads) // (1 << 30)
    table = np.cumsum(np.array([max(1, weight // scale) for weight in loads]))
    lot = jax.random.randint(jax.random.fold_in(rng, 1), dims, 0, int(table[len(loads) - 1]))
    start = jnp.left_shift(1, jnp.searchsorted(jnp.asarray(table, jnp.int32), lot, side="right").astype(jnp.int32))
    standing = start - 1 + jax.random.randint(jax.random.fold_in(rng, 4), dims, 0, 1 << 30) % jnp.minimum(start, amount + 1 - start)
    return jax.random.permutation(jax.random.fold_in(rng, 2), amount)[standing].astype(jnp.int32)


def noise(own_key, shape, scale, reach, cuts=(), kind=jnp.bfloat16):
    result = scale * jax.random.normal(own_key, shape, jnp.float32)
    if cuts:
        result = result * steps_of(own_key, shape, cuts, -0.22, 0.18)
    return jnp.clip(result, -reach, reach).astype(kind)


def setup_inputs(seed: int = 0) -> dict:
    seeds = jax.random.split(jax.random.key(seed), 17)
    return {
        "tokens": noise(seeds[0], (ROWS, SEG, D), 1.0, 6.0, ((0, 32),)),
        "memory": noise(seeds[1], (ROWS, SEG, D), 1.0, 6.0, ((0, 16),)),
        "neighbours": noise(seeds[2], (ROWS, SEG, NEIGH, D), 1.0, 6.0, ((0, 32),)),
        "neighbour_ids": with_ends(skewed_wide(seeds[3], (ROWS, SEG, NEIGH), VOCAB, 2), jax.random.fold_in(seeds[3], 3), 0, VOCAB - 1).astype(jnp.int32),
        "doc_starts": with_ends((jax.random.randint(seeds[4], (ROWS,), 0, 3) < 1).astype(jnp.int32), jax.random.fold_in(seeds[4], 1), 0, 1),
        "bin_edges": draw_bin_edges(jax.random.fold_in(seeds[16], 71), 0),
        "w_query": noise(seeds[6], (D, D), D ** -0.5, 0.25, ((1, 2),)),
        "w_key": noise(seeds[7], (D, D), D ** -0.5, 0.25, ((1, 2),)),
        "w_value": noise(seeds[8], (D, D), D ** -0.5, 0.25, ((1, 2),)),
        "w_out": noise(seeds[9], (D, D), 2 ** -0.5, 4.0, ((0, 2),)),
        "w_up": noise(seeds[10], (D, FF), D ** -0.5, 0.25, ((1, 2),)),
        "w_down": noise(seeds[11], (FF, D), FF ** -0.5, 0.125, ((0, 2),)),
        "gain_attn": jnp.clip(1.0 + 0.1 * jax.random.normal(seeds[12], (D,), jnp.float32), 0.5, 1.5),
        "gain_ffn": jnp.clip(1.0 + 0.1 * jax.random.normal(seeds[13], (D,), jnp.float32), 0.5, 1.5),
        "w_gate": noise(seeds[14], (D,), D ** -0.5, 0.25, (), jnp.float32),
        "cotangent": noise(seeds[15], (ROWS, SEG, D), 1.0, 6.0, ((0, 32),)),
    }


EPS = 1e-05
HIGH = lax.Precision.HIGHEST

@jax.custom_vjp
def low(v):
    return lax.optimization_barrier(v.astype(jnp.bfloat16)).astype(jnp.float32)

@jax.custom_vjp
def low_back(v):
    return v

def low_keep(v):
    return (low(v), None)

def low_pass(kept, grad):
    return (grad,)

def back_keep(v):
    return (v, None)

def back_low(kept, grad):
    return (low(grad),)
low.defvjp(low_keep, low_pass)
low_back.defvjp(back_keep, back_low)

def both_ways(value):
    return low(low_back(value))

def matmul_high(left, right):
    return jnp.matmul(left, right, precision=HIGH)

def layer_norm(values, gain):
    centre = values - lax.optimization_barrier(jnp.mean(values, -1, keepdims=True))
    spread = lax.optimization_barrier(jnp.mean(centre * centre, -1, keepdims=True))
    return centre * lax.rsqrt(spread + EPS) * gain

def key_mask(length, starts):
    query_pos = lax.broadcasted_iota(jnp.int32, (length, 2 * length), 0)
    key_pos = lax.broadcasted_iota(jnp.int32, (length, 2 * length), 1)
    causal = (key_pos >= length) & (key_pos - length <= query_pos)
    return causal | (key_pos < length) & (starts == 0)

def neighbour_mix(hidden, neighbours, w_gate):
    affinity = jnp.einsum('rtkd,rtd->rtk', neighbours, hidden, precision=HIGH) * hidden.shape[-1] ** (-0.5)
    weights = jax.nn.softmax(affinity, axis=-1)
    recalled = jnp.einsum('rtk,rtkd->rtd', weights, neighbours, precision=HIGH)
    gate = jax.nn.sigmoid(lax.optimization_barrier(jnp.sum(hidden * w_gate, -1)))
    return (hidden + gate[..., None] * recalled, gate)

def layer_rows(param_set, token_block, memory_block, neighbour_block, start_block):
    w_query, w_key, w_value, w_out, w_up, w_down, gain_attn, gain_ffn, w_gate = param_set
    rows, length, width = token_block.shape
    normed = low(layer_norm(token_block, gain_attn))
    mem_normed = low(layer_norm(memory_block, gain_attn))
    kv_input = jnp.concatenate([mem_normed, normed], axis=1)
    query = both_ways(matmul_high(normed, w_query)).reshape(rows, length, HEADS, HEAD)
    keys = both_ways(matmul_high(kv_input, w_key)).reshape(rows, 2 * length, HEADS, HEAD)
    values = both_ways(matmul_high(kv_input, w_value)).reshape(rows, 2 * length, HEADS, HEAD)
    raw = low_back(jnp.einsum('rqhc,rkhc->rhqk', query, keys, precision=HIGH) * HEAD ** (-0.5))
    allowed = key_mask(length, start_block[:, None, None])[:, None]
    scores = jnp.where(allowed, raw, -1e+30)
    top = lax.optimization_barrier(jnp.max(scores, -1, keepdims=True))
    log_total = top + jnp.log(lax.optimization_barrier(jnp.sum(jnp.exp(scores - top), -1, keepdims=True)))
    probs = low(jnp.exp(scores - log_total))
    context = both_ways(jnp.einsum('rhqk,rkhc->rqhc', probs, values, precision=HIGH).reshape(rows, length, width))
    hidden = token_block + low_back(matmul_high(context, w_out))
    mixed, gate = neighbour_mix(hidden, neighbour_block, w_gate)
    ffn_in = low(layer_norm(mixed, gain_ffn))
    pre_act = low_back(matmul_high(ffn_in, w_up))
    activ = low(jax.nn.gelu(pre_act))
    return (mixed + low_back(matmul_high(activ, w_down)), gate)

def reference(tokens, memory, neighbours, neighbour_ids, doc_starts, bin_edges, w_query, w_key, w_value, w_out, w_up, w_down, gain_attn, gain_ffn, w_gate, cotangent):
    params = tuple((member.astype(jnp.float32) for member in (w_query, w_key, w_value, w_out, w_up, w_down, gain_attn, gain_ffn, w_gate)))
    groups = ROWS // 4

    def split_rows(values):
        return values.reshape((groups, 4) + values.shape[1:])
    memory_rows = split_rows(memory.astype(jnp.float32))
    neighbour_rows = split_rows(neighbours.astype(jnp.float32))
    start_rows = split_rows(doc_starts)

    def forward(param_set, token_rows):

        def one_group(blocks):
            return layer_rows(param_set, blocks[0], blocks[1], blocks[2], blocks[3])
        outputs, gates = lax.map(jax.checkpoint(one_group), (split_rows(token_rows), memory_rows, neighbour_rows, start_rows))
        return (outputs.reshape(token_rows.shape), gates.reshape(ROWS, SEG))
    outputs, pull, gates = jax.vjp(forward, params, tokens.astype(jnp.float32), has_aux=True)
    grad_params, grad_tokens = pull(cotangent.astype(jnp.float32))
    low_edge = bin_edges[:-1]
    high_edge = bin_edges[1:]

    def bin_mass(blocks):
        id_block, gate_block = blocks
        inside = ((id_block[..., None] >= low_edge) & (id_block[..., None] < high_edge)).astype(jnp.float32)
        return lax.optimization_barrier(jnp.sum(gate_block[:, :, None, None] * inside, axis=(0, 1, 2)))
    masses = lax.map(bin_mass, (split_rows(neighbour_ids), split_rows(gates)))
    gate_hist = lax.optimization_barrier(jnp.sum(masses, 0)) * (BINS / (ROWS * SEG * NEIGH))
    gate_mean = jnp.mean(gates)
    return (outputs.astype(jnp.bfloat16), grad_tokens.astype(jnp.bfloat16), grad_params[0], grad_params[1], grad_params[2], grad_params[3], grad_params[4], grad_params[5], grad_params[6], grad_params[7], grad_params[8], gate_mean, gate_hist)
```

```python
import jax
import jax.numpy as jnp
from jax import lax
from jax.experimental import pallas as pl
from jax.experimental.pallas import tpu as pltpu
from jax.sharding import PartitionSpec as P

HEAD = 64
NEIGH = 4
BINS = 128
PAIR = 2 * HEAD
QROWS = 256
TILE = 256

EPS = 1e-05
BF16 = jnp.bfloat16
F32 = jnp.float32
VMEM_LIMIT = 56 * 1024 * 1024


def dot(left, right, left_dim=1, right_dim=0):
    return lax.dot_general(
        left, right, (((left_dim,), (right_dim,)), ((), ())), preferred_element_type=F32
    )


def normalize(values):
    centre = values - jnp.mean(values, -1, keepdims=True)
    spread = jnp.mean(centre * centre, -1, keepdims=True)
    rstd = lax.rsqrt(spread + EPS)
    return centre * rstd, rstd


def core_index():
    return lax.rem(lax.axis_index("dp"), 2)


def head_lanes(rows, head):
    lane = lax.broadcasted_iota(jnp.int32, (rows, PAIR), 1)
    return (lane >= head * HEAD) & (lane < (head + 1) * HEAD)


def only_head(block, head):
    return jnp.where(head_lanes(block.shape[0], head), block, jnp.zeros_like(block))


def attend(qkv_ref, p_ref, ctx_ref, length, with_memory):
    mem_keys = pl.ds(length, length)
    values = [only_head(qkv_ref[0, 0, pl.ds(3 * length, 2 * length), :], head) for head in range(2)]
    for first in range(0, length, QROWS):
        rows = pl.ds(first, QROWS)
        seen = first + QROWS
        total = None
        for head in range(2):
            query = only_head(qkv_ref[0, 0, rows, :], head)
            seg = dot(query, qkv_ref[0, 0, pl.ds(2 * length, seen), :], 1, 1)
            at = lax.broadcasted_iota(jnp.int32, (QROWS, seen), 0) + first
            key = lax.broadcasted_iota(jnp.int32, (QROWS, seen), 1)
            seg = jnp.where(key <= at, seg, -1e30)
            top = jnp.max(seg, -1, keepdims=True)
            if with_memory:
                mem = dot(query, qkv_ref[0, 0, mem_keys, :], 1, 1)
                top = jnp.maximum(top, jnp.max(mem, -1, keepdims=True))
                mem = jnp.exp(mem - top)
            seg = jnp.exp(seg - top)
            mass = jnp.sum(seg, -1, keepdims=True)
            if with_memory:
                mass = mass + jnp.sum(mem, -1, keepdims=True)
            part = 1.0 / mass
            seg = (seg * part).astype(BF16)
            p_ref[0, 0, head, rows, pl.ds(length, seen)] = seg
            add = dot(seg, values[head][length : length + seen])
            if with_memory:
                mem = (mem * part).astype(BF16)
                p_ref[0, 0, head, rows, pl.ds(0, length)] = mem
                add = add + dot(mem, values[head][:length])
            total = add if total is None else total + add
        ctx_ref[0, rows, :] = total.astype(BF16)


def forward_body(starts_ref, kv_ref, pack_ref, qkv_ref, p_ref, ctx_ref):
    length = kv_ref.shape[1] // 2
    pair = pl.program_id(1)
    kv = kv_ref[0]
    here = pl.multiple_of(3 * pair * PAIR, PAIR)
    query = dot(kv[length:], pack_ref[:, pl.ds(here, PAIR)]).astype(BF16)
    qkv_ref[0, 0, pl.ds(0, length), :] = (query.astype(F32) * HEAD ** (-0.5)).astype(BF16)
    both = dot(kv, pack_ref[:, pl.ds(here + PAIR, 2 * PAIR)]).astype(BF16)
    qkv_ref[0, 0, pl.ds(length, 2 * length), :] = both[:, :PAIR]
    qkv_ref[0, 0, pl.ds(3 * length, 2 * length), :] = both[:, PAIR:]
    start = starts_ref[lax.axis_index("mp") * pl.num_programs(0) + pl.program_id(0)]

    @pl.when(start == 0)
    def _():
        attend(qkv_ref, p_ref, ctx_ref, length, True)

    @pl.when(start != 0)
    def _():
        attend(qkv_ref, p_ref, ctx_ref, length, False)


def first_forward(
    starts_ref, tok_ref, mem_ref, gain_ref, wq_ref, wk_ref, wv_ref, kv_ref, pack_ref, *outs
):
    length = tok_ref.shape[1]

    @pl.when((pl.program_id(0) == 0) & (pl.program_id(1) == 0))
    def _():
        for i, weight in enumerate((wq_ref, wk_ref, wv_ref)):
            for p in range(2):
                pack_ref[:, pl.ds((3 * p + i) * PAIR, PAIR)] = weight[:, pl.ds(p * PAIR, PAIR)]

    @pl.when(pl.program_id(1) == 0)
    def _():
        gain = gain_ref[...]
        kv_ref[0, pl.ds(0, length), :] = (normalize(mem_ref[0].astype(F32))[0] * gain).astype(BF16)
        kv_ref[0, pl.ds(length, length), :] = (
            normalize(tok_ref[0].astype(F32))[0] * gain
        ).astype(BF16)

    forward_body(starts_ref, kv_ref, pack_ref, *outs)


def second_forward(starts_ref, kv_ref, mine_ref, sibling_ref, pack_ref, *outs):
    rows = mine_ref.shape[0]
    core = core_index()

    @pl.when((pl.program_id(0) == 0) & (pl.program_id(1) == 0))
    def _():
        for block, which in ((mine_ref, core), (sibling_ref, 1 - core)):
            to = pl.ds(pl.multiple_of(which * rows, rows), rows)
            for i in range(3):
                for p in range(2):
                    pack_ref[to, pl.ds((3 * p + i) * PAIR, PAIR)] = block[
                        :, pl.ds((2 * i + p) * PAIR, PAIR)
                    ]

    forward_body(starts_ref, kv_ref, pack_ref, *outs)


def attention_forward(starts, tokens, memory, gain, kv, weights):
    rows, length, width = tokens.shape
    pairs = 2
    pack = (width, 3 * pairs * PAIR)
    outs = [
        jax.ShapeDtypeStruct(pack, BF16),
        jax.ShapeDtypeStruct((rows, pairs, 5 * length, PAIR), BF16),
        jax.ShapeDtypeStruct((rows, pairs, 2, length, 2 * length), BF16),
        jax.ShapeDtypeStruct((rows, length, pairs * PAIR), BF16),
    ]
    out_specs = [
        pl.BlockSpec(pack, lambda r, p: (0, 0)),
        pl.BlockSpec((1, 1, 5 * length, PAIR), lambda r, p: (r, p, 0, 0)),
        pl.BlockSpec((1, 1, 2, length, 2 * length), lambda r, p: (r, p, 0, 0, 0)),
        pl.BlockSpec((1, length, PAIR), lambda r, p: (r, 0, p)),
    ]
    kv_spec = pl.BlockSpec((1, 2 * length, width), lambda r, p: (r, 0, 0))
    in_specs = [pl.BlockSpec(memory_space=pltpu.SMEM)]
    if kv is None:
        body = first_forward
        ins = [tokens, memory, gain]
        in_specs += [
            pl.BlockSpec((1, length, width), lambda r, p: (r, 0, 0)),
            pl.BlockSpec((1, length, width), lambda r, p: (lax.axis_index("mp") * rows + r, 0, 0)),
            pl.BlockSpec((1, width), lambda r, p: (0, 0)),
        ]
        outs = [jax.ShapeDtypeStruct((rows, 2 * length, width), BF16)] + outs
        out_specs = [kv_spec] + out_specs
    else:
        body = second_forward
        ins = [kv]
        in_specs += [kv_spec]
    in_specs += [pl.BlockSpec(w.shape, lambda r, p: (0, 0)) for w in weights]
    return pl.pallas_call(
        body,
        grid=(rows, pairs),
        in_specs=in_specs,
        out_specs=out_specs,
        out_shape=outs,
        compiler_params=pltpu.CompilerParams(vmem_limit_bytes=VMEM_LIMIT),
        cost_estimate=pl.CostEstimate(flops=6 * 10**9, bytes_accessed=16 * 2**20, transcendentals=0),
    )(starts, *ins, *weights)


def gelu_parts(pre):
    c0 = 0.7978845608028654
    c1 = c0 * 0.044715
    square = pre * pre
    part = 0.5 * jnp.tanh(pre * (c1 * square + c0)) + 0.5
    act = pre * part
    return act, part + act * (1.0 - part) * ((6.0 * c1) * square + 2.0 * c0)


def weighted(weights, values):
    return sum(w * v for w, v in zip(weights[1:], values[1:])) + weights[0] * values[0]


def middle_body(
    tok_ref,
    ctx_own_ref,
    ctx_oth_ref,
    nb_ref,
    ids_ref,
    cot_ref,
    up_far,
    down_far,
    out_far,
    mine_far,
    sibling_far,
    edges_ref,
    gains_ref,
    result_ref,
    grad_hidden_ref,
    gctx_own_ref,
    gctx_oth_ref,
    sent_far,
    kept_far,
    sums_ref,
    e_ref,
    hist_ref,
    edge_ref,
    up_ref,
    down_ref,
    out_ref,
    oth_ref,
    stage_ref,
    ffn_in_ref,
    act_ref,
    gpre_ref,
    cots_ref,
    low_ref,
    ctx_ref,
    in_sems,
    out_sems,
):
    step = pl.program_id(0)
    here = pl.ds(pl.multiple_of(step * TILE, TILE), TILE)
    width = tok_ref.shape[-1]
    hidden_units = down_ref.shape[0]
    half = width // 2
    chunks = hidden_units // width
    scale = width ** (-0.5)
    core = core_index()
    copies = [
        pltpu.make_async_copy(far, near, in_sems.at[i])
        for i, (far, near) in enumerate(
            (
                (out_far, out_ref),
                (mine_far, oth_ref.at[core]),
                (sibling_far, oth_ref.at[1 - core]),
                (up_far, up_ref),
                (down_far, down_ref),
            )
        )
    ]

    @pl.when(step == 0)
    def _():
        for copy in copies:
            copy.start()
        sums_ref[...] = jnp.zeros_like(sums_ref)
        hist_ref[...] = jnp.zeros_like(hist_ref)
        edges = edges_ref[...].astype(F32)
        for i in range(2):
            edge_ref[i] = jnp.broadcast_to(edges[:, i : i + BINS], (BINS, BINS)).T
        for copy in copies[:3]:
            copy.wait()

    def other_out():
        at = pl.ds(2 * width, half // 2)
        return jnp.concatenate([oth_ref[0, at, :], oth_ref[1, at, :]], 0)

    wgate = gains_ref[pl.ds(1, 1), :]
    gain = gains_ref[pl.ds(0, 1), :]

    def front():
        ctx_ref[here, pl.ds(0, half)] = ctx_own_ref[0]
        ctx_ref[here, pl.ds(half, half)] = ctx_oth_ref[0]
        cots_ref[here, :] = cot_ref[0]
        hidden = (
            tok_ref[0].astype(F32)
            + dot(ctx_own_ref[0], out_ref[...])
            + dot(ctx_oth_ref[0], other_out())
        )
        affinity = []
        for k in range(NEIGH):
            e = nb_ref[0, :, k, :].astype(F32)
            e_ref[k] = e
            affinity.append(jnp.sum(e * hidden, -1, keepdims=True) * scale)
        top = jnp.maximum(
            jnp.maximum(affinity[0], affinity[1]), jnp.maximum(affinity[2], affinity[3])
        )
        raised = [jnp.exp(a - top) for a in affinity]
        inverse = 1.0 / (raised[0] + raised[1] + raised[2] + raised[3])
        weights = [a * inverse for a in raised]
        gate = jax.nn.sigmoid(jnp.sum(hidden * wgate, -1, keepdims=True))
        recalled = weighted(weights, [e_ref[k] for k in range(NEIGH)])
        mixed = hidden + gate * recalled
        normal, rstd = normalize(mixed)
        ffn_in_ref[here, :] = (normal * gain).astype(BF16)
        return hidden, weights, gate, mixed, normal, rstd

    def feed():
        ffn_in = ffn_in_ref[here, :]
        cot = cot_ref[0]
        down_sum = None
        grad_sum = None
        for side in range(2):
            for c in range(chunks):
                if side == 0:
                    up = up_ref[:, pl.ds(c * width, width)]
                    down = down_ref[pl.ds(c * width, width), :]
                else:
                    part = pl.ds(c * half, half)
                    up = jnp.concatenate([oth_ref[0, part, :], oth_ref[1, part, :]], 0)
                    down = oth_ref[c, pl.ds(width, width), :]
                at = pl.ds((side * chunks + c) * width, width)
                act, slope = gelu_parts(dot(ffn_in, up))
                act = act.astype(BF16)
                gpre = (dot(cot, down, 1, 1) * slope).astype(BF16)
                act_ref[here, at] = act
                gpre_ref[here, at] = gpre
                add = dot(act, down)
                down_sum = add if down_sum is None else down_sum + add
                add = dot(gpre, up, 1, 1)
                grad_sum = add if grad_sum is None else grad_sum + add
        return down_sum, grad_sum

    def back(kept, sums):
        hidden, weights, gate, mixed, normal, rstd = kept
        down_sum, grad_sum = sums
        result_ref[0] = (mixed + down_sum).astype(BF16)
        gain_part = jnp.sum(grad_sum * normal, 0, keepdims=True)
        grad_normal = grad_sum * gain
        grad_mixed = cot_ref[0].astype(F32) + rstd * (
            grad_normal
            - jnp.mean(grad_normal, -1, keepdims=True)
            - normal * jnp.mean(grad_normal * normal, -1, keepdims=True)
        )
        pulls = [
            jnp.sum(grad_mixed * e_ref[k], -1, keepdims=True) for k in range(NEIGH)
        ]
        pulled = weighted(weights, pulls)
        gate_grad = gate * (1.0 - gate) * pulled
        grad_hidden = grad_mixed + gate_grad * wgate
        for k in range(NEIGH):
            grad_hidden = (
                grad_hidden + (scale * gate * weights[k] * (pulls[k] - pulled)) * e_ref[k]
            )
        grad_hidden_ref[0] = grad_hidden
        low = grad_hidden.astype(BF16)
        low_ref[here, :] = low
        gctx_own_ref[0] = dot(low, out_ref[...], 1, 1).astype(BF16)
        gctx_oth_ref[0] = dot(low, other_out(), 1, 1).astype(BF16)
        gate_wide = jnp.broadcast_to(gate, (TILE, BINS)).T
        low_edge = jnp.concatenate([edge_ref[0]] * (TILE // BINS), 1)
        high_edge = jnp.concatenate([edge_ref[1]] * (TILE // BINS), 1)
        mass = jnp.zeros_like(gate_wide)
        for k in range(NEIGH):
            ids = ids_ref[0, pl.ds(k, 1), :].astype(F32)
            mass = mass + jnp.where((ids >= low_edge) & (ids < high_edge), gate_wide, 0.0)
        gate_sum = jnp.sum(jnp.broadcast_to(gate, (TILE, width)), 0, keepdims=True)
        sums_ref[pl.ds(0, 1), :] += gain_part
        sums_ref[pl.ds(1, 1), :] += gate_sum
        sums_ref[pl.ds(2, 1), :] += jnp.sum(gate_grad * hidden, 0, keepdims=True)
        hist_ref[...] += mass

    kept = front()

    @pl.when(step == 0)
    def _():
        for copy in copies[3:]:
            copy.wait()

    back(kept, feed())

    @pl.when(step == pl.num_programs(0) - 1)
    def _():
        sums_ref[pl.ds(3, 1), pl.ds(0, BINS)] = jnp.sum(hist_ref[...].T, 0, keepdims=True)
        moves = []
        for far, which in ((sent_far, 1 - core), (kept_far, core)):
            for side in range(2):
                at = pl.ds(pl.multiple_of((side * chunks + which) * width, width), width)
                here = pl.ds(pl.multiple_of((2 * side + which) * PAIR, PAIR), PAIR)
                for to, left, right in (
                    (pl.ds(0, width), ffn_in_ref[...], gpre_ref[:, at]),
                    (pl.ds(width, width), act_ref[:, at], cots_ref[...]),
                    (pl.ds(2 * width, PAIR), ctx_ref[:, here], low_ref[...]),
                ):
                    slot = len(moves)
                    stage = stage_ref.at[slot // 3, to, :]
                    stage[...] = dot(left, right, 0, 0).astype(BF16)
                    move = pltpu.make_async_copy(stage, far.at[side, to, :], out_sems.at[slot])
                    move.start()
                    moves.append(move)
        for move in moves:
            move.wait()


def middle_layer(tokens, ctx_own, ctx_oth, nb, ids, cot, weights, received, edges, gains):
    rows, length, width = tokens.shape
    hidden_units = weights[1].shape[0]
    steps = length // TILE
    tiles = rows * steps
    count = rows * length
    assert hidden_units == 2 * width

    def place_of(i):
        return i // steps, i % steps

    def tiled(last):
        return pl.BlockSpec((1, TILE, last), lambda i: (*place_of(i), 0))

    def whole(shape):
        return pl.BlockSpec(shape, lambda i: (0,) * len(shape))

    far = pl.BlockSpec(memory_space=pl.ANY)
    return pl.pallas_call(
        middle_body,
        grid=(tiles,),
            in_specs=[
                tiled(width),
                tiled(width // 2),
                tiled(width // 2),
                pl.BlockSpec((1, TILE, NEIGH, width), lambda i: (*place_of(i), 0, 0)),
                pl.BlockSpec(
                    (1, NEIGH, TILE), lambda i: (place_of(i)[0], 0, place_of(i)[1])
                ),
                tiled(width),
                *[far] * 5,
                whole((1, BINS + 1)),
                whole((2, width)),
            ],
            out_specs=[
                tiled(width),
                tiled(width),
                tiled(width // 2),
                tiled(width // 2),
                far,
                far,
                whole((8, width)),
            ],
            scratch_shapes=[
                pltpu.VMEM((NEIGH, TILE, width), F32),
                pltpu.VMEM((BINS, TILE), F32),
                pltpu.VMEM((2, BINS, BINS), F32),
                *[pltpu.VMEM(w.shape, BF16) for w in weights],
                pltpu.VMEM((2, *received[0].shape), BF16),
                pltpu.VMEM((4, 2 * width + PAIR, width), BF16),
                pltpu.VMEM((count, width), BF16),
                pltpu.VMEM((count, 2 * hidden_units), BF16),
                pltpu.VMEM((count, 2 * hidden_units), BF16),
                pltpu.VMEM((count, width), BF16),
                pltpu.VMEM((count, width), BF16),
                pltpu.VMEM((count, width), BF16),
                pltpu.SemaphoreType.DMA((5,)),
                pltpu.SemaphoreType.DMA((12,)),
            ],
        out_shape=[
            jax.ShapeDtypeStruct((rows, length, width), BF16),
            jax.ShapeDtypeStruct((rows, length, width), F32),
            jax.ShapeDtypeStruct((rows, length, width // 2), BF16),
            jax.ShapeDtypeStruct((rows, length, width // 2), BF16),
            jax.ShapeDtypeStruct((2, 2 * width + PAIR, width), BF16),
            jax.ShapeDtypeStruct((2, 2 * width + PAIR, width), BF16),
            jax.ShapeDtypeStruct((8, width), F32),
        ],
        compiler_params=pltpu.CompilerParams(vmem_limit_bytes=VMEM_LIMIT),
        cost_estimate=pl.CostEstimate(flops=15 * 10**9, bytes_accessed=30 * 2**20, transcendentals=0),
    )(tokens, ctx_own, ctx_oth, nb, ids, cot, *weights, *received, edges, gains)


def attend_back(
    head, qkv_ref, p_ref, gctx_ref, ctx_ref, ds_ref, dq_ref, t_ref, dk_ref, dv_ref, with_memory
):
    length = ctx_ref.shape[1]
    grad = only_head(gctx_ref[0], head)
    delta = jnp.sum(grad.astype(F32) * ctx_ref[0].astype(F32), -1, keepdims=True)
    keys = only_head(qkv_ref[0, 0, pl.ds(length, 2 * length), :], head)
    lanes = pl.ds(pl.multiple_of(head * HEAD, HEAD), HEAD)
    for first in range(0, length, QROWS):
        rows = pl.ds(first, QROWS)
        seen = first + QROWS
        spans = [(length, seen)] + ([(0, length)] if with_memory else [])
        total = dq_ref[rows, :]
        for at, span in spans:
            here = pl.ds(at, span)
            probs = p_ref[0, 0, 0, rows, here].astype(F32)
            values = qkv_ref[0, 0, pl.ds(3 * length + at, span), :]
            grad_probs = dot(grad[first : first + QROWS], values, 1, 1)
            ds = (probs * (grad_probs - delta[first : first + QROWS])).astype(BF16)
            ds_ref[rows, here] = ds
            total = total + dot(ds, keys[at : at + span])
        dq_ref[rows, :] = total
    for out_ref, left, right in (
        (dk_ref, t_ref[0, lanes, :], ds_ref),
        (dv_ref, t_ref[1, lanes, :], p_ref.at[0, 0, 0]),
    ):
        if with_memory:
            out_ref[lanes, :length] = dot(left, right[:, :length]).astype(BF16)
        else:
            out_ref[lanes, :length] = jnp.zeros((HEAD, length), BF16)
        for first in range(0, length, QROWS):
            here = pl.ds(length + first, QROWS)
            out_ref[lanes, here] = dot(
                left[:, first:], right[pl.ds(first, length - first), here]
            ).astype(BF16)


def backward_body(
    starts_ref,
    qkv_ref,
    p_ref,
    gctx_ref,
    ctx_ref,
    kv_far,
    pack_ref,
    grads_ref,
    dw_ref,
    gain_ref,
    ds_ref,
    dq_ref,
    t_ref,
    dk_ref,
    dv_ref,
    acc_ref,
    kv_ref,
    sem,
):
    length = ctx_ref.shape[1]
    row = pl.program_id(0)
    head = pl.program_id(1)
    start = starts_ref[lax.axis_index("mp") * pl.num_programs(0) + row]
    fetch = pltpu.make_async_copy(kv_far.at[row], kv_ref, sem)
    args = (qkv_ref, p_ref, gctx_ref, ctx_ref, ds_ref, dq_ref, t_ref, dk_ref, dv_ref)

    @pl.when(head == 0)
    def _():
        fetch.start()
        dq_ref[...] = jnp.zeros_like(dq_ref)
        t_ref[0] = qkv_ref[0, 0, pl.ds(0, length), :].T
        t_ref[1] = gctx_ref[0].T

    @pl.when(start == 0)
    def _():
        attend_back(head, *args, True)

    @pl.when(start != 0)
    def _():
        attend_back(head, *args, False)

    @pl.when(head == 1)
    def _():
        dq_t = (dq_ref[...] * HEAD ** (-0.5)).astype(BF16).T
        grads_ref[0, pl.ds(0, PAIR), :] = dq_t
        grads_ref[0, pl.ds(PAIR, PAIR), :] = dk_ref[:, length:]
        grads_ref[0, pl.ds(2 * PAIR, PAIR), :] = dv_ref[:, length:]
        fetch.wait()
        for i, add in enumerate(
            (
                dot(dq_t, kv_ref[pl.ds(length, length), :]),
                dot(dk_ref[...], kv_ref[...]),
                dot(dv_ref[...], kv_ref[...]),
            )
        ):
            acc_ref[i] = jnp.where(row == 0, add, acc_ref[i] + add)

    @pl.when((head == 1) & (row == pl.num_programs(0) - 1))
    def _():
        part = None
        for i in range(3):
            total = acc_ref[i]
            dw_ref[i] = total.astype(BF16)
            weight = pack_ref[:, pl.ds(i * PAIR, PAIR)].T.astype(F32)
            add = jnp.sum(total * weight, 0, keepdims=True)
            part = add if part is None else part + add
        gain_ref[...] = jnp.broadcast_to(part, gain_ref.shape)


def attention_backward(starts, saved, gctx, kv, sibling):
    pack, qkv, p, ctx = saved
    rows, _, _, length, _ = p.shape
    width = kv.shape[-1]

    def pair():
        return 1 - core_index() if sibling else core_index()

    return pl.pallas_call(
        backward_body,
        grid=(rows, 2),
        in_specs=[
            pl.BlockSpec(memory_space=pltpu.SMEM),
            pl.BlockSpec((1, 1, 5 * length, PAIR), lambda r, h: (r, pair(), 0, 0)),
            pl.BlockSpec((1, 1, 1, length, 2 * length), lambda r, h: (r, pair(), h, 0, 0)),
            pl.BlockSpec((1, length, PAIR), lambda r, h: (r, 0, pair())),
            pl.BlockSpec((1, length, PAIR), lambda r, h: (r, 0, pair())),
            pl.BlockSpec(memory_space=pl.ANY),
            pl.BlockSpec((width, 3 * PAIR), lambda r, h: (0, pair())),
        ],
        out_specs=[
            pl.BlockSpec((1, 3 * PAIR, length), lambda r, h: (r, 0, 0)),
            pl.BlockSpec((3, PAIR, width), lambda r, h: (0, 0, 0)),
            pl.BlockSpec((8, width), lambda r, h: (0, 0)),
        ],
        scratch_shapes=[
            pltpu.VMEM((length, 2 * length), BF16),
            pltpu.VMEM((length, PAIR), F32),
            pltpu.VMEM((2, PAIR, length), BF16),
            pltpu.VMEM((PAIR, 2 * length), BF16),
            pltpu.VMEM((PAIR, 2 * length), BF16),
            pltpu.VMEM((3, PAIR, width), F32),
            pltpu.VMEM((2 * length, width), BF16),
            pltpu.SemaphoreType.DMA,
        ],
        out_shape=[
            jax.ShapeDtypeStruct((rows, 3 * PAIR, length), BF16),
            jax.ShapeDtypeStruct((3, PAIR, width), BF16),
            jax.ShapeDtypeStruct((8, width), F32),
        ],
        compiler_params=pltpu.CompilerParams(vmem_limit_bytes=VMEM_LIMIT),
        cost_estimate=pl.CostEstimate(flops=4 * 10**9, bytes_accessed=8 * 2**20, transcendentals=0),
    )(starts, qkv, p, gctx, ctx, kv, pack)


def input_body(
    tok_ref,
    grad_hidden_ref,
    gain_ref,
    oth_first_ref,
    oth_last_ref,
    own_first_ref,
    own_last_ref,
    oth_pack_ref,
    own_pack_ref,
    out_ref,
):
    core = core_index()
    total = None
    for block, pack, which in (
        (oth_first_ref, oth_pack_ref, 1 - core),
        (oth_last_ref, oth_pack_ref, core),
        (own_first_ref, own_pack_ref, 1 - core),
        (own_last_ref, own_pack_ref, core),
    ):
        here = pl.ds(pl.multiple_of(which * 3 * PAIR, 3 * PAIR), 3 * PAIR)
        add = dot(block[0], pack[:, here], 0, 1)
        total = add if total is None else total + add
    normal, rstd = normalize(tok_ref[0].astype(F32))
    grad = total * gain_ref[...]
    out_ref[0] = (
        grad_hidden_ref[0]
        + rstd
        * (
            grad
            - jnp.mean(grad, -1, keepdims=True)
            - normal * jnp.mean(grad * normal, -1, keepdims=True)
        )
    ).astype(BF16)


def input_grad(tokens, grad_hidden, gain, grads, packs):
    rows, length, width = tokens.shape
    row = pl.BlockSpec((1, length, width), lambda r: (r, 0, 0))

    def whole(array):
        return pl.BlockSpec(array.shape, lambda r: (0, 0))

    return pl.pallas_call(
        input_body,
        grid=(rows,),
        in_specs=[
            row,
            row,
            whole(gain),
            *[pl.BlockSpec((1,) + g.shape[1:], lambda r: (r, 0, 0)) for g in grads],
            *[whole(p) for p in packs],
        ],
        out_specs=row,
        out_shape=jax.ShapeDtypeStruct(tokens.shape, BF16),
        compiler_params=pltpu.CompilerParams(vmem_limit_bytes=VMEM_LIMIT),
        cost_estimate=pl.CostEstimate(flops=2 * 10**9, bytes_accessed=8 * 2**20, transcendentals=0),
    )(tokens, grad_hidden, gain, *grads, *packs)


def finish_body(
    ffn_mine,
    ffn_sibling,
    attn_mine,
    attn_sibling,
    q_far,
    k_far,
    v_far,
    out_far,
    up_far,
    down_far,
    q_ref,
    k_ref,
    v_ref,
    out_ref,
    up_ref,
    down_ref,
    sems,
):
    core = core_index()
    width = up_far.shape[0]
    half = width // 2
    rows = attn_mine.shape[1]
    moves = []

    def pair(mine, sibling):
        return (
            jnp.where(core == 0, mine, sibling).astype(F32),
            jnp.where(core == 0, sibling, mine).astype(F32),
        )

    def move(near, far):
        moves.append(pltpu.make_async_copy(near, far, sems.at[len(moves)]))
        moves[-1].start()

    for x in range(2):
        to = pl.ds(x * half, half)
        for which, part in enumerate(
            pair(ffn_mine[x, pl.ds(0, half), :], ffn_sibling[x, pl.ds(0, half), :])
        ):
            up_ref[to, pl.ds(which * width, width)] = part
        move(up_ref.at[to, :], up_far.at[to, :])
    size = half + PAIR // 2
    for which, low in enumerate(
        zip(*(pair(ffn_mine[x, pl.ds(half, size), :], ffn_sibling[x, pl.ds(half, size), :]) for x in range(2)))
    ):
        first, last = low
        to = pl.ds(which * width, width)
        down_ref[pl.ds(which * width, size), :] = first
        down_ref[pl.ds(which * width + size, width - size), :] = last[: width - size]
        out_ref[pl.ds(which * PAIR, PAIR), :] = last[width - size :]
        move(down_ref.at[to, :], down_far.at[to, :])
    move(out_ref, out_far)
    for i, (near, far) in enumerate(((q_ref, q_far), (k_ref, k_far), (v_ref, v_far))):
        first, last = pair(attn_mine[i], attn_sibling[pl.ds(i * rows, rows), :])
        near[...] = jnp.concatenate([first, last], 0).T
        move(near, far)
    for one in moves:
        one.wait()


def finish(ffn, attn):
    width = ffn[0].shape[-1]
    quarter = attn[0].shape[1]
    shapes = [(width, 2 * quarter)] * 3
    shapes += [(2 * quarter, width), (width, 2 * width), (2 * width, width)]

    def whole(array):
        return pl.BlockSpec(array.shape, lambda i: (0,) * array.ndim)

    return pl.pallas_call(
        finish_body,
        grid=(1,),
        in_specs=[whole(a) for a in (*ffn, *attn)],
        out_specs=[pl.BlockSpec(memory_space=pl.ANY)] * 6,
        scratch_shapes=[pltpu.VMEM(s, F32) for s in shapes] + [pltpu.SemaphoreType.DMA((8,))],
        out_shape=[jax.ShapeDtypeStruct(s, F32) for s in shapes],
        compiler_params=pltpu.CompilerParams(vmem_limit_bytes=VMEM_LIMIT),
    )(*ffn, *attn)


def swap(array, axis, bit):
    size = lax.axis_size(axis)
    return lax.ppermute(array, axis, [(i, i ^ bit) for i in range(size)])


def bit_of(axis, bit):
    return (lax.axis_index(axis) // bit) % 2


def part_of(array, which, dim):
    half = array.shape[dim] // 2
    return lax.dynamic_slice_in_dim(array, which * half, half, dim)


def add_low(left, right):
    return (left.astype(F32) + right.astype(F32)).astype(BF16)


def join(mine, other, bit, dim):
    return jnp.where(
        bit_of("dp", bit) == 0,
        lax.concatenate([mine, other], dim),
        lax.concatenate([other, mine], dim),
    )


def after(value, *others):
    return lax.optimization_barrier((value, *others))[0]


class Chain:
    def __init__(self, array, dim):
        self.pieces = (array,)
        self.dim = dim

    def total(self, cut=lambda piece: piece):
        pieces = [cut(piece) for piece in self.pieces]
        if len(pieces) == 1:
            return pieces[0]
        return sum(piece.astype(F32) for piece in pieces).astype(BF16)

    def pass_on(self, sent, kept, bit, *others):
        self.sent = after(sent, *others)
        self.kept = kept
        self.come = swap(self.sent, "dp", bit)
        return self.sent

    def halve(self, bit, *others):
        mine = bit_of("dp", bit)
        self.sent = after(self.total(lambda p: part_of(p, 1 - mine, self.dim)), *others)
        self.kept = self.total(lambda p: part_of(p, mine, self.dim))
        self.come = swap(self.sent, "dp", bit)
        return self.sent

    def give(self, index, *others):
        self.sent = after(self.total(lambda p: p[index]), *others)
        self.kept = self.total(lambda p: p[1 - index])
        self.dim -= 1
        self.come = swap(self.sent, "mp", 1)
        return self.sent

    def send(self, bit, *others):
        self.sent = self.kept = after(self.total(), *others)
        self.come = swap(self.sent, "dp", bit)
        return self.sent

    def add(self, *others):
        self.come = after(self.come, *others)
        self.pieces = (self.kept, self.come)

    def join(self, bit, *others):
        self.pieces = (join(self.sent, after(self.come, *others), bit, self.dim),)


class Ride:
    def __init__(self, rows):
        self.rows = rows

    def below(self, array):
        left = self.rows
        parts = [array.reshape(-1, array.shape[-1])]
        for _ in range(3):
            part = lax.reduce_precision(left, 8, 7)
            parts.append(part.astype(BF16))
            left = left - part
        spare = -3 * left.shape[0] % 16
        parts.append(jnp.zeros((spare, left.shape[1]), BF16))
        return lax.concatenate(parts, 0)

    def add(self, block, like):
        size = like.size // like.shape[-1]
        count = self.rows.shape[0]
        for i in range(3):
            at = size + i * count
            self.rows = self.rows + block[at : at + count].astype(F32)
        return block[:size].reshape(like.shape)


def shards(
    tokens,
    memory,
    neighbours,
    neighbour_ids,
    doc_starts,
    bin_edges,
    w_query,
    w_key,
    w_value,
    w_out,
    w_up,
    w_down,
    gain_attn,
    gain_ffn,
    w_gate,
    cotangent,
):
    rows, length, width = tokens.shape
    count = rows * length
    dp = lax.axis_size("dp")
    core = bit_of("dp", 1)
    attn_gain = gain_attn.reshape(1, width)
    gains = jnp.stack([gain_ffn, w_gate])
    qkv = (w_query, w_key, w_value)
    far = []
    bit = 2
    while bit < dp:
        far.append(bit)
        bit *= 2

    qkv_sent = lax.concatenate([part_of(w, core, 0) for w in qkv], 1)
    up_part = part_of(w_up, core, 0)
    ffn_sent = lax.concatenate(
        [up_part[:, :width], up_part[:, width:], part_of(w_down, core, 0), part_of(w_out, core, 0)],
        0,
    )
    qkv_mine = swap(qkv_sent, "mp", 1)
    ffn_mine = swap(after(ffn_sent, qkv_sent), "mp", 1)
    kv, *own = attention_forward(
        doc_starts, after(tokens, qkv_sent, ffn_sent), memory, attn_gain, None, qkv
    )
    qkv_mine = after(qkv_mine, kv)
    qkv_got = (qkv_mine, swap(qkv_mine, "dp", 1))
    oth = attention_forward(doc_starts, tokens, memory, attn_gain, kv, qkv_got)
    ffn_mine = after(ffn_mine, oth[3])
    ffn_got = (ffn_mine, swap(ffn_mine, "dp", 1))
    ids = jnp.swapaxes(neighbour_ids, 1, 2)
    edges = bin_edges.reshape(1, BINS + 1)
    (
        result,
        grad_hidden,
        gctx_own,
        gctx_oth,
        ffn_first,
        ffn_last,
        sums,
    ) = middle_layer(
        tokens,
        own[3],
        oth[3],
        neighbours,
        ids,
        cotangent,
        (w_up, w_down, w_out),
        ffn_got,
        edges,
        gains,
    )
    ffn = Chain(None, 1)
    sent = ffn.pass_on(ffn_first, ffn_last, 1)
    g_oth_first, da_first, gain_1 = attention_backward(
        doc_starts, oth, after(gctx_oth, sent), kv, True
    )
    ffn.add(da_first)
    up = Chain(None, 1)
    up.pieces = tuple(p[:, :width] for p in ffn.pieces)
    down = Chain(None, 1)
    down.pieces = tuple(p[:, width:] for p in ffn.pieces)
    sent = up.give(1)
    sent = down.halve(far[0], sent)
    attn = Chain(None, 1)
    sent = attn.pass_on(da_first, None, 1, sent)
    g_oth_last, da_last, gain_2 = attention_backward(
        doc_starts, oth, after(gctx_oth, sent), kv, False
    )
    attn.come = after(attn.come, da_last)
    up.add(da_last)
    down.add(da_last)
    sent = up.halve(far[0])
    sent = down.give(1, sent)
    attn_sent = after(add_low(da_last, attn.come), sent)
    attn_come = swap(attn_sent, "mp", 1)
    g_own_first, da_first, gain_3 = attention_backward(
        doc_starts, own, after(gctx_own, attn_sent), kv, True
    )
    up.add(da_first)
    down.add(da_first)
    both = Chain(None, 0)
    both.pieces = tuple(lax.concatenate([u, d], 0) for u, d in zip(up.pieces, down.pieces))
    sent = both.halve(far[1])
    first_sent = after(da_first, sent)
    first_come = swap(first_sent, "dp", 1)
    g_own_last, da_last, gain_4 = attention_backward(
        doc_starts, own, after(gctx_own, first_sent), kv, False
    )
    attn_come, first_come = lax.optimization_barrier((attn_come, first_come, da_last))[:2]
    attn = Chain(None, 1)
    attn.pieces = (da_last, first_come, attn_come)
    both.add(da_last)
    gain_part = (gain_1[:1] + gain_2[:1] + gain_3[:1] + gain_4[:1]) / attn_gain
    small = lax.concatenate([sums[:4], gain_part], 0)
    sent = attn.halve(far[0])
    sent = both.send(far[2], sent)
    small_sent = after(small, sent)
    small_come = swap(small_sent, "mp", 1)
    grad_input = input_grad(
        tokens,
        after(grad_hidden, small_sent),
        attn_gain,
        (g_oth_first, g_oth_last, g_own_first, g_own_last),
        (oth[0], own[0]),
    )
    attn.come, small_come = lax.optimization_barrier((attn.come, small_come, grad_input))[:2]
    attn.pieces = (attn.kept, attn.come)
    ride = Ride(small_sent + small_come)

    mine = bit_of("dp", far[1])
    part = attn.total(lambda p: part_of(p, 1 - mine, 1))
    kept = attn.total(lambda p: part_of(p, mine, 1))
    come = swap(ride.below(part), "dp", far[1])
    come, both.come = lax.optimization_barrier((come, both.come))
    total = add_low(kept, ride.add(come, kept))
    ffn_total = add_low(both.sent, both.come)
    for bit in far[3:]:
        ffn_total = add_low(ffn_total, swap(ffn_total, "dp", bit))
    for bit in far[2:]:
        sent = ride.below(total)
        come = swap(sent, "dp", bit)
        if bit == far[2]:
            ffn_sent = after(ffn_total, sent)
            ffn_come = swap(ffn_sent, "dp", far[0])
            come, ffn_come = lax.optimization_barrier((come, ffn_come))
        total = add_low(total, ride.add(come, total))
    come = swap(total, "dp", far[1])
    ffn_halves = after(join(ffn_sent[None], ffn_come[None], far[0], 0), total)
    ffn_come = swap(ffn_halves[0], "dp", far[1])
    come, ffn_come = lax.optimization_barrier((come, ffn_come))
    ffn_first = join(ffn_halves[0], ffn_come, far[1], 0)
    total = join(total, come, far[1], 1)
    sent = ride.below(total)
    come = swap(sent, "dp", far[0])
    ffn_come = swap(after(ffn_halves[1], sent), "dp", far[1])
    come, ffn_come = lax.optimization_barrier((come, ffn_come))
    total = join(total, ride.add(come, total), far[0], 1)
    sent = ride.below(total)
    come = swap(sent, "dp", 1)
    ffn_last = join(ffn_halves[1], ffn_come, far[1], 0)
    ffn_total = after(lax.concatenate([ffn_first[None], ffn_last[None]], 0), sent)
    ffn_come = swap(ffn_total, "dp", 1)
    ride.add(come, total)
    small = ride.rows
    total_count = count * dp * lax.axis_size("mp")
    g_query, g_key, g_value, g_out, g_up, g_down = finish(
        (ffn_total, ffn_come), (total, come)
    )
    return (
        result,
        grad_input,
        g_query,
        g_key,
        g_value,
        g_out,
        g_up,
        g_down,
        small[4],
        small[0],
        small[2],
        small[1, 0] / total_count,
        small[3, :BINS] * (BINS / (total_count * NEIGH)),
    )


def solution(mesh):
    in_specs = (
        P(("dp", "mp"), None, None),
        P("dp", None, None),
        P(("dp", "mp"), None, None, None),
        P(("dp", "mp"), None, None),
        P("dp"),
        P(),
        P(None, "mp"),
        P(None, "mp"),
        P(None, "mp"),
        P("mp", None),
        P(None, "mp"),
        P("mp", None),
        P(),
        P(),
        P(),
        P(("dp", "mp"), None, None),
    )
    out_specs = (
        P(("dp", "mp"), None, None),
        P(("dp", "mp"), None, None),
        P(None, "mp"),
        P(None, "mp"),
        P(None, "mp"),
        P("mp", None),
        P(None, "mp"),
        P("mp", None),
        P(),
        P(),
        P(),
        P(),
        P(),
    )
    return jax.shard_map(shards, mesh=mesh, in_specs=in_specs, out_specs=out_specs, check_vma=False)
```

```python
import jax
import jax.numpy as jnp
from jax import lax
from jax.experimental import pallas as pl
from jax.experimental.pallas import tpu as pltpu
from jax.sharding import PartitionSpec as P

HEAD = 64
NEIGH = 4
BINS = 128
PAIR = 2 * HEAD
QROWS = 256
TILE = 256
GROUP = 64

EPS = 1e-05
BF16 = jnp.bfloat16
F32 = jnp.float32
VMEM_LIMIT = 56 * 1024 * 1024
MIDDLE_VMEM = 56 * 1024 * 1024
FINISH_VMEM = 24 * 1024 * 1024


def dot(left, right, left_dim=1, right_dim=0):
    return lax.dot_general(
        left, right, (((left_dim,), (right_dim,)), ((), ())), preferred_element_type=F32
    )


def normalize(values):
    centre = values - jnp.mean(values, -1, keepdims=True)
    spread = jnp.mean(centre * centre, -1, keepdims=True)
    rstd = lax.rsqrt(spread + EPS)
    return centre * rstd, rstd


def core_index():
    return lax.rem(lax.axis_index("dp"), 2)


def head_lanes(rows, head):
    lane = lax.broadcasted_iota(jnp.int32, (rows, PAIR), 1)
    return (lane >= head * HEAD) & (lane < (head + 1) * HEAD)


def only_head(block, head):
    return jnp.where(head_lanes(block.shape[0], head), block, jnp.zeros_like(block))


def attend(qkv_ref, p_ref, ctx_ref, length, with_memory):
    values = [only_head(qkv_ref[0, 0, pl.ds(3 * length, 2 * length), :], head) for head in range(2)]
    low = 0 if with_memory else length
    for first in range(0, length, QROWS):
        rows = pl.ds(first, QROWS)
        high = length + first + QROWS
        total = None
        for head in range(2):
            query = only_head(qkv_ref[0, 0, rows, :], head)
            scores = dot(query, qkv_ref[0, 0, pl.ds(length + low, high - low), :], 1, 1)
            seg = scores[:, length - low :]
            at = lax.broadcasted_iota(jnp.int32, seg.shape, 0) + first
            key = lax.broadcasted_iota(jnp.int32, seg.shape, 1)
            seg = jnp.where(key <= at, seg, -1e30)
            top = jnp.max(seg, -1, keepdims=True)
            if with_memory:
                mem = scores[:, :length]
                top = jnp.maximum(top, jnp.max(mem, -1, keepdims=True))
                mem = jnp.exp(mem - top)
            probs = jnp.exp(seg - top)
            mass = jnp.sum(probs, -1, keepdims=True)
            if with_memory:
                mass = mass + jnp.sum(mem, -1, keepdims=True)
            part = 1.0 / mass
            probs = (probs * part).astype(BF16)
            if with_memory:
                probs = jnp.concatenate([(mem * part).astype(BF16), probs], 1)
            p_ref[0, 0, head, rows, pl.ds(low, high - low)] = probs
            add = dot(probs, values[head][low:high])
            total = add if total is None else total + add
        ctx_ref[0, rows, :] = total.astype(BF16)


def forward_body(starts_ref, kv_ref, pack_ref, qkv_ref, p_ref, ctx_ref):
    length = kv_ref.shape[1] // 2
    pair = pl.program_id(1)
    kv = kv_ref[0]
    here = pl.multiple_of(3 * pair * PAIR, PAIR)
    query = dot(kv[length:], pack_ref[:, pl.ds(here, PAIR)]).astype(BF16)
    qkv_ref[0, 0, pl.ds(0, length), :] = (query.astype(F32) * HEAD ** (-0.5)).astype(BF16)
    both = dot(kv, pack_ref[:, pl.ds(here + PAIR, 2 * PAIR)]).astype(BF16)
    qkv_ref[0, 0, pl.ds(length, 2 * length), :] = both[:, :PAIR]
    qkv_ref[0, 0, pl.ds(3 * length, 2 * length), :] = both[:, PAIR:]
    start = starts_ref[lax.axis_index("mp") * pl.num_programs(0) + pl.program_id(0)]

    @pl.when(start == 0)
    def _():
        attend(qkv_ref, p_ref, ctx_ref, length, True)

    @pl.when(start != 0)
    def _():
        attend(qkv_ref, p_ref, ctx_ref, length, False)


def first_forward(
    starts_ref, tok_ref, mem_ref, gain_ref, wq_ref, wk_ref, wv_ref, kv_ref, pack_ref, *outs
):
    length = tok_ref.shape[1]

    @pl.when((pl.program_id(0) == 0) & (pl.program_id(1) == 0))
    def _():
        for i, weight in enumerate((wq_ref, wk_ref, wv_ref)):
            for p in range(2):
                pack_ref[:, pl.ds((3 * p + i) * PAIR, PAIR)] = weight[:, pl.ds(p * PAIR, PAIR)]

    @pl.when(pl.program_id(1) == 0)
    def _():
        gain = gain_ref[...]
        kv_ref[0, pl.ds(0, length), :] = (normalize(mem_ref[0].astype(F32))[0] * gain).astype(BF16)
        kv_ref[0, pl.ds(length, length), :] = (
            normalize(tok_ref[0].astype(F32))[0] * gain
        ).astype(BF16)

    forward_body(starts_ref, kv_ref, pack_ref, *outs)


def second_forward(starts_ref, kv_ref, mine_ref, sibling_ref, pack_ref, *outs):
    rows = mine_ref.shape[0]
    core = core_index()

    @pl.when((pl.program_id(0) == 0) & (pl.program_id(1) == 0))
    def _():
        for block, which in ((mine_ref, core), (sibling_ref, 1 - core)):
            to = pl.ds(pl.multiple_of(which * rows, rows), rows)
            for i in range(3):
                for p in range(2):
                    pack_ref[to, pl.ds((3 * p + i) * PAIR, PAIR)] = block[
                        :, pl.ds((2 * i + p) * PAIR, PAIR)
                    ]

    forward_body(starts_ref, kv_ref, pack_ref, *outs)


def attention_forward(starts, tokens, memory, gain, kv, weights):
    rows, length, width = tokens.shape
    pairs = 2
    pack = (width, 3 * pairs * PAIR)
    outs = [
        jax.ShapeDtypeStruct(pack, BF16),
        jax.ShapeDtypeStruct((rows, pairs, 5 * length, PAIR), BF16),
        jax.ShapeDtypeStruct((rows, pairs, 2, length, 2 * length), BF16),
        jax.ShapeDtypeStruct((rows, length, pairs * PAIR), BF16),
    ]
    out_specs = [
        pl.BlockSpec(pack, lambda r, p: (0, 0)),
        pl.BlockSpec((1, 1, 5 * length, PAIR), lambda r, p: (r, p, 0, 0)),
        pl.BlockSpec((1, 1, 2, length, 2 * length), lambda r, p: (r, p, 0, 0, 0)),
        pl.BlockSpec((1, length, PAIR), lambda r, p: (r, 0, p)),
    ]
    kv_spec = pl.BlockSpec((1, 2 * length, width), lambda r, p: (r, 0, 0))
    in_specs = [pl.BlockSpec(memory_space=pltpu.SMEM)]
    if kv is None:
        body = first_forward
        ins = [tokens, memory, gain]
        in_specs += [
            pl.BlockSpec((1, length, width), lambda r, p: (r, 0, 0)),
            pl.BlockSpec((1, length, width), lambda r, p: (lax.axis_index("mp") * rows + r, 0, 0)),
            pl.BlockSpec((1, width), lambda r, p: (0, 0)),
        ]
        outs = [jax.ShapeDtypeStruct((rows, 2 * length, width), BF16)] + outs
        out_specs = [kv_spec] + out_specs
    else:
        body = second_forward
        ins = [kv]
        in_specs += [kv_spec]
    in_specs += [pl.BlockSpec(w.shape, lambda r, p: (0, 0)) for w in weights]
    return pl.pallas_call(
        body,
        grid=(rows, pairs),
        in_specs=in_specs,
        out_specs=out_specs,
        out_shape=outs,
        compiler_params=pltpu.CompilerParams(vmem_limit_bytes=VMEM_LIMIT),
        cost_estimate=pl.CostEstimate(flops=6 * 10**9, bytes_accessed=16 * 2**20, transcendentals=0),
    )(starts, *ins, *weights)


def gelu_parts(pre):
    c0 = 0.7978845608028654
    c1 = c0 * 0.044715
    square = pre * pre
    part = 0.5 * jnp.tanh(pre * (c1 * square + c0)) + 0.5
    act = pre * part
    return act, part + act * (1.0 - part) * ((6.0 * c1) * square + 2.0 * c0)


def weighted(weights, values):
    return sum(w * v for w, v in zip(weights[1:], values[1:])) + weights[0] * values[0]


def middle_body(
    tok_ref,
    ctx_own_ref,
    ctx_oth_ref,
    nb_ref,
    ids_ref,
    cot_ref,
    up_far,
    down_far,
    out_far,
    mine_far,
    sibling_far,
    edges_ref,
    gains_ref,
    result_ref,
    grad_hidden_ref,
    gctx_own_ref,
    gctx_oth_ref,
    sent_up_far,
    sent_down_far,
    kept_up_far,
    kept_down_far,
    sums_ref,
    e_ref,
    hist_ref,
    edge_ref,
    pick_ref,
    up_ref,
    down_ref,
    out_ref,
    oth_ref,
    stage_ref,
    ffn_in_ref,
    act_ref,
    gpre_ref,
    cots_ref,
    low_ref,
    ctx_ref,
    in_sems,
    out_sems,
):
    step = pl.program_id(0)
    here = pl.ds(pl.multiple_of(step * TILE, TILE), TILE)
    width = tok_ref.shape[-1]
    hidden_units = down_ref.shape[0]
    half = width // 2
    chunks = hidden_units // width
    scale = width ** (-0.5)
    core = core_index()
    copies = [
        pltpu.make_async_copy(far, near, in_sems.at[i])
        for i, (far, near) in enumerate(
            (
                (out_far, out_ref),
                (mine_far, oth_ref.at[core]),
                (sibling_far, oth_ref.at[1 - core]),
                (up_far, up_ref),
                (down_far, down_ref),
            )
        )
    ]

    @pl.when(step == 0)
    def _():
        for copy in copies:
            copy.start()
        sums_ref[...] = jnp.zeros_like(sums_ref)
        hist_ref[...] = jnp.zeros_like(hist_ref)
        row = lax.broadcasted_iota(jnp.int32, pick_ref.shape, 0)
        column = lax.broadcasted_iota(jnp.int32, pick_ref.shape, 1)
        from_row = NEIGH * (row % GROUP) + row // GROUP
        pick_ref[...] = (column == from_row).astype(F32).astype(BF16)
        edges = edges_ref[...].astype(F32)
        for i in range(2):
            edge_ref[i] = jnp.broadcast_to(edges[:, i : i + BINS], (BINS, BINS)).T
        for copy in copies[:3]:
            copy.wait()

    def other_out():
        at = pl.ds(2 * width, half // 2)
        return jnp.concatenate([oth_ref[0, at, :], oth_ref[1, at, :]], 0)

    wgate = gains_ref[pl.ds(1, 1), :]
    gain = gains_ref[pl.ds(0, 1), :]

    def front():
        ctx_ref[here, pl.ds(0, half)] = ctx_own_ref[0]
        ctx_ref[here, pl.ds(half, half)] = ctx_oth_ref[0]
        cots_ref[here, :] = cot_ref[0]
        hidden = (
            tok_ref[0].astype(F32)
            + dot(ctx_own_ref[0], out_ref[...])
            + dot(ctx_oth_ref[0], other_out())
        )
        for first in range(0, TILE, GROUP):
            mixed_rows = nb_ref[0, pl.ds(first, GROUP)].reshape(NEIGH * GROUP, width)
            planes = dot(pick_ref[...], mixed_rows)
            for k in range(NEIGH):
                e_ref[k, pl.ds(first, GROUP), :] = planes[k * GROUP : (k + 1) * GROUP]
        affinity = [
            jnp.sum(e_ref[k] * hidden, -1, keepdims=True) * scale for k in range(NEIGH)
        ]
        top = jnp.maximum(
            jnp.maximum(affinity[0], affinity[1]), jnp.maximum(affinity[2], affinity[3])
        )
        raised = [jnp.exp(a - top) for a in affinity]
        inverse = 1.0 / (raised[0] + raised[1] + raised[2] + raised[3])
        weights = [a * inverse for a in raised]
        gate = jax.nn.sigmoid(jnp.sum(hidden * wgate, -1, keepdims=True))
        recalled = weighted(weights, [e_ref[k] for k in range(NEIGH)])
        mixed = hidden + gate * recalled
        normal, rstd = normalize(mixed)
        ffn_in_ref[here, :] = (normal * gain).astype(BF16)
        return hidden, weights, gate, mixed, normal, rstd

    def feed():
        ffn_in = ffn_in_ref[here, :]
        cot = cot_ref[0]
        down_sum = None
        grad_sum = None
        for side in range(2):
            for c in range(chunks):
                if side == 0:
                    up = up_ref[:, pl.ds(c * width, width)]
                    down = down_ref[pl.ds(c * width, width), :]
                else:
                    part = pl.ds(c * half, half)
                    up = jnp.concatenate([oth_ref[0, part, :], oth_ref[1, part, :]], 0)
                    down = oth_ref[c, pl.ds(width, width), :]
                at = pl.ds((side * chunks + c) * width, width)
                act, slope = gelu_parts(dot(ffn_in, up))
                act = act.astype(BF16)
                gpre = (dot(cot, down, 1, 1) * slope).astype(BF16)
                act_ref[here, at] = act
                gpre_ref[here, at] = gpre
                add = dot(act, down)
                down_sum = add if down_sum is None else down_sum + add
                add = dot(gpre, up, 1, 1)
                grad_sum = add if grad_sum is None else grad_sum + add
        return down_sum, grad_sum

    def back(kept, sums):
        hidden, weights, gate, mixed, normal, rstd = kept
        down_sum, grad_sum = sums
        result_ref[0] = (mixed + down_sum).astype(BF16)
        gain_part = jnp.sum(grad_sum * normal, 0, keepdims=True)
        grad_normal = grad_sum * gain
        grad_mixed = cot_ref[0].astype(F32) + rstd * (
            grad_normal
            - jnp.mean(grad_normal, -1, keepdims=True)
            - normal * jnp.mean(grad_normal * normal, -1, keepdims=True)
        )
        pulls = [
            jnp.sum(grad_mixed * e_ref[k], -1, keepdims=True) for k in range(NEIGH)
        ]
        pulled = weighted(weights, pulls)
        gate_grad = gate * (1.0 - gate) * pulled
        grad_hidden = grad_mixed + gate_grad * wgate
        for k in range(NEIGH):
            grad_hidden = (
                grad_hidden + (scale * gate * weights[k] * (pulls[k] - pulled)) * e_ref[k]
            )
        grad_hidden_ref[0] = grad_hidden
        low = grad_hidden.astype(BF16)
        low_ref[here, :] = low
        gctx_own_ref[0] = dot(low, out_ref[...], 1, 1).astype(BF16)
        gctx_oth_ref[0] = dot(low, other_out(), 1, 1).astype(BF16)
        gate_wide = jnp.broadcast_to(gate, (TILE, BINS)).T
        low_edge = jnp.concatenate([edge_ref[0]] * (TILE // BINS), 1)
        high_edge = jnp.concatenate([edge_ref[1]] * (TILE // BINS), 1)
        mass = jnp.zeros_like(gate_wide)
        for k in range(NEIGH):
            ids = ids_ref[0, pl.ds(k, 1), :].astype(F32)
            mass = mass + jnp.where((ids >= low_edge) & (ids < high_edge), gate_wide, 0.0)
        gate_sum = jnp.sum(jnp.broadcast_to(gate, (TILE, width)), 0, keepdims=True)
        sums_ref[pl.ds(0, 1), :] += gain_part
        sums_ref[pl.ds(1, 1), :] += gate_sum
        sums_ref[pl.ds(2, 1), :] += jnp.sum(gate_grad * hidden, 0, keepdims=True)
        hist_ref[...] += mass

    kept = front()

    @pl.when(step == 0)
    def _():
        for copy in copies[3:]:
            copy.wait()

    back(kept, feed())

    @pl.when(step == pl.num_programs(0) - 1)
    def _():
        sums_ref[pl.ds(3, 1), pl.ds(0, BINS)] = jnp.sum(hist_ref[...].T, 0, keepdims=True)
        cut = sent_up_far.shape[1]
        moves = []
        for fars, which in (
            ((sent_up_far, sent_down_far), 1 - core),
            ((kept_up_far, kept_down_far), core),
        ):
            for side in range(2):
                at = pl.ds(pl.multiple_of((side * chunks + which) * width, width), width)
                here = pl.ds(pl.multiple_of((2 * side + which) * PAIR, PAIR), PAIR)
                slot = len(moves) // 2
                first = 0
                for left, right in (
                    (ffn_in_ref[...], gpre_ref[:, at]),
                    (act_ref[:, at], cots_ref[...]),
                    (ctx_ref[:, here], low_ref[...]),
                ):
                    piece = dot(left, right, 0, 0).astype(BF16)
                    stage_ref[slot, pl.ds(first, piece.shape[0]), :] = piece
                    first += piece.shape[0]
                for i, far in enumerate(fars):
                    move = pltpu.make_async_copy(
                        stage_ref.at[slot, pl.ds(i * cut, cut), :],
                        far.at[side],
                        out_sems.at[len(moves)],
                    )
                    move.start()
                    moves.append(move)
        for move in moves:
            move.wait()


def middle_layer(tokens, ctx_own, ctx_oth, nb, ids, cot, weights, received, edges, gains):
    rows, length, width = tokens.shape
    hidden_units = weights[1].shape[0]
    steps = length // TILE
    tiles = rows * steps
    count = rows * length
    assert hidden_units == 2 * width

    def place_of(i):
        return i // steps, i % steps

    def tiled(last):
        return pl.BlockSpec((1, TILE, last), lambda i: (*place_of(i), 0))

    def whole(shape):
        return pl.BlockSpec(shape, lambda i: (0,) * len(shape))

    far = pl.BlockSpec(memory_space=pl.ANY)
    return pl.pallas_call(
        middle_body,
        grid=(tiles,),
            in_specs=[
                tiled(width),
                tiled(width // 2),
                tiled(width // 2),
                pl.BlockSpec((1, TILE, NEIGH, width), lambda i: (*place_of(i), 0, 0)),
                pl.BlockSpec(
                    (1, NEIGH, TILE), lambda i: (place_of(i)[0], 0, place_of(i)[1])
                ),
                tiled(width),
                *[far] * 5,
                whole((1, BINS + 1)),
                whole((2, width)),
            ],
            out_specs=[
                tiled(width),
                tiled(width),
                tiled(width // 2),
                tiled(width // 2),
                far,
                far,
                far,
                far,
                whole((8, width)),
            ],
            scratch_shapes=[
                pltpu.VMEM((NEIGH, TILE, width), F32),
                pltpu.VMEM((BINS, TILE), F32),
                pltpu.VMEM((2, BINS, BINS), F32),
                pltpu.VMEM((NEIGH * GROUP, NEIGH * GROUP), BF16),
                *[pltpu.VMEM(w.shape, BF16) for w in weights],
                pltpu.VMEM((2, *received[0].shape), BF16),
                pltpu.VMEM((4, 2 * width + PAIR, width), BF16),
                pltpu.VMEM((count, width), BF16),
                pltpu.VMEM((count, 2 * hidden_units), BF16),
                pltpu.VMEM((count, 2 * hidden_units), BF16),
                pltpu.VMEM((count, width), BF16),
                pltpu.VMEM((count, width), BF16),
                pltpu.VMEM((count, width), BF16),
                pltpu.SemaphoreType.DMA((5,)),
                pltpu.SemaphoreType.DMA((8,)),
            ],
        out_shape=[
            jax.ShapeDtypeStruct((rows, length, width), BF16),
            jax.ShapeDtypeStruct((rows, length, width), F32),
            jax.ShapeDtypeStruct((rows, length, width // 2), BF16),
            jax.ShapeDtypeStruct((rows, length, width // 2), BF16),
            *[jax.ShapeDtypeStruct((2, width + PAIR // 2, width), BF16)] * 4,
            jax.ShapeDtypeStruct((8, width), F32),
        ],
        compiler_params=pltpu.CompilerParams(vmem_limit_bytes=MIDDLE_VMEM),
        cost_estimate=pl.CostEstimate(flops=15 * 10**9, bytes_accessed=30 * 2**20, transcendentals=0),
    )(tokens, ctx_own, ctx_oth, nb, ids, cot, *weights, *received, edges, gains)


def attend_back(
    head, qkv_ref, p_ref, gctx_ref, ctx_ref, ds_ref, dq_ref, t_ref, dk_ref, dv_ref, with_memory
):
    length = ctx_ref.shape[1]
    grad = only_head(gctx_ref[0], head)
    delta = jnp.sum(grad.astype(F32) * ctx_ref[0].astype(F32), -1, keepdims=True)
    keys = only_head(qkv_ref[0, 0, pl.ds(length, 2 * length), :], head)
    lanes = pl.ds(pl.multiple_of(head * HEAD, HEAD), HEAD)
    low = 0 if with_memory else length
    for first in range(0, length, QROWS):
        rows = pl.ds(first, QROWS)
        high = length + first + QROWS
        here = pl.ds(low, high - low)
        probs = p_ref[0, 0, 0, rows, here].astype(F32)
        values = qkv_ref[0, 0, pl.ds(3 * length + low, high - low), :]
        grad_probs = dot(grad[first : first + QROWS], values, 1, 1)
        ds = (probs * (grad_probs - delta[first : first + QROWS])).astype(BF16)
        ds_ref[rows, here] = ds
        dq_ref[rows, :] += dot(ds, keys[low:high])
    for out_ref, left, right in (
        (dk_ref, t_ref[0, lanes, :], ds_ref),
        (dv_ref, t_ref[1, lanes, :], p_ref.at[0, 0, 0]),
    ):
        if not with_memory:
            out_ref[lanes, :length] = jnp.zeros((HEAD, length), BF16)
        for first in range(0, length, QROWS):
            start = low if first == 0 else length + first
            here = pl.ds(start, length + first + QROWS - start)
            out_ref[lanes, here] = dot(
                left[:, first:], right[pl.ds(first, length - first), here]
            ).astype(BF16)


def backward_body(
    starts_ref,
    qkv_ref,
    p_ref,
    gctx_ref,
    ctx_ref,
    kv_far,
    pack_ref,
    grads_ref,
    dw_ref,
    gain_ref,
    ds_ref,
    dq_ref,
    t_ref,
    dk_ref,
    dv_ref,
    acc_ref,
    kv_ref,
    sem,
):
    length = ctx_ref.shape[1]
    row = pl.program_id(1)
    head = pl.program_id(2)
    start = starts_ref[lax.axis_index("mp") * pl.num_programs(1) + row]
    fetch = pltpu.make_async_copy(kv_far.at[row], kv_ref, sem)
    args = (qkv_ref, p_ref, gctx_ref, ctx_ref, ds_ref, dq_ref, t_ref, dk_ref, dv_ref)

    @pl.when(head == 0)
    def _():
        fetch.start()
        dq_ref[...] = jnp.zeros_like(dq_ref)
        t_ref[0] = qkv_ref[0, 0, pl.ds(0, length), :].T
        t_ref[1] = gctx_ref[0].T

    @pl.when(start == 0)
    def _():
        attend_back(head, *args, True)

    @pl.when(start != 0)
    def _():
        attend_back(head, *args, False)

    @pl.when(head == 1)
    def _():
        dq_t = (dq_ref[...] * HEAD ** (-0.5)).astype(BF16).T
        grads_ref[0, 0, pl.ds(0, PAIR), :] = dq_t
        grads_ref[0, 0, pl.ds(PAIR, PAIR), :] = dk_ref[:, length:]
        grads_ref[0, 0, pl.ds(2 * PAIR, PAIR), :] = dv_ref[:, length:]
        fetch.wait()
        for i, add in enumerate(
            (
                dot(dq_t, kv_ref[pl.ds(length, length), :]),
                dot(dk_ref[...], kv_ref[...]),
                dot(dv_ref[...], kv_ref[...]),
            )
        ):
            acc_ref[i] = jnp.where(row == 0, add, acc_ref[i] + add)

    @pl.when((head == 1) & (row == pl.num_programs(1) - 1))
    def _():
        part = None
        for i in range(3):
            total = acc_ref[i]
            dw_ref[0, i] = total.astype(BF16)
            weight = pack_ref[:, pl.ds(i * PAIR, PAIR)].T.astype(F32)
            add = jnp.sum(total * weight, 0, keepdims=True)
            part = add if part is None else part + add
        gain_ref[0] = jnp.broadcast_to(part, gain_ref.shape[1:])


def attention_backward(starts, saved, gctx, kv, shift, many):
    pack, qkv, p, ctx = saved
    rows, _, _, length, _ = p.shape
    width = kv.shape[-1]

    def pair(n):
        return lax.rem(core_index() + shift + n, 2)

    return pl.pallas_call(
        backward_body,
        grid=(many, rows, 2),
        in_specs=[
            pl.BlockSpec(memory_space=pltpu.SMEM),
            pl.BlockSpec((1, 1, 5 * length, PAIR), lambda n, r, h: (r, pair(n), 0, 0)),
            pl.BlockSpec((1, 1, 1, length, 2 * length), lambda n, r, h: (r, pair(n), h, 0, 0)),
            pl.BlockSpec((1, length, PAIR), lambda n, r, h: (r, 0, pair(n))),
            pl.BlockSpec((1, length, PAIR), lambda n, r, h: (r, 0, pair(n))),
            pl.BlockSpec(memory_space=pl.ANY),
            pl.BlockSpec((width, 3 * PAIR), lambda n, r, h: (0, pair(n))),
        ],
        out_specs=[
            pl.BlockSpec((1, 1, 3 * PAIR, length), lambda n, r, h: (n, r, 0, 0)),
            pl.BlockSpec((1, 3, PAIR, width), lambda n, r, h: (n, 0, 0, 0)),
            pl.BlockSpec((1, 8, width), lambda n, r, h: (n, 0, 0)),
        ],
        scratch_shapes=[
            pltpu.VMEM((length, 2 * length), BF16),
            pltpu.VMEM((length, PAIR), F32),
            pltpu.VMEM((2, PAIR, length), BF16),
            pltpu.VMEM((PAIR, 2 * length), BF16),
            pltpu.VMEM((PAIR, 2 * length), BF16),
            pltpu.VMEM((3, PAIR, width), F32),
            pltpu.VMEM((2 * length, width), BF16),
            pltpu.SemaphoreType.DMA,
        ],
        out_shape=[
            jax.ShapeDtypeStruct((many, rows, 3 * PAIR, length), BF16),
            jax.ShapeDtypeStruct((many, 3, PAIR, width), BF16),
            jax.ShapeDtypeStruct((many, 8, width), F32),
        ],
        compiler_params=pltpu.CompilerParams(vmem_limit_bytes=VMEM_LIMIT),
        cost_estimate=pl.CostEstimate(
            flops=4 * 10**9 * many, bytes_accessed=8 * 2**20 * many, transcendentals=0
        ),
    )(starts, qkv, p, gctx, ctx, kv, pack)


def input_body(
    tok_ref,
    grad_hidden_ref,
    gain_ref,
    oth_ref,
    own_first_ref,
    own_last_ref,
    oth_pack_ref,
    own_pack_ref,
    out_ref,
):
    core = core_index()
    total = None
    for block, pack, which in (
        (oth_ref[0, 0], oth_pack_ref, 1 - core),
        (oth_ref[1, 0], oth_pack_ref, core),
        (own_first_ref[0, 0], own_pack_ref, 1 - core),
        (own_last_ref[0, 0], own_pack_ref, core),
    ):
        here = pl.ds(pl.multiple_of(which * 3 * PAIR, 3 * PAIR), 3 * PAIR)
        add = dot(block, pack[:, here], 0, 1)
        total = add if total is None else total + add
    normal, rstd = normalize(tok_ref[0].astype(F32))
    grad = total * gain_ref[...]
    out_ref[0] = (
        grad_hidden_ref[0]
        + rstd
        * (
            grad
            - jnp.mean(grad, -1, keepdims=True)
            - normal * jnp.mean(grad * normal, -1, keepdims=True)
        )
    ).astype(BF16)


def input_grad(tokens, grad_hidden, gain, grads, packs):
    rows, length, width = tokens.shape
    row = pl.BlockSpec((1, length, width), lambda r: (r, 0, 0))

    def whole(array):
        return pl.BlockSpec(array.shape, lambda r: (0, 0))

    return pl.pallas_call(
        input_body,
        grid=(rows,),
        in_specs=[
            row,
            row,
            whole(gain),
            *[pl.BlockSpec((g.shape[0], 1) + g.shape[2:], lambda r: (0, r, 0, 0)) for g in grads],
            *[whole(p) for p in packs],
        ],
        out_specs=row,
        out_shape=jax.ShapeDtypeStruct(tokens.shape, BF16),
        compiler_params=pltpu.CompilerParams(vmem_limit_bytes=VMEM_LIMIT),
        cost_estimate=pl.CostEstimate(flops=2 * 10**9, bytes_accessed=8 * 2**20, transcendentals=0),
    )(tokens, grad_hidden, gain, *grads, *packs)


def finish_body(
    ffn_mine,
    ffn_sibling,
    attn_mine,
    attn_sibling,
    q_far,
    k_far,
    v_far,
    out_far,
    up_far,
    down_far,
    q_ref,
    k_ref,
    v_ref,
    out_ref,
    up_ref,
    down_ref,
    sems,
):
    core = core_index()
    width = up_far.shape[0]
    rows = attn_mine.shape[1]
    moves = []

    def pair(mine, sibling):
        return (
            jnp.where(core == 0, mine, sibling).astype(F32),
            jnp.where(core == 0, sibling, mine).astype(F32),
        )

    def move(near, far):
        moves.append(pltpu.make_async_copy(near, far, sems.at[len(moves)]))
        moves[-1].start()

    size = ffn_mine.shape[1] // 2
    pieces = [(x, pl.ds(y * size, size)) for y in range(2) for x in range(2)]
    halves = zip(*(pair(ffn_mine[x, y, :], ffn_sibling[x, y, :]) for x, y in pieces))
    for which, parts in enumerate(halves):
        rows_of = jnp.concatenate(parts, 0)
        to = pl.ds(which * width, width)
        up_ref[:, to] = rows_of[:width]
        down_ref[to, :] = rows_of[width : 2 * width]
        out_ref[pl.ds(which * PAIR, PAIR), :] = rows_of[2 * width :]
        move(down_ref.at[to, :], down_far.at[to, :])
    move(up_ref, up_far)
    move(out_ref, out_far)
    for i, (near, far) in enumerate(((q_ref, q_far), (k_ref, k_far), (v_ref, v_far))):
        first, last = pair(attn_mine[i], attn_sibling[pl.ds(i * rows, rows), :])
        near[...] = jnp.concatenate([first, last], 0).T
        move(near, far)
    for one in moves:
        one.wait()


def finish(ffn, attn):
    width = ffn[0].shape[-1]
    quarter = attn[0].shape[1]
    shapes = [(width, 2 * quarter)] * 3
    shapes += [(2 * quarter, width), (width, 2 * width), (2 * width, width)]

    def whole(array):
        return pl.BlockSpec(array.shape, lambda i: (0,) * array.ndim)

    return pl.pallas_call(
        finish_body,
        grid=(1,),
        in_specs=[whole(a) for a in (*ffn, *attn)],
        out_specs=[pl.BlockSpec(memory_space=pl.ANY)] * 6,
        scratch_shapes=[pltpu.VMEM(s, F32) for s in shapes] + [pltpu.SemaphoreType.DMA((8,))],
        out_shape=[jax.ShapeDtypeStruct(s, F32) for s in shapes],
        compiler_params=pltpu.CompilerParams(vmem_limit_bytes=FINISH_VMEM),
    )(*ffn, *attn)


def swap(array, axis, bit):
    size = lax.axis_size(axis)
    return lax.ppermute(array, axis, [(i, i ^ bit) for i in range(size)])


def bit_of(axis, bit):
    return (lax.axis_index(axis) // bit) % 2


def part_of(array, which, dim):
    half = array.shape[dim] // 2
    return lax.dynamic_slice_in_dim(array, which * half, half, dim)


def add_low(left, right):
    return (left.astype(F32) + right.astype(F32)).astype(BF16)


def join(mine, other, bit, dim):
    return jnp.where(
        bit_of("dp", bit) == 0,
        lax.concatenate([mine, other], dim),
        lax.concatenate([other, mine], dim),
    )


def swap_diagonal(array, first, last):
    size = lax.axis_size("dp")
    return lax.ppermute(array, "dp", [(i, i ^ first ^ last) for i in range(size)])


def join_four(mine, by_first, by_last, by_both, first, last):
    return join(
        join(mine, by_last, last, 0)[None], join(by_first, by_both, last, 0)[None], first, 0
    )


def after(value, *others):
    return lax.optimization_barrier((value, *others))[0]


class Chain:
    def __init__(self, array, dim):
        self.pieces = (array,)
        self.dim = dim

    def total(self, cut=lambda piece: piece):
        pieces = [cut(piece) for piece in self.pieces]
        if len(pieces) == 1:
            return pieces[0]
        return sum(piece.astype(F32) for piece in pieces).astype(BF16)

    def pass_on(self, sent, kept, bit, *others):
        self.sent = after(sent, *others)
        self.kept = kept
        self.come = swap(self.sent, "dp", bit)
        return self.sent

    def halve(self, bit, *others):
        mine = bit_of("dp", bit)
        self.sent = after(self.total(lambda p: part_of(p, 1 - mine, self.dim)), *others)
        self.kept = self.total(lambda p: part_of(p, mine, self.dim))
        self.come = swap(self.sent, "dp", bit)
        return self.sent

    def give(self, index, *others):
        self.sent = after(self.total(lambda p: p[index]), *others)
        self.kept = self.total(lambda p: p[1 - index])
        self.dim -= 1
        self.come = swap(self.sent, "mp", 1)
        return self.sent

    def send(self, bit, *others):
        self.sent = self.kept = after(self.total(), *others)
        self.come = swap(self.sent, "dp", bit)
        return self.sent

    def add(self, *others):
        self.come = after(self.come, *others)
        self.pieces = (self.kept, self.come)

    def join(self, bit, *others):
        self.pieces = (join(self.sent, after(self.come, *others), bit, self.dim),)


class Ride:
    def __init__(self, rows):
        self.rows = rows

    def below(self, array):
        left = self.rows
        parts = [array.reshape(-1, array.shape[-1])]
        for _ in range(3):
            part = lax.reduce_precision(left, 8, 7)
            parts.append(part.astype(BF16))
            left = left - part
        spare = -3 * left.shape[0] % 16
        parts.append(jnp.zeros((spare, left.shape[1]), BF16))
        return lax.concatenate(parts, 0)

    def add(self, block, like):
        size = like.size // like.shape[-1]
        count = self.rows.shape[0]
        for i in range(3):
            at = size + i * count
            self.rows = self.rows + block[at : at + count].astype(F32)
        return block[:size].reshape(like.shape)


def shards(
    tokens,
    memory,
    neighbours,
    neighbour_ids,
    doc_starts,
    bin_edges,
    w_query,
    w_key,
    w_value,
    w_out,
    w_up,
    w_down,
    gain_attn,
    gain_ffn,
    w_gate,
    cotangent,
):
    rows, length, width = tokens.shape
    count = rows * length
    dp = lax.axis_size("dp")
    core = bit_of("dp", 1)
    attn_gain = gain_attn.reshape(1, width)
    gains = jnp.stack([gain_ffn, w_gate])
    qkv = (w_query, w_key, w_value)
    far = []
    bit = 2
    while bit < dp:
        far.append(bit)
        bit *= 2

    qkv_sent = lax.concatenate([part_of(w, core, 0) for w in qkv], 1)
    up_part = part_of(w_up, core, 0)
    ffn_sent = lax.concatenate(
        [up_part[:, :width], up_part[:, width:], part_of(w_down, core, 0), part_of(w_out, core, 0)],
        0,
    )
    qkv_mine = swap(qkv_sent, "mp", 1)
    ffn_mine = swap(after(ffn_sent, qkv_sent), "mp", 1)
    kv, *own = attention_forward(
        doc_starts, after(tokens, qkv_sent, ffn_sent), memory, attn_gain, None, qkv
    )
    qkv_mine = after(qkv_mine, kv)
    qkv_got = (qkv_mine, swap(qkv_mine, "dp", 1))
    oth = attention_forward(doc_starts, tokens, memory, attn_gain, kv, qkv_got)
    ffn_mine = after(ffn_mine, oth[3])
    ffn_got = (ffn_mine, swap(ffn_mine, "dp", 1))
    ids = jnp.swapaxes(neighbour_ids, 1, 2)
    edges = bin_edges.reshape(1, BINS + 1)
    (
        result,
        grad_hidden,
        gctx_own,
        gctx_oth,
        sent_up,
        sent_down,
        kept_up,
        kept_down,
        sums,
    ) = middle_layer(
        tokens,
        own[3],
        oth[3],
        neighbours,
        ids,
        cotangent,
        (w_up, w_down, w_out),
        ffn_got,
        edges,
        gains,
    )
    up = Chain(None, 1)
    down = Chain(None, 1)
    up.pass_on(sent_up, kept_up, 1)
    down.pass_on(sent_down, kept_down, 1)
    up.add()
    down.add()
    sent = up.give(1)
    sent = down.halve(far[0], sent)
    g_oth, da, gain_oth = attention_backward(
        doc_starts, oth, after(gctx_oth, sent), kv, 1, 2
    )
    up.add(da)
    down.add(da)
    sent = up.halve(far[0])
    sent = down.give(1, sent)
    attn = Chain(None, 1)
    sent = attn.pass_on(da[0], da[1], 1, sent)
    g_own_first, da_first, gain_first = attention_backward(
        doc_starts, own, after(gctx_own, sent), kv, 1, 1
    )
    da_first = da_first[0]
    attn.add(da_first)
    up.add(da_first)
    down.add(da_first)
    both = Chain(None, 0)
    both.pieces = tuple(lax.concatenate([u, d], 0) for u, d in zip(up.pieces, down.pieces))
    sent = both.halve(far[1])
    attn_sent = after(attn.total(), sent)
    attn_come = swap(attn_sent, "mp", 1)
    first_sent = after(da_first, attn_sent)
    first_come = swap(first_sent, "dp", 1)
    g_own_last, da_last, gain_last = attention_backward(
        doc_starts, own, after(gctx_own, first_sent), kv, 0, 1
    )
    da_last = da_last[0]
    attn_come, first_come = lax.optimization_barrier((attn_come, first_come, da_last))[:2]
    attn = Chain(None, 1)
    attn.pieces = (da_last, first_come, attn_come)
    both.add(da_last)
    gain_part = sum(g[:, 0].sum(0) for g in (gain_oth, gain_first, gain_last))[None] / attn_gain
    small = lax.concatenate([sums[:4], gain_part], 0)
    sent = both.send(far[2])
    sent = attn.halve(far[0], sent)
    small_sent = after(small, sent)
    small_come = swap(small_sent, "mp", 1)
    grad_input = input_grad(
        tokens,
        after(grad_hidden, small_sent),
        attn_gain,
        (g_oth, g_own_first, g_own_last),
        (oth[0], own[0]),
    )
    attn.come, small_come = lax.optimization_barrier((attn.come, small_come, grad_input))[:2]
    attn.pieces = (attn.kept, attn.come)
    ride = Ride(small_sent + small_come)

    mine = bit_of("dp", far[1])
    part = attn.total(lambda p: part_of(p, 1 - mine, 1))
    kept = attn.total(lambda p: part_of(p, mine, 1))
    come = swap(part, "dp", far[1])
    come, both.come = lax.optimization_barrier((come, both.come))
    total = add_low(kept, come)
    ffn_total = add_low(both.sent, both.come)
    for bit in far[3:]:
        ffn_total = add_low(ffn_total, swap(ffn_total, "dp", bit))
    ffn_sent = ffn_total
    for bit in far[2:]:
        sent = ride.below(total)
        come = swap(sent, "dp", bit)
        if bit == far[2]:
            ffn_sent = after(ffn_total, sent)
            ffn_x = swap(ffn_sent, "dp", far[0])
            ffn_z = swap(ffn_sent, "dp", far[1])
            come, ffn_x, ffn_z = lax.optimization_barrier((come, ffn_x, ffn_z))
        total = add_low(total, ride.add(come, total))
    sent = ride.below(total)
    come_x = swap(sent, "dp", far[0])
    come_z = swap(sent, "dp", far[1])
    come_d = swap_diagonal(sent, far[0], far[1])
    ffn_d = swap_diagonal(after(ffn_sent, sent), far[0], far[1])
    come_x, come_z, come_d, ffn_d = lax.optimization_barrier((come_x, come_z, come_d, ffn_d))
    flat = total.reshape(-1, width)
    parts = [ride.add(come, flat) for come in (come_x, come_z, come_d)]
    shape = total.shape
    total = join_four(
        flat.reshape(shape).swapaxes(0, 1),
        *[part.reshape(shape).swapaxes(0, 1) for part in parts],
        far[0],
        far[1],
    )
    total = total.reshape(-1, *shape[:1], width).swapaxes(0, 1)
    sent = ride.below(total)
    come = swap(sent, "dp", 1)
    ffn_total = after(join_four(ffn_sent, ffn_x, ffn_z, ffn_d, far[0], far[1]), sent)
    ffn_come = swap(ffn_total, "dp", 1)
    ride.add(come, total)
    small = ride.rows
    total_count = count * dp * lax.axis_size("mp")
    g_query, g_key, g_value, g_out, g_up, g_down = finish(
        (ffn_total, ffn_come), (total, come)
    )
    return (
        result,
        grad_input,
        g_query,
        g_key,
        g_value,
        g_out,
        g_up,
        g_down,
        small[4],
        small[0],
        small[2],
        small[1, 0] / total_count,
        small[3, :BINS] * (BINS / (total_count * NEIGH)),
    )


def solution(mesh):
    in_specs = (
        P(("dp", "mp"), None, None),
        P("dp", None, None),
        P(("dp", "mp"), None, None, None),
        P(("dp", "mp"), None, None),
        P("dp"),
        P(),
        P(None, "mp"),
        P(None, "mp"),
        P(None, "mp"),
        P("mp", None),
        P(None, "mp"),
        P("mp", None),
        P(),
        P(),
        P(),
        P(("dp", "mp"), None, None),
    )
    out_specs = (
        P(("dp", "mp"), None, None),
        P(("dp", "mp"), None, None),
        P(None, "mp"),
        P(None, "mp"),
        P(None, "mp"),
        P("mp", None),
        P(None, "mp"),
        P("mp", None),
        P(),
        P(),
        P(),
        P(),
        P(),
    )
    return jax.shard_map(shards, mesh=mesh, in_specs=in_specs, out_specs=out_specs, check_vma=False)
```

```python
import functools

import jax
import jax.numpy as jnp
from jax import lax
from jax.experimental import pallas as pl
from jax.experimental.pallas import tpu as pltpu
from jax.sharding import PartitionSpec as P

HEAD = 64
NEIGH = 4
BINS = 128
PAIR = 2 * HEAD
QROWS = 256
TILE = 256
GROUP = 64

EPS = 1e-05
BF16 = jnp.bfloat16
F32 = jnp.float32
VMEM_LIMIT = 56 * 1024 * 1024
FORWARD_VMEM = 52 * 1024 * 1024
BACKWARD_VMEM = 48 * 1024 * 1024
FINISH_VMEM = 24 * 1024 * 1024


def dot(left, right, left_dim=1, right_dim=0):
    return lax.dot_general(
        left, right, (((left_dim,), (right_dim,)), ((), ())), preferred_element_type=F32
    )


def normalize(values):
    centre = values - jnp.mean(values, -1, keepdims=True)
    spread = jnp.mean(centre * centre, -1, keepdims=True)
    rstd = lax.rsqrt(spread + EPS)
    return centre * rstd, rstd


def core_index():
    return lax.rem(lax.axis_index("dp"), 2)


def head_lanes(rows, head):
    lane = lax.broadcasted_iota(jnp.int32, (rows, PAIR), 1)
    return (lane >= head * HEAD) & (lane < (head + 1) * HEAD)


def only_head(block, head):
    return jnp.where(head_lanes(block.shape[0], head), block, jnp.zeros_like(block))


def attend(qkv_ref, p_ref, ctx_ref, length, with_memory):
    values = [only_head(qkv_ref[0, 0, pl.ds(3 * length, 2 * length), :], head) for head in range(2)]
    low = 0 if with_memory else length
    for first in range(0, length, QROWS):
        rows = pl.ds(first, QROWS)
        high = length + first + QROWS
        total = None
        for head in range(2):
            query = only_head(qkv_ref[0, 0, rows, :], head)
            scores = dot(query, qkv_ref[0, 0, pl.ds(length + low, high - low), :], 1, 1)
            seg = scores[:, length - low :]
            at = lax.broadcasted_iota(jnp.int32, seg.shape, 0) + first
            key = lax.broadcasted_iota(jnp.int32, seg.shape, 1)
            seg = jnp.where(key <= at, seg, -1e30)
            top = jnp.max(seg, -1, keepdims=True)
            if with_memory:
                mem = scores[:, :length]
                top = jnp.maximum(top, jnp.max(mem, -1, keepdims=True))
                mem = jnp.exp(mem - top)
            probs = jnp.exp(seg - top)
            mass = jnp.sum(probs, -1, keepdims=True)
            if with_memory:
                mass = mass + jnp.sum(mem, -1, keepdims=True)
            part = 1.0 / mass
            probs = (probs * part).astype(BF16)
            if with_memory:
                probs = jnp.concatenate([(mem * part).astype(BF16), probs], 1)
            p_ref[0, 0, head, rows, pl.ds(low, high - low)] = probs
            add = dot(probs, values[head][low:high])
            total = add if total is None else total + add
        ctx_ref[0, rows, :] = total.astype(BF16)


def forward_body(starts_ref, kv_ref, pack_ref, qkv_ref, p_ref, ctx_ref):
    length = kv_ref.shape[1] // 2
    pair = pl.program_id(1)
    kv = kv_ref[0]
    here = pl.multiple_of(3 * pair * PAIR, PAIR)
    query = dot(kv[length:], pack_ref[:, pl.ds(here, PAIR)]).astype(BF16)
    qkv_ref[0, 0, pl.ds(0, length), :] = (query.astype(F32) * HEAD ** (-0.5)).astype(BF16)
    both = dot(kv, pack_ref[:, pl.ds(here + PAIR, 2 * PAIR)]).astype(BF16)
    qkv_ref[0, 0, pl.ds(length, 2 * length), :] = both[:, :PAIR]
    qkv_ref[0, 0, pl.ds(3 * length, 2 * length), :] = both[:, PAIR:]
    start = starts_ref[lax.axis_index("mp") * pl.num_programs(0) + pl.program_id(0)]

    @pl.when(start == 0)
    def _():
        attend(qkv_ref, p_ref, ctx_ref, length, True)

    @pl.when(start != 0)
    def _():
        attend(qkv_ref, p_ref, ctx_ref, length, False)


def first_forward(
    starts_ref, tok_ref, mem_ref, gain_ref, wq_ref, wk_ref, wv_ref, kv_ref, pack_ref, *outs
):
    length = tok_ref.shape[1]

    @pl.when((pl.program_id(0) == 0) & (pl.program_id(1) == 0))
    def _():
        for i, weight in enumerate((wq_ref, wk_ref, wv_ref)):
            for p in range(2):
                pack_ref[:, pl.ds((3 * p + i) * PAIR, PAIR)] = weight[:, pl.ds(p * PAIR, PAIR)]

    @pl.when(pl.program_id(1) == 0)
    def _():
        gain = gain_ref[...]
        kv_ref[0, pl.ds(0, length), :] = (normalize(mem_ref[0].astype(F32))[0] * gain).astype(BF16)
        kv_ref[0, pl.ds(length, length), :] = (
            normalize(tok_ref[0].astype(F32))[0] * gain
        ).astype(BF16)

    forward_body(starts_ref, kv_ref, pack_ref, *outs)


def second_forward(starts_ref, kv_ref, mine_ref, sibling_ref, pack_ref, *outs):
    rows = mine_ref.shape[0]
    core = core_index()

    @pl.when((pl.program_id(0) == 0) & (pl.program_id(1) == 0))
    def _():
        for block, which in ((mine_ref, core), (sibling_ref, 1 - core)):
            to = pl.ds(pl.multiple_of(which * rows, rows), rows)
            for i in range(3):
                for p in range(2):
                    pack_ref[to, pl.ds((3 * p + i) * PAIR, PAIR)] = block[
                        :, pl.ds((2 * i + p) * PAIR, PAIR)
                    ]

    forward_body(starts_ref, kv_ref, pack_ref, *outs)


def attention_forward(starts, tokens, memory, gain, kv, weights):
    rows, length, width = tokens.shape
    pairs = 2
    pack = (width, 3 * pairs * PAIR)
    outs = [
        jax.ShapeDtypeStruct(pack, BF16),
        jax.ShapeDtypeStruct((rows, pairs, 5 * length, PAIR), BF16),
        jax.ShapeDtypeStruct((rows, pairs, 2, length, 2 * length), BF16),
        jax.ShapeDtypeStruct((rows, length, pairs * PAIR), BF16),
    ]
    out_specs = [
        pl.BlockSpec(pack, lambda r, p: (0, 0)),
        pl.BlockSpec((1, 1, 5 * length, PAIR), lambda r, p: (r, p, 0, 0)),
        pl.BlockSpec((1, 1, 2, length, 2 * length), lambda r, p: (r, p, 0, 0, 0)),
        pl.BlockSpec((1, length, PAIR), lambda r, p: (r, 0, p)),
    ]
    kv_spec = pl.BlockSpec((1, 2 * length, width), lambda r, p: (r, 0, 0))
    in_specs = [pl.BlockSpec(memory_space=pltpu.SMEM)]
    if kv is None:
        body = first_forward
        ins = [tokens, memory, gain]
        in_specs += [
            pl.BlockSpec((1, length, width), lambda r, p: (r, 0, 0)),
            pl.BlockSpec((1, length, width), lambda r, p: (lax.axis_index("mp") * rows + r, 0, 0)),
            pl.BlockSpec((1, width), lambda r, p: (0, 0)),
        ]
        outs = [jax.ShapeDtypeStruct((rows, 2 * length, width), BF16)] + outs
        out_specs = [kv_spec] + out_specs
    else:
        body = second_forward
        ins = [kv]
        in_specs += [kv_spec]
    in_specs += [pl.BlockSpec(w.shape, lambda r, p: (0, 0)) for w in weights]
    return pl.pallas_call(
        body,
        grid=(rows, pairs),
        in_specs=in_specs,
        out_specs=out_specs,
        out_shape=outs,
        compiler_params=pltpu.CompilerParams(vmem_limit_bytes=FORWARD_VMEM),
        cost_estimate=pl.CostEstimate(flops=6 * 10**9, bytes_accessed=16 * 2**20, transcendentals=0),
    )(starts, *ins, *weights)


def gelu_parts(pre):
    c0 = 0.7978845608028654
    c1 = c0 * 0.044715
    square = pre * pre
    part = 0.5 * jnp.tanh(pre * (c1 * square + c0)) + 0.5
    act = pre * part
    return act, part + act * (1.0 - part) * ((6.0 * c1) * square + 2.0 * c0)


def weighted(weights, values):
    return sum(w * v for w, v in zip(weights[1:], values[1:])) + weights[0] * values[0]


def middle_body(
    tok_ref,
    ctx_own_ref,
    ctx_oth_ref,
    nb_ref,
    ids_ref,
    cot_ref,
    up_far,
    down_far,
    out_far,
    mine_far,
    sibling_far,
    edges_ref,
    gains_ref,
    result_ref,
    grad_hidden_ref,
    gctx_own_ref,
    gctx_oth_ref,
    sent_up_far,
    sent_down_far,
    kept_up_far,
    kept_down_far,
    sums_ref,
    e_ref,
    hist_ref,
    edge_ref,
    pick_ref,
    up_ref,
    down_ref,
    out_ref,
    oth_ref,
    stage_ref,
    ffn_in_ref,
    act_ref,
    gpre_ref,
    cots_ref,
    low_ref,
    ctx_ref,
    in_sems,
    out_sems,
):
    step = pl.program_id(0)
    here = pl.ds(pl.multiple_of(step * TILE, TILE), TILE)
    width = tok_ref.shape[-1]
    hidden_units = down_ref.shape[0]
    half = width // 2
    chunks = hidden_units // width
    scale = width ** (-0.5)
    core = core_index()
    copies = [
        pltpu.make_async_copy(far, near, in_sems.at[i])
        for i, (far, near) in enumerate(
            (
                (out_far, out_ref),
                (mine_far, oth_ref.at[core]),
                (sibling_far, oth_ref.at[1 - core]),
                (up_far, up_ref),
                (down_far, down_ref),
            )
        )
    ]

    @pl.when(step == 0)
    def _():
        for copy in copies:
            copy.start()
        sums_ref[...] = jnp.zeros_like(sums_ref)
        hist_ref[...] = jnp.zeros_like(hist_ref)
        row = lax.broadcasted_iota(jnp.int32, pick_ref.shape, 0)
        column = lax.broadcasted_iota(jnp.int32, pick_ref.shape, 1)
        from_row = NEIGH * (row % GROUP) + row // GROUP
        pick_ref[...] = (column == from_row).astype(F32).astype(BF16)
        edges = edges_ref[...].astype(F32)
        for i in range(2):
            edge_ref[i] = jnp.broadcast_to(edges[:, i : i + BINS], (BINS, BINS)).T
        for copy in copies[:3]:
            copy.wait()

    def other_out():
        at = pl.ds(2 * width, half // 2)
        return jnp.concatenate([oth_ref[0, at, :], oth_ref[1, at, :]], 0)

    wgate = gains_ref[pl.ds(1, 1), :]
    gain = gains_ref[pl.ds(0, 1), :]

    def front():
        ctx_ref[here, pl.ds(0, half)] = ctx_own_ref[0]
        ctx_ref[here, pl.ds(half, half)] = ctx_oth_ref[0]
        cots_ref[here, :] = cot_ref[0]
        hidden = (
            tok_ref[0].astype(F32)
            + dot(ctx_own_ref[0], out_ref[...])
            + dot(ctx_oth_ref[0], other_out())
        )
        for first in range(0, TILE, GROUP):
            mixed_rows = nb_ref[0, pl.ds(first, GROUP)].reshape(NEIGH * GROUP, width)
            planes = dot(pick_ref[...], mixed_rows)
            for k in range(NEIGH):
                e_ref[k, pl.ds(first, GROUP), :] = planes[k * GROUP : (k + 1) * GROUP]
        affinity = [
            jnp.sum(e_ref[k] * hidden, -1, keepdims=True) * scale for k in range(NEIGH)
        ]
        top = jnp.maximum(
            jnp.maximum(affinity[0], affinity[1]), jnp.maximum(affinity[2], affinity[3])
        )
        raised = [jnp.exp(a - top) for a in affinity]
        inverse = 1.0 / (raised[0] + raised[1] + raised[2] + raised[3])
        weights = [a * inverse for a in raised]
        gate = jax.nn.sigmoid(jnp.sum(hidden * wgate, -1, keepdims=True))
        recalled = weighted(weights, [e_ref[k] for k in range(NEIGH)])
        mixed = hidden + gate * recalled
        normal, rstd = normalize(mixed)
        ffn_in_ref[here, :] = (normal * gain).astype(BF16)
        return hidden, weights, gate, mixed, normal, rstd

    def feed():
        ffn_in = ffn_in_ref[here, :]
        cot = cot_ref[0]
        down_sum = None
        grad_sum = None
        for side in range(2):
            for c in range(chunks):
                if side == 0:
                    up = up_ref[:, pl.ds(c * width, width)]
                    down = down_ref[pl.ds(c * width, width), :]
                else:
                    part = pl.ds(c * half, half)
                    up = jnp.concatenate([oth_ref[0, part, :], oth_ref[1, part, :]], 0)
                    down = oth_ref[c, pl.ds(width, width), :]
                at = pl.ds((side * chunks + c) * width, width)
                act, slope = gelu_parts(dot(ffn_in, up))
                act = act.astype(BF16)
                gpre = (dot(cot, down, 1, 1) * slope).astype(BF16)
                act_ref[here, at] = act
                gpre_ref[here, at] = gpre
                add = dot(act, down)
                down_sum = add if down_sum is None else down_sum + add
                add = dot(gpre, up, 1, 1)
                grad_sum = add if grad_sum is None else grad_sum + add
        return down_sum, grad_sum

    def back(kept, sums):
        hidden, weights, gate, mixed, normal, rstd = kept
        down_sum, grad_sum = sums
        result_ref[0] = (mixed + down_sum).astype(BF16)
        gain_part = jnp.sum(grad_sum * normal, 0, keepdims=True)
        grad_normal = grad_sum * gain
        grad_mixed = cot_ref[0].astype(F32) + rstd * (
            grad_normal
            - jnp.mean(grad_normal, -1, keepdims=True)
            - normal * jnp.mean(grad_normal * normal, -1, keepdims=True)
        )
        pulls = [
            jnp.sum(grad_mixed * e_ref[k], -1, keepdims=True) for k in range(NEIGH)
        ]
        pulled = weighted(weights, pulls)
        gate_grad = gate * (1.0 - gate) * pulled
        grad_hidden = grad_mixed + gate_grad * wgate
        for k in range(NEIGH):
            grad_hidden = (
                grad_hidden + (scale * gate * weights[k] * (pulls[k] - pulled)) * e_ref[k]
            )
        grad_hidden_ref[0] = grad_hidden
        low = grad_hidden.astype(BF16)
        low_ref[here, :] = low
        gctx_own_ref[0] = dot(low, out_ref[...], 1, 1).astype(BF16)
        gctx_oth_ref[0] = dot(low, other_out(), 1, 1).astype(BF16)
        gate_wide = jnp.broadcast_to(gate, (TILE, BINS)).T
        low_edge = jnp.concatenate([edge_ref[0]] * (TILE // BINS), 1)
        high_edge = jnp.concatenate([edge_ref[1]] * (TILE // BINS), 1)
        mass = jnp.zeros_like(gate_wide)
        for k in range(NEIGH):
            ids = ids_ref[0, pl.ds(k, 1), :].astype(F32)
            mass = mass + jnp.where((ids >= low_edge) & (ids < high_edge), gate_wide, 0.0)
        gate_sum = jnp.sum(jnp.broadcast_to(gate, (TILE, width)), 0, keepdims=True)
        sums_ref[pl.ds(0, 1), :] += gain_part
        sums_ref[pl.ds(1, 1), :] += gate_sum
        sums_ref[pl.ds(2, 1), :] += jnp.sum(gate_grad * hidden, 0, keepdims=True)
        hist_ref[...] += mass

    kept = front()

    @pl.when(step == 0)
    def _():
        for copy in copies[3:]:
            copy.wait()

    back(kept, feed())

    @pl.when(step == pl.num_programs(0) - 1)
    def _():
        sums_ref[pl.ds(3, 1), pl.ds(0, BINS)] = jnp.sum(hist_ref[...].T, 0, keepdims=True)
        cut = sent_up_far.shape[1]
        moves = []
        for fars, which in (
            ((sent_up_far, sent_down_far), 1 - core),
            ((kept_up_far, kept_down_far), core),
        ):
            for side in range(2):
                at = pl.ds(pl.multiple_of((side * chunks + which) * width, width), width)
                here = pl.ds(pl.multiple_of((2 * side + which) * PAIR, PAIR), PAIR)
                slot = len(moves) // 2
                first = 0
                for left, right in (
                    (ffn_in_ref[...], gpre_ref[:, at]),
                    (act_ref[:, at], cots_ref[...]),
                    (ctx_ref[:, here], low_ref[...]),
                ):
                    piece = dot(left, right, 0, 0).astype(BF16)
                    stage_ref[slot, pl.ds(first, piece.shape[0]), :] = piece
                    first += piece.shape[0]
                for i, far in enumerate(fars):
                    move = pltpu.make_async_copy(
                        stage_ref.at[slot, pl.ds(i * cut, cut), :],
                        far.at[side],
                        out_sems.at[len(moves)],
                    )
                    move.start()
                    moves.append(move)
        for move in moves:
            move.wait()


def middle_layer(tokens, ctx_own, ctx_oth, nb, ids, cot, weights, received, edges, gains):
    rows, length, width = tokens.shape
    hidden_units = weights[1].shape[0]
    steps = length // TILE
    tiles = rows * steps
    count = rows * length
    assert hidden_units == 2 * width

    def place_of(i):
        return i // steps, i % steps

    def tiled(last):
        return pl.BlockSpec((1, TILE, last), lambda i: (*place_of(i), 0))

    def whole(shape):
        return pl.BlockSpec(shape, lambda i: (0,) * len(shape))

    far = pl.BlockSpec(memory_space=pl.ANY)
    return pl.pallas_call(
        middle_body,
        grid=(tiles,),
            in_specs=[
                tiled(width),
                tiled(width // 2),
                tiled(width // 2),
                pl.BlockSpec((1, TILE, NEIGH, width), lambda i: (*place_of(i), 0, 0)),
                pl.BlockSpec(
                    (1, NEIGH, TILE), lambda i: (place_of(i)[0], 0, place_of(i)[1])
                ),
                tiled(width),
                *[far] * 5,
                whole((1, BINS + 1)),
                whole((2, width)),
            ],
            out_specs=[
                tiled(width),
                tiled(width),
                tiled(width // 2),
                tiled(width // 2),
                far,
                far,
                far,
                far,
                whole((8, width)),
            ],
            scratch_shapes=[
                pltpu.VMEM((NEIGH, TILE, width), F32),
                pltpu.VMEM((BINS, TILE), F32),
                pltpu.VMEM((2, BINS, BINS), F32),
                pltpu.VMEM((NEIGH * GROUP, NEIGH * GROUP), BF16),
                *[pltpu.VMEM(w.shape, BF16) for w in weights],
                pltpu.VMEM((2, *received[0].shape), BF16),
                pltpu.VMEM((4, 2 * width + PAIR, width), BF16),
                pltpu.VMEM((count, width), BF16),
                pltpu.VMEM((count, 2 * hidden_units), BF16),
                pltpu.VMEM((count, 2 * hidden_units), BF16),
                pltpu.VMEM((count, width), BF16),
                pltpu.VMEM((count, width), BF16),
                pltpu.VMEM((count, width), BF16),
                pltpu.SemaphoreType.DMA((5,)),
                pltpu.SemaphoreType.DMA((8,)),
            ],
        out_shape=[
            jax.ShapeDtypeStruct((rows, length, width), BF16),
            jax.ShapeDtypeStruct((rows, length, width), F32),
            jax.ShapeDtypeStruct((rows, length, width // 2), BF16),
            jax.ShapeDtypeStruct((rows, length, width // 2), BF16),
            *[jax.ShapeDtypeStruct((2, width + PAIR // 2, width), BF16)] * 4,
            jax.ShapeDtypeStruct((8, width), F32),
        ],
        compiler_params=pltpu.CompilerParams(vmem_limit_bytes=VMEM_LIMIT),
        cost_estimate=pl.CostEstimate(flops=15 * 10**9, bytes_accessed=30 * 2**20, transcendentals=0),
    )(tokens, ctx_own, ctx_oth, nb, ids, cot, *weights, *received, edges, gains)


def attend_back(
    head, qkv_ref, p_ref, gctx_ref, ctx_ref, ds_ref, dq_ref, t_ref, dk_ref, dv_ref, with_memory
):
    length = ctx_ref.shape[1]
    grad = only_head(gctx_ref[0], head)
    delta = jnp.sum(grad.astype(F32) * ctx_ref[0].astype(F32), -1, keepdims=True)
    keys = only_head(qkv_ref[0, 0, pl.ds(length, 2 * length), :], head)
    lanes = pl.ds(pl.multiple_of(head * HEAD, HEAD), HEAD)
    low = 0 if with_memory else length
    for first in range(0, length, QROWS):
        rows = pl.ds(first, QROWS)
        high = length + first + QROWS
        here = pl.ds(low, high - low)
        probs = p_ref[0, 0, 0, rows, here].astype(F32)
        values = qkv_ref[0, 0, pl.ds(3 * length + low, high - low), :]
        grad_probs = dot(grad[first : first + QROWS], values, 1, 1)
        ds = (probs * (grad_probs - delta[first : first + QROWS])).astype(BF16)
        ds_ref[rows, here] = ds
        dq_ref[rows, :] += dot(ds, keys[low:high])
    for out_ref, left, right in (
        (dk_ref, t_ref[0, lanes, :], ds_ref),
        (dv_ref, t_ref[1, lanes, :], p_ref.at[0, 0, 0]),
    ):
        if not with_memory:
            out_ref[lanes, :length] = jnp.zeros((HEAD, length), BF16)
        for first in range(0, length, QROWS):
            start = low if first == 0 else length + first
            here = pl.ds(start, length + first + QROWS - start)
            out_ref[lanes, here] = dot(
                left[:, first:], right[pl.ds(first, length - first), here]
            ).astype(BF16)


def backward_body(
    starts_ref,
    qkv_ref,
    p_ref,
    gctx_ref,
    ctx_ref,
    kv_far,
    pack_ref,
    grads_ref,
    dw_ref,
    gain_ref,
    ds_ref,
    dq_ref,
    t_ref,
    dk_ref,
    dv_ref,
    acc_ref,
    kv_ref,
    sem,
):
    length = ctx_ref.shape[1]
    row = pl.program_id(1)
    head = pl.program_id(2)
    start = starts_ref[lax.axis_index("mp") * pl.num_programs(1) + row]
    fetch = pltpu.make_async_copy(kv_far.at[row], kv_ref, sem)
    args = (qkv_ref, p_ref, gctx_ref, ctx_ref, ds_ref, dq_ref, t_ref, dk_ref, dv_ref)

    @pl.when(head == 0)
    def _():
        fetch.start()
        dq_ref[...] = jnp.zeros_like(dq_ref)
        t_ref[0] = qkv_ref[0, 0, pl.ds(0, length), :].T
        t_ref[1] = gctx_ref[0].T

    @pl.when(start == 0)
    def _():
        attend_back(head, *args, True)

    @pl.when(start != 0)
    def _():
        attend_back(head, *args, False)

    @pl.when(head == 1)
    def _():
        dq_t = (dq_ref[...] * HEAD ** (-0.5)).astype(BF16).T
        grads_ref[0, 0, pl.ds(0, PAIR), :] = dq_t
        grads_ref[0, 0, pl.ds(PAIR, PAIR), :] = dk_ref[:, length:]
        grads_ref[0, 0, pl.ds(2 * PAIR, PAIR), :] = dv_ref[:, length:]
        fetch.wait()
        for i, add in enumerate(
            (
                dot(dq_t, kv_ref[pl.ds(length, length), :]),
                dot(dk_ref[...], kv_ref[...]),
                dot(dv_ref[...], kv_ref[...]),
            )
        ):
            acc_ref[i] = jnp.where(row == 0, add, acc_ref[i] + add)

    @pl.when((head == 1) & (row == pl.num_programs(1) - 1))
    def _():
        part = None
        for i in range(3):
            total = acc_ref[i]
            dw_ref[0, i] = total.astype(BF16)
            weight = pack_ref[:, pl.ds(i * PAIR, PAIR)].T.astype(F32)
            add = jnp.sum(total * weight, 0, keepdims=True)
            part = add if part is None else part + add
        gain_ref[0] = jnp.broadcast_to(part, gain_ref.shape[1:])


def attention_backward(starts, saved, gctx, kv, shift, many):
    pack, qkv, p, ctx = saved
    rows, _, _, length, _ = p.shape
    width = kv.shape[-1]

    def pair(n):
        return lax.rem(core_index() + shift + n, 2)

    return pl.pallas_call(
        backward_body,
        grid=(many, rows, 2),
        in_specs=[
            pl.BlockSpec(memory_space=pltpu.SMEM),
            pl.BlockSpec((1, 1, 5 * length, PAIR), lambda n, r, h: (r, pair(n), 0, 0)),
            pl.BlockSpec((1, 1, 1, length, 2 * length), lambda n, r, h: (r, pair(n), h, 0, 0)),
            pl.BlockSpec((1, length, PAIR), lambda n, r, h: (r, 0, pair(n))),
            pl.BlockSpec((1, length, PAIR), lambda n, r, h: (r, 0, pair(n))),
            pl.BlockSpec(memory_space=pl.ANY),
            pl.BlockSpec((width, 3 * PAIR), lambda n, r, h: (0, pair(n))),
        ],
        out_specs=[
            pl.BlockSpec((1, 1, 3 * PAIR, length), lambda n, r, h: (n, r, 0, 0)),
            pl.BlockSpec((1, 3, PAIR, width), lambda n, r, h: (n, 0, 0, 0)),
            pl.BlockSpec((1, 8, width), lambda n, r, h: (n, 0, 0)),
        ],
        scratch_shapes=[
            pltpu.VMEM((length, 2 * length), BF16),
            pltpu.VMEM((length, PAIR), F32),
            pltpu.VMEM((2, PAIR, length), BF16),
            pltpu.VMEM((PAIR, 2 * length), BF16),
            pltpu.VMEM((PAIR, 2 * length), BF16),
            pltpu.VMEM((3, PAIR, width), F32),
            pltpu.VMEM((2 * length, width), BF16),
            pltpu.SemaphoreType.DMA,
        ],
        out_shape=[
            jax.ShapeDtypeStruct((many, rows, 3 * PAIR, length), BF16),
            jax.ShapeDtypeStruct((many, 3, PAIR, width), BF16),
            jax.ShapeDtypeStruct((many, 8, width), F32),
        ],
        compiler_params=pltpu.CompilerParams(vmem_limit_bytes=BACKWARD_VMEM),
        cost_estimate=pl.CostEstimate(
            flops=4 * 10**9 * many, bytes_accessed=8 * 2**20 * many, transcendentals=0
        ),
    )(starts, qkv, p, gctx, ctx, kv, pack)


def input_body(
    tok_ref,
    grad_hidden_ref,
    gain_ref,
    oth_ref,
    own_first_ref,
    own_last_ref,
    oth_pack_ref,
    own_pack_ref,
    out_ref,
):
    core = core_index()
    total = None
    for block, pack, which in (
        (oth_ref[0, 0], oth_pack_ref, 1 - core),
        (oth_ref[1, 0], oth_pack_ref, core),
        (own_first_ref[0, 0], own_pack_ref, 1 - core),
        (own_last_ref[0, 0], own_pack_ref, core),
    ):
        here = pl.ds(pl.multiple_of(which * 3 * PAIR, 3 * PAIR), 3 * PAIR)
        add = dot(block, pack[:, here], 0, 1)
        total = add if total is None else total + add
    normal, rstd = normalize(tok_ref[0].astype(F32))
    grad = total * gain_ref[...]
    out_ref[0] = (
        grad_hidden_ref[0]
        + rstd
        * (
            grad
            - jnp.mean(grad, -1, keepdims=True)
            - normal * jnp.mean(grad * normal, -1, keepdims=True)
        )
    ).astype(BF16)


def input_grad(tokens, grad_hidden, gain, grads, packs):
    rows, length, width = tokens.shape
    row = pl.BlockSpec((1, length, width), lambda r: (r, 0, 0))

    def whole(array):
        return pl.BlockSpec(array.shape, lambda r: (0, 0))

    return pl.pallas_call(
        input_body,
        grid=(rows,),
        in_specs=[
            row,
            row,
            whole(gain),
            *[pl.BlockSpec((g.shape[0], 1) + g.shape[2:], lambda r: (0, r, 0, 0)) for g in grads],
            *[whole(p) for p in packs],
        ],
        out_specs=row,
        out_shape=jax.ShapeDtypeStruct(tokens.shape, BF16),
        compiler_params=pltpu.CompilerParams(vmem_limit_bytes=VMEM_LIMIT),
        cost_estimate=pl.CostEstimate(flops=2 * 10**9, bytes_accessed=8 * 2**20, transcendentals=0),
    )(tokens, grad_hidden, gain, *grads, *packs)


def finish_body(
    ffn_mine,
    ffn_sibling,
    attn_mine,
    attn_sibling,
    small_ref,
    q_far,
    k_far,
    v_far,
    out_far,
    up_far,
    down_far,
    gain_attn_ref,
    gain_ffn_ref,
    gate_ref,
    mean_ref,
    hist_ref,
    q_ref,
    k_ref,
    v_ref,
    out_ref,
    up_ref,
    down_ref,
    sems,
    tokens,
):
    core = core_index()
    width = up_far.shape[0]
    rows = attn_mine.shape[1]
    moves = []

    def pair(mine, sibling):
        return (
            jnp.where(core == 0, mine, sibling).astype(F32),
            jnp.where(core == 0, sibling, mine).astype(F32),
        )

    def move(near, far):
        moves.append(pltpu.make_async_copy(near, far, sems.at[len(moves)]))
        moves[-1].start()

    size = ffn_mine.shape[1] // 2
    pieces = [(x, pl.ds(y * size, size)) for y in range(2) for x in range(2)]
    halves = zip(*(pair(ffn_mine[x, y, :], ffn_sibling[x, y, :]) for x, y in pieces))
    for which, parts in enumerate(halves):
        rows_of = jnp.concatenate(parts, 0)
        to = pl.ds(which * width, width)
        up_ref[:, to] = rows_of[:width]
        down_ref[to, :] = rows_of[width : 2 * width]
        out_ref[pl.ds(which * PAIR, PAIR), :] = rows_of[2 * width :]
        move(down_ref.at[to, :], down_far.at[to, :])
    move(up_ref, up_far)
    move(out_ref, out_far)
    for i, (near, far) in enumerate(((q_ref, q_far), (k_ref, k_far), (v_ref, v_far))):
        first, last = pair(attn_mine[i], attn_sibling[pl.ds(i * rows, rows), :])
        near[...] = jnp.concatenate([first, last], 0).T
        move(near, far)
    count = small_ref.shape[0]
    below = attn_sibling[pl.ds(3 * rows, -(-3 * count // 16) * 16), :].astype(F32)
    small = small_ref[...]
    for i in range(3):
        small = small + below[i * count : (i + 1) * count]
    gain_ffn_ref[...] = small[0:1]
    mean_ref[...] = small[1:2, 0:1] / tokens
    gate_ref[...] = small[2:3]
    hist_ref[...] = small[3:4, :BINS] * (BINS / (tokens * NEIGH))
    gain_attn_ref[...] = small[4:5]
    for one in moves:
        one.wait()


def finish(ffn, attn, small, tokens):
    width = ffn[0].shape[-1]
    quarter = attn[0].shape[1]
    shapes = [(width, 2 * quarter)] * 3
    shapes += [(2 * quarter, width), (width, 2 * width), (2 * width, width)]
    rows = [(1, width)] * 3 + [(1, 1), (1, BINS)]

    def whole(array):
        return pl.BlockSpec(array.shape, lambda i: (0,) * array.ndim)

    return pl.pallas_call(
        functools.partial(finish_body, tokens=tokens),
        grid=(1,),
        in_specs=[whole(a) for a in (*ffn, *attn, small)],
        out_specs=[pl.BlockSpec(memory_space=pl.ANY)] * 6
        + [pl.BlockSpec(s, lambda i: (0, 0)) for s in rows],
        scratch_shapes=[pltpu.VMEM(s, F32) for s in shapes] + [pltpu.SemaphoreType.DMA((8,))],
        out_shape=[jax.ShapeDtypeStruct(s, F32) for s in shapes + rows],
        compiler_params=pltpu.CompilerParams(vmem_limit_bytes=FINISH_VMEM),
    )(*ffn, *attn, small)


def swap(array, axis, bit):
    size = lax.axis_size(axis)
    return lax.ppermute(array, axis, [(i, i ^ bit) for i in range(size)])


def bit_of(axis, bit):
    return (lax.axis_index(axis) // bit) % 2


def part_of(array, which, dim):
    half = array.shape[dim] // 2
    return lax.dynamic_slice_in_dim(array, which * half, half, dim)


def add_low(left, right):
    return (left.astype(F32) + right.astype(F32)).astype(BF16)


def join(mine, other, bit, dim):
    return jnp.where(
        bit_of("dp", bit) == 0,
        lax.concatenate([mine, other], dim),
        lax.concatenate([other, mine], dim),
    )


def swap_diagonal(array, first, last):
    size = lax.axis_size("dp")
    return lax.ppermute(array, "dp", [(i, i ^ first ^ last) for i in range(size)])


def join_four(mine, by_first, by_last, by_both, first, last):
    return join(
        join(mine, by_last, last, 0)[None], join(by_first, by_both, last, 0)[None], first, 0
    )


def after(value, *others):
    return lax.optimization_barrier((value, *others))[0]


class Chain:
    def __init__(self, array, dim):
        self.pieces = (array,)
        self.dim = dim

    def total(self, cut=lambda piece: piece):
        pieces = [cut(piece) for piece in self.pieces]
        if len(pieces) == 1:
            return pieces[0]
        return sum(piece.astype(F32) for piece in pieces).astype(BF16)

    def pass_on(self, sent, kept, bit, *others):
        self.sent = after(sent, *others)
        self.kept = kept
        self.come = swap(self.sent, "dp", bit)
        return self.sent

    def halve(self, bit, *others):
        mine = bit_of("dp", bit)
        self.sent = after(self.total(lambda p: part_of(p, 1 - mine, self.dim)), *others)
        self.kept = self.total(lambda p: part_of(p, mine, self.dim))
        self.come = swap(self.sent, "dp", bit)
        return self.sent

    def give(self, index, *others):
        self.sent = after(self.total(lambda p: p[index]), *others)
        self.kept = self.total(lambda p: p[1 - index])
        self.dim -= 1
        self.come = swap(self.sent, "mp", 1)
        return self.sent

    def send(self, bit, *others):
        self.sent = self.kept = after(self.total(), *others)
        self.come = swap(self.sent, "dp", bit)
        return self.sent

    def add(self, *others):
        self.come = after(self.come, *others)
        self.pieces = (self.kept, self.come)

    def join(self, bit, *others):
        self.pieces = (join(self.sent, after(self.come, *others), bit, self.dim),)


class Ride:
    def __init__(self, rows):
        self.rows = rows

    def below(self, array):
        left = self.rows
        parts = [array.reshape(-1, array.shape[-1])]
        for _ in range(3):
            part = lax.reduce_precision(left, 8, 7)
            parts.append(part.astype(BF16))
            left = left - part
        spare = -3 * left.shape[0] % 16
        parts.append(jnp.zeros((spare, left.shape[1]), BF16))
        return lax.concatenate(parts, 0)

    def add(self, block, like):
        size = like.size // like.shape[-1]
        count = self.rows.shape[0]
        for i in range(3):
            at = size + i * count
            self.rows = self.rows + block[at : at + count].astype(F32)
        return block[:size].reshape(like.shape)


def shards(
    tokens,
    memory,
    neighbours,
    neighbour_ids,
    doc_starts,
    bin_edges,
    w_query,
    w_key,
    w_value,
    w_out,
    w_up,
    w_down,
    gain_attn,
    gain_ffn,
    w_gate,
    cotangent,
):
    rows, length, width = tokens.shape
    count = rows * length
    dp = lax.axis_size("dp")
    core = bit_of("dp", 1)
    attn_gain = gain_attn.reshape(1, width)
    gains = jnp.stack([gain_ffn, w_gate])
    qkv = (w_query, w_key, w_value)
    far = []
    bit = 2
    while bit < dp:
        far.append(bit)
        bit *= 2

    qkv_sent = lax.concatenate([part_of(w, core, 0) for w in qkv], 1)
    up_part = part_of(w_up, core, 0)
    ffn_sent = lax.concatenate(
        [up_part[:, :width], up_part[:, width:], part_of(w_down, core, 0), part_of(w_out, core, 0)],
        0,
    )
    qkv_mine = swap(qkv_sent, "mp", 1)
    ffn_mine = swap(after(ffn_sent, qkv_sent), "mp", 1)
    kv, *own = attention_forward(
        doc_starts, after(tokens, qkv_sent, ffn_sent), memory, attn_gain, None, qkv
    )
    qkv_mine = after(qkv_mine, kv)
    qkv_got = (qkv_mine, swap(qkv_mine, "dp", 1))
    oth = attention_forward(doc_starts, tokens, memory, attn_gain, kv, qkv_got)
    ffn_mine = after(ffn_mine, oth[3])
    ffn_got = (ffn_mine, swap(ffn_mine, "dp", 1))
    ids = jnp.swapaxes(neighbour_ids, 1, 2)
    edges = bin_edges.reshape(1, BINS + 1)
    (
        result,
        grad_hidden,
        gctx_own,
        gctx_oth,
        sent_up,
        sent_down,
        kept_up,
        kept_down,
        sums,
    ) = middle_layer(
        tokens,
        own[3],
        oth[3],
        neighbours,
        ids,
        cotangent,
        (w_up, w_down, w_out),
        ffn_got,
        edges,
        gains,
    )
    up = Chain(None, 1)
    down = Chain(None, 1)
    up.pass_on(sent_up, kept_up, 1)
    down.pass_on(sent_down, kept_down, 1)
    up.add()
    down.add()
    sent = up.give(1)
    sent = down.halve(far[0], sent)
    g_oth, da, gain_oth = attention_backward(
        doc_starts, oth, after(gctx_oth, sent), kv, 1, 2
    )
    up.add(da)
    down.add(da)
    sent = up.halve(far[0])
    sent = down.give(1, sent)
    attn = Chain(None, 1)
    sent = attn.pass_on(da[0], da[1], 1, sent)
    g_own_first, da_first, gain_first = attention_backward(
        doc_starts, own, after(gctx_own, sent), kv, 1, 1
    )
    da_first = da_first[0]
    attn.add(da_first)
    up.add(da_first)
    down.add(da_first)
    both = Chain(None, 0)
    both.pieces = tuple(lax.concatenate([u, d], 0) for u, d in zip(up.pieces, down.pieces))
    sent = both.halve(far[1])
    attn_sent = after(attn.total(), sent)
    attn_come = swap(attn_sent, "mp", 1)
    first_sent = after(da_first, attn_sent)
    first_come = swap(first_sent, "dp", 1)
    g_own_last, da_last, gain_last = attention_backward(
        doc_starts, own, after(gctx_own, first_sent), kv, 0, 1
    )
    da_last = da_last[0]
    attn_come, first_come = lax.optimization_barrier((attn_come, first_come, da_last))[:2]
    attn = Chain(None, 1)
    attn.pieces = (da_last, first_come, attn_come)
    both.add(da_last)
    gain_part = sum(g[:, 0].sum(0) for g in (gain_oth, gain_first, gain_last))[None] / attn_gain
    small = lax.concatenate([sums[:4], gain_part], 0)
    first_bit, last_bit = far[:2]

    def quarter(piece, by_first, by_last):
        at = 2 * (bit_of("dp", first_bit) ^ by_first) + (bit_of("dp", last_bit) ^ by_last)
        size = piece.shape[1] // 4
        return lax.dynamic_slice_in_dim(piece, at * size, size, 1)

    sent_x = attn.total(lambda p: quarter(p, 1, 0))
    sent_z = attn.total(lambda p: quarter(p, 0, 1))
    sent_d = attn.total(lambda p: quarter(p, 1, 1))
    kept = attn.total(lambda p: quarter(p, 0, 0))
    come_x = swap(sent_x, "dp", first_bit)
    come_z = swap(sent_z, "dp", last_bit)
    come_d = swap_diagonal(sent_d, first_bit, last_bit)
    sent = both.send(far[2], sent_x, sent_z, sent_d)
    small_sent = after(small, sent)
    small_come = swap(small_sent, "mp", 1)
    grad_input = input_grad(
        tokens,
        after(grad_hidden, small_sent),
        attn_gain,
        (g_oth, g_own_first, g_own_last),
        (oth[0], own[0]),
    )
    come_x, come_z, come_d, small_come = lax.optimization_barrier(
        (come_x, come_z, come_d, small_come, grad_input)
    )[:4]
    ride = Ride(small_sent + small_come)
    total = sum(part.astype(F32) for part in (kept, come_x, come_z, come_d)).astype(BF16)
    for bit in far[2:]:
        sent = ride.below(total)
        come = swap(sent, "dp", bit)
        if bit == far[2]:
            come, both.come = lax.optimization_barrier((come, both.come))
        total = add_low(total, ride.add(come, total))
    ffn_sent = add_low(both.sent, both.come)
    for bit in far[3:]:
        ffn_sent = add_low(ffn_sent, swap(ffn_sent, "dp", bit))
    sent = ride.below(total)
    come_x = swap(sent, "dp", first_bit)
    come_z = swap(sent, "dp", last_bit)
    come_d = swap_diagonal(sent, first_bit, last_bit)
    ffn_sent = after(ffn_sent, sent)
    ffn_x = swap(ffn_sent, "dp", first_bit)
    ffn_z = swap(ffn_sent, "dp", last_bit)
    ffn_d = swap_diagonal(ffn_sent, first_bit, last_bit)
    come_x, come_z, come_d, ffn_x, ffn_z, ffn_d = lax.optimization_barrier(
        (come_x, come_z, come_d, ffn_x, ffn_z, ffn_d)
    )
    flat = total.reshape(-1, width)
    parts = [ride.add(come, flat) for come in (come_x, come_z, come_d)]
    shape = total.shape
    total = join_four(
        flat.reshape(shape).swapaxes(0, 1),
        *[part.reshape(shape).swapaxes(0, 1) for part in parts],
        far[0],
        far[1],
    )
    total = total.reshape(-1, *shape[:1], width).swapaxes(0, 1)
    sent = ride.below(total)
    come = swap(sent, "dp", 1)
    ffn_total = after(join_four(ffn_sent, ffn_x, ffn_z, ffn_d, far[0], far[1]), sent)
    ffn_come = swap(ffn_total, "dp", 1)
    grads = finish(
        (ffn_total, ffn_come),
        (total, come),
        ride.rows,
        count * dp * lax.axis_size("mp"),
    )
    gain_attn_sum, gain_ffn_sum, gate_sum, mean, histogram = grads[6:]
    return (
        result,
        grad_input,
        *grads[:6],
        gain_attn_sum.reshape(width),
        gain_ffn_sum.reshape(width),
        gate_sum.reshape(width),
        mean.reshape(()),
        histogram.reshape(BINS),
    )


def solution(mesh):
    in_specs = (
        P(("dp", "mp"), None, None),
        P("dp", None, None),
        P(("dp", "mp"), None, None, None),
        P(("dp", "mp"), None, None),
        P("dp"),
        P(),
        P(None, "mp"),
        P(None, "mp"),
        P(None, "mp"),
        P("mp", None),
        P(None, "mp"),
        P("mp", None),
        P(),
        P(),
        P(),
        P(("dp", "mp"), None, None),
    )
    out_specs = (
        P(("dp", "mp"), None, None),
        P(("dp", "mp"), None, None),
        P(None, "mp"),
        P(None, "mp"),
        P(None, "mp"),
        P("mp", None),
        P(None, "mp"),
        P("mp", None),
        P(),
        P(),
        P(),
        P(),
        P(),
    )
    return jax.shard_map(shards, mesh=mesh, in_specs=in_specs, out_specs=out_specs, check_vma=False)
```

```python
import functools

import jax
import jax.numpy as jnp
from jax import lax
from jax.experimental import pallas as pl
from jax.experimental.pallas import tpu as pltpu
from jax.sharding import PartitionSpec as P

HEAD = 64
NEIGH = 4
BINS = 128
PAIR = 2 * HEAD
QROWS = 256
TILE = 256
GROUP = 64

EPS = 1e-05
BF16 = jnp.bfloat16
F32 = jnp.float32
VMEM_LIMIT = 56 * 1024 * 1024
FORWARD_VMEM = 52 * 1024 * 1024
BACKWARD_VMEM = 48 * 1024 * 1024
FINISH_VMEM = 24 * 1024 * 1024


def dot(left, right, left_dim=1, right_dim=0):
    return lax.dot_general(
        left, right, (((left_dim,), (right_dim,)), ((), ())), preferred_element_type=F32
    )


def normalize(values):
    centre = values - jnp.mean(values, -1, keepdims=True)
    spread = jnp.mean(centre * centre, -1, keepdims=True)
    rstd = lax.rsqrt(spread + EPS)
    return centre * rstd, rstd


def core_index():
    return lax.rem(lax.axis_index("dp"), 2)


def head_lanes(rows, head):
    lane = lax.broadcasted_iota(jnp.int32, (rows, PAIR), 1)
    return (lane >= head * HEAD) & (lane < (head + 1) * HEAD)


def only_head(block, head):
    return jnp.where(head_lanes(block.shape[0], head), block, jnp.zeros_like(block))


def attend(qkv_ref, p_ref, ctx_ref, length, with_memory):
    values = [only_head(qkv_ref[0, 0, pl.ds(3 * length, 2 * length), :], head) for head in range(2)]
    low = 0 if with_memory else length
    for first in range(0, length, QROWS):
        rows = pl.ds(first, QROWS)
        high = length + first + QROWS
        total = None
        for head in range(2):
            query = only_head(qkv_ref[0, 0, rows, :], head)
            scores = dot(query, qkv_ref[0, 0, pl.ds(length + low, high - low), :], 1, 1)
            seg = scores[:, length - low :]
            at = lax.broadcasted_iota(jnp.int32, seg.shape, 0) + first
            key = lax.broadcasted_iota(jnp.int32, seg.shape, 1)
            seg = jnp.where(key <= at, seg, -1e30)
            top = jnp.max(seg, -1, keepdims=True)
            if with_memory:
                mem = scores[:, :length]
                top = jnp.maximum(top, jnp.max(mem, -1, keepdims=True))
                mem = jnp.exp(mem - top)
            probs = jnp.exp(seg - top)
            mass = jnp.sum(probs, -1, keepdims=True)
            if with_memory:
                mass = mass + jnp.sum(mem, -1, keepdims=True)
            part = 1.0 / mass
            probs = (probs * part).astype(BF16)
            if with_memory:
                probs = jnp.concatenate([(mem * part).astype(BF16), probs], 1)
            p_ref[0, 0, head, rows, pl.ds(low, high - low)] = probs
            add = dot(probs, values[head][low:high])
            total = add if total is None else total + add
        ctx_ref[0, rows, :] = total.astype(BF16)


def forward_body(starts_ref, kv_ref, pack_ref, qkv_ref, p_ref, ctx_ref):
    length = kv_ref.shape[1] // 2
    pair = pl.program_id(1)
    kv = kv_ref[0]
    here = pl.multiple_of(3 * pair * PAIR, PAIR)
    query = dot(kv[length:], pack_ref[:, pl.ds(here, PAIR)]).astype(BF16)
    qkv_ref[0, 0, pl.ds(0, length), :] = (query.astype(F32) * HEAD ** (-0.5)).astype(BF16)
    both = dot(kv, pack_ref[:, pl.ds(here + PAIR, 2 * PAIR)]).astype(BF16)
    qkv_ref[0, 0, pl.ds(length, 2 * length), :] = both[:, :PAIR]
    qkv_ref[0, 0, pl.ds(3 * length, 2 * length), :] = both[:, PAIR:]
    start = starts_ref[lax.axis_index("mp") * pl.num_programs(0) + pl.program_id(0)]

    @pl.when(start == 0)
    def _():
        attend(qkv_ref, p_ref, ctx_ref, length, True)

    @pl.when(start != 0)
    def _():
        attend(qkv_ref, p_ref, ctx_ref, length, False)


def first_forward(
    starts_ref, tok_ref, mem_ref, gain_ref, wq_ref, wk_ref, wv_ref, kv_ref, pack_ref, *outs
):
    length = tok_ref.shape[1]

    @pl.when((pl.program_id(0) == 0) & (pl.program_id(1) == 0))
    def _():
        for i, weight in enumerate((wq_ref, wk_ref, wv_ref)):
            for p in range(2):
                pack_ref[:, pl.ds((3 * p + i) * PAIR, PAIR)] = weight[:, pl.ds(p * PAIR, PAIR)]

    @pl.when(pl.program_id(1) == 0)
    def _():
        gain = gain_ref[...]
        kv_ref[0, pl.ds(0, length), :] = (normalize(mem_ref[0].astype(F32))[0] * gain).astype(BF16)
        kv_ref[0, pl.ds(length, length), :] = (
            normalize(tok_ref[0].astype(F32))[0] * gain
        ).astype(BF16)

    forward_body(starts_ref, kv_ref, pack_ref, *outs)


def second_forward(starts_ref, kv_ref, mine_ref, sibling_ref, pack_ref, *outs):
    rows = mine_ref.shape[0]
    core = core_index()

    @pl.when((pl.program_id(0) == 0) & (pl.program_id(1) == 0))
    def _():
        for block, which in ((mine_ref, core), (sibling_ref, 1 - core)):
            to = pl.ds(pl.multiple_of(which * rows, rows), rows)
            for i in range(3):
                for p in range(2):
                    pack_ref[to, pl.ds((3 * p + i) * PAIR, PAIR)] = block[
                        :, pl.ds((2 * i + p) * PAIR, PAIR)
                    ]

    forward_body(starts_ref, kv_ref, pack_ref, *outs)


def attention_forward(starts, tokens, memory, gain, kv, weights):
    rows, length, width = tokens.shape
    pairs = 2
    pack = (width, 3 * pairs * PAIR)
    outs = [
        jax.ShapeDtypeStruct(pack, BF16),
        jax.ShapeDtypeStruct((rows, pairs, 5 * length, PAIR), BF16),
        jax.ShapeDtypeStruct((rows, pairs, 2, length, 2 * length), BF16),
        jax.ShapeDtypeStruct((rows, length, pairs * PAIR), BF16),
    ]
    out_specs = [
        pl.BlockSpec(pack, lambda r, p: (0, 0)),
        pl.BlockSpec((1, 1, 5 * length, PAIR), lambda r, p: (r, p, 0, 0)),
        pl.BlockSpec((1, 1, 2, length, 2 * length), lambda r, p: (r, p, 0, 0, 0)),
        pl.BlockSpec((1, length, PAIR), lambda r, p: (r, 0, p)),
    ]
    kv_spec = pl.BlockSpec((1, 2 * length, width), lambda r, p: (r, 0, 0))
    in_specs = [pl.BlockSpec(memory_space=pltpu.SMEM)]
    if kv is None:
        body = first_forward
        ins = [tokens, memory, gain]
        in_specs += [
            pl.BlockSpec((1, length, width), lambda r, p: (r, 0, 0)),
            pl.BlockSpec((1, length, width), lambda r, p: (lax.axis_index("mp") * rows + r, 0, 0)),
            pl.BlockSpec((1, width), lambda r, p: (0, 0)),
        ]
        outs = [jax.ShapeDtypeStruct((rows, 2 * length, width), BF16)] + outs
        out_specs = [kv_spec] + out_specs
    else:
        body = second_forward
        ins = [kv]
        in_specs += [kv_spec]
    in_specs += [pl.BlockSpec(w.shape, lambda r, p: (0, 0)) for w in weights]
    return pl.pallas_call(
        body,
        grid=(rows, pairs),
        in_specs=in_specs,
        out_specs=out_specs,
        out_shape=outs,
        compiler_params=pltpu.CompilerParams(vmem_limit_bytes=FORWARD_VMEM),
        cost_estimate=pl.CostEstimate(flops=6 * 10**9, bytes_accessed=16 * 2**20, transcendentals=0),
    )(starts, *ins, *weights)


def gelu_parts(pre):
    c0 = 0.7978845608028654
    c1 = c0 * 0.044715
    square = pre * pre
    part = 0.5 * jnp.tanh(pre * (c1 * square + c0)) + 0.5
    act = pre * part
    return act, part + act * (1.0 - part) * ((6.0 * c1) * square + 2.0 * c0)


def weighted(weights, values):
    return sum(w * v for w, v in zip(weights[1:], values[1:])) + weights[0] * values[0]


def middle_body(
    tok_ref,
    ctx_own_ref,
    ctx_oth_ref,
    nb_ref,
    ids_ref,
    cot_ref,
    up_far,
    down_far,
    out_far,
    mine_far,
    sibling_far,
    edges_ref,
    gains_ref,
    result_ref,
    grad_hidden_ref,
    gctx_own_ref,
    gctx_oth_ref,
    sent_up_far,
    sent_down_far,
    kept_up_far,
    kept_down_far,
    sums_ref,
    e_ref,
    hist_ref,
    edge_ref,
    pick_ref,
    up_ref,
    down_ref,
    out_ref,
    oth_ref,
    stage_ref,
    ffn_in_ref,
    act_ref,
    gpre_ref,
    cots_ref,
    low_ref,
    ctx_ref,
    in_sems,
    out_sems,
):
    step = pl.program_id(0)
    here = pl.ds(pl.multiple_of(step * TILE, TILE), TILE)
    width = tok_ref.shape[-1]
    hidden_units = down_ref.shape[0]
    half = width // 2
    chunks = hidden_units // width
    scale = width ** (-0.5)
    core = core_index()
    copies = [
        pltpu.make_async_copy(far, near, in_sems.at[i])
        for i, (far, near) in enumerate(
            (
                (out_far, out_ref),
                (mine_far, oth_ref.at[core]),
                (sibling_far, oth_ref.at[1 - core]),
                (up_far, up_ref),
                (down_far, down_ref),
            )
        )
    ]

    @pl.when(step == 0)
    def _():
        for copy in copies:
            copy.start()
        sums_ref[...] = jnp.zeros_like(sums_ref)
        hist_ref[...] = jnp.zeros_like(hist_ref)
        row = lax.broadcasted_iota(jnp.int32, pick_ref.shape, 0)
        column = lax.broadcasted_iota(jnp.int32, pick_ref.shape, 1)
        from_row = NEIGH * (row % GROUP) + row // GROUP
        pick_ref[...] = (column == from_row).astype(F32).astype(BF16)
        edges = edges_ref[...].astype(F32)
        for i in range(2):
            edge_ref[i] = jnp.broadcast_to(edges[:, i : i + BINS], (BINS, BINS)).T
        for copy in copies[:3]:
            copy.wait()

    def other_out():
        at = pl.ds(2 * width, half // 2)
        return jnp.concatenate([oth_ref[0, at, :], oth_ref[1, at, :]], 0)

    wgate = gains_ref[pl.ds(1, 1), :]
    gain = gains_ref[pl.ds(0, 1), :]

    def front():
        ctx_ref[here, pl.ds(0, half)] = ctx_own_ref[0]
        ctx_ref[here, pl.ds(half, half)] = ctx_oth_ref[0]
        cots_ref[here, :] = cot_ref[0]
        hidden = (
            tok_ref[0].astype(F32)
            + dot(ctx_own_ref[0], out_ref[...])
            + dot(ctx_oth_ref[0], other_out())
        )
        for first in range(0, TILE, GROUP):
            mixed_rows = nb_ref[0, pl.ds(first, GROUP)].reshape(NEIGH * GROUP, width)
            planes = dot(pick_ref[...], mixed_rows)
            for k in range(NEIGH):
                e_ref[k, pl.ds(first, GROUP), :] = planes[k * GROUP : (k + 1) * GROUP]
        affinity = [
            jnp.sum(e_ref[k] * hidden, -1, keepdims=True) * scale for k in range(NEIGH)
        ]
        top = jnp.maximum(
            jnp.maximum(affinity[0], affinity[1]), jnp.maximum(affinity[2], affinity[3])
        )
        raised = [jnp.exp(a - top) for a in affinity]
        inverse = 1.0 / (raised[0] + raised[1] + raised[2] + raised[3])
        weights = [a * inverse for a in raised]
        gate = jax.nn.sigmoid(jnp.sum(hidden * wgate, -1, keepdims=True))
        recalled = weighted(weights, [e_ref[k] for k in range(NEIGH)])
        mixed = hidden + gate * recalled
        normal, rstd = normalize(mixed)
        ffn_in_ref[here, :] = (normal * gain).astype(BF16)
        return hidden, weights, gate, mixed, normal, rstd

    def feed():
        ffn_in = ffn_in_ref[here, :]
        cot = cot_ref[0]
        down_sum = None
        grad_sum = None
        for side in range(2):
            for c in range(chunks):
                if side == 0:
                    up = up_ref[:, pl.ds(c * width, width)]
                    down = down_ref[pl.ds(c * width, width), :]
                else:
                    part = pl.ds(c * half, half)
                    up = jnp.concatenate([oth_ref[0, part, :], oth_ref[1, part, :]], 0)
                    down = oth_ref[c, pl.ds(width, width), :]
                at = pl.ds((side * chunks + c) * width, width)
                act, slope = gelu_parts(dot(ffn_in, up))
                act = act.astype(BF16)
                gpre = (dot(cot, down, 1, 1) * slope).astype(BF16)
                act_ref[here, at] = act
                gpre_ref[here, at] = gpre
                add = dot(act, down)
                down_sum = add if down_sum is None else down_sum + add
                add = dot(gpre, up, 1, 1)
                grad_sum = add if grad_sum is None else grad_sum + add
        return down_sum, grad_sum

    def back(kept, sums):
        hidden, weights, gate, mixed, normal, rstd = kept
        down_sum, grad_sum = sums
        result_ref[0] = (mixed + down_sum).astype(BF16)
        gain_part = jnp.sum(grad_sum * normal, 0, keepdims=True)
        grad_normal = grad_sum * gain
        grad_mixed = cot_ref[0].astype(F32) + rstd * (
            grad_normal
            - jnp.mean(grad_normal, -1, keepdims=True)
            - normal * jnp.mean(grad_normal * normal, -1, keepdims=True)
        )
        pulls = [
            jnp.sum(grad_mixed * e_ref[k], -1, keepdims=True) for k in range(NEIGH)
        ]
        pulled = weighted(weights, pulls)
        gate_grad = gate * (1.0 - gate) * pulled
        grad_hidden = grad_mixed + gate_grad * wgate
        for k in range(NEIGH):
            grad_hidden = (
                grad_hidden + (scale * gate * weights[k] * (pulls[k] - pulled)) * e_ref[k]
            )
        grad_hidden_ref[0] = grad_hidden
        low = grad_hidden.astype(BF16)
        low_ref[here, :] = low
        gctx_own_ref[0] = dot(low, out_ref[...], 1, 1).astype(BF16)
        gctx_oth_ref[0] = dot(low, other_out(), 1, 1).astype(BF16)
        gate_wide = jnp.broadcast_to(gate, (TILE, BINS)).T
        low_edge = jnp.concatenate([edge_ref[0]] * (TILE // BINS), 1)
        high_edge = jnp.concatenate([edge_ref[1]] * (TILE // BINS), 1)
        mass = jnp.zeros_like(gate_wide)
        for k in range(NEIGH):
            ids = ids_ref[0, pl.ds(k, 1), :].astype(F32)
            mass = mass + jnp.where((ids >= low_edge) & (ids < high_edge), gate_wide, 0.0)
        gate_sum = jnp.sum(jnp.broadcast_to(gate, (TILE, width)), 0, keepdims=True)
        sums_ref[pl.ds(0, 1), :] += gain_part
        sums_ref[pl.ds(1, 1), :] += gate_sum
        sums_ref[pl.ds(2, 1), :] += jnp.sum(gate_grad * hidden, 0, keepdims=True)
        hist_ref[...] += mass

    kept = front()

    @pl.when(step == 0)
    def _():
        for copy in copies[3:]:
            copy.wait()

    back(kept, feed())

    @pl.when(step == pl.num_programs(0) - 1)
    def _():
        sums_ref[pl.ds(3, 1), pl.ds(0, BINS)] = jnp.sum(hist_ref[...].T, 0, keepdims=True)
        cut = sent_up_far.shape[1]
        moves = []
        for fars, which in (
            ((sent_up_far, sent_down_far), 1 - core),
            ((kept_up_far, kept_down_far), core),
        ):
            for side in range(2):
                at = pl.ds(pl.multiple_of((side * chunks + which) * width, width), width)
                here = pl.ds(pl.multiple_of((2 * side + which) * PAIR, PAIR), PAIR)
                slot = len(moves) // 2
                first = 0
                for left, right in (
                    (ffn_in_ref[...], gpre_ref[:, at]),
                    (act_ref[:, at], cots_ref[...]),
                    (ctx_ref[:, here], low_ref[...]),
                ):
                    piece = dot(left, right, 0, 0).astype(BF16)
                    stage_ref[slot, pl.ds(first, piece.shape[0]), :] = piece
                    first += piece.shape[0]
                for i, far in enumerate(fars):
                    move = pltpu.make_async_copy(
                        stage_ref.at[slot, pl.ds(i * cut, cut), :],
                        far.at[side],
                        out_sems.at[len(moves)],
                    )
                    move.start()
                    moves.append(move)
        for move in moves:
            move.wait()


def middle_layer(tokens, ctx_own, ctx_oth, nb, ids, cot, weights, received, edges, gains):
    rows, length, width = tokens.shape
    hidden_units = weights[1].shape[0]
    steps = length // TILE
    tiles = rows * steps
    count = rows * length
    assert hidden_units == 2 * width

    def place_of(i):
        return i // steps, i % steps

    def tiled(last):
        return pl.BlockSpec((1, TILE, last), lambda i: (*place_of(i), 0))

    def whole(shape):
        return pl.BlockSpec(shape, lambda i: (0,) * len(shape))

    far = pl.BlockSpec(memory_space=pl.ANY)
    return pl.pallas_call(
        middle_body,
        grid=(tiles,),
            in_specs=[
                tiled(width),
                tiled(width // 2),
                tiled(width // 2),
                pl.BlockSpec((1, TILE, NEIGH, width), lambda i: (*place_of(i), 0, 0)),
                pl.BlockSpec(
                    (1, NEIGH, TILE), lambda i: (place_of(i)[0], 0, place_of(i)[1])
                ),
                tiled(width),
                *[far] * 5,
                whole((1, BINS + 1)),
                whole((2, width)),
            ],
            out_specs=[
                tiled(width),
                tiled(width),
                tiled(width // 2),
                tiled(width // 2),
                far,
                far,
                far,
                far,
                whole((8, width)),
            ],
            scratch_shapes=[
                pltpu.VMEM((NEIGH, TILE, width), F32),
                pltpu.VMEM((BINS, TILE), F32),
                pltpu.VMEM((2, BINS, BINS), F32),
                pltpu.VMEM((NEIGH * GROUP, NEIGH * GROUP), BF16),
                *[pltpu.VMEM(w.shape, BF16) for w in weights],
                pltpu.VMEM((2, *received[0].shape), BF16),
                pltpu.VMEM((4, 2 * width + PAIR, width), BF16),
                pltpu.VMEM((count, width), BF16),
                pltpu.VMEM((count, 2 * hidden_units), BF16),
                pltpu.VMEM((count, 2 * hidden_units), BF16),
                pltpu.VMEM((count, width), BF16),
                pltpu.VMEM((count, width), BF16),
                pltpu.VMEM((count, width), BF16),
                pltpu.SemaphoreType.DMA((5,)),
                pltpu.SemaphoreType.DMA((8,)),
            ],
        out_shape=[
            jax.ShapeDtypeStruct((rows, length, width), BF16),
            jax.ShapeDtypeStruct((rows, length, width), F32),
            jax.ShapeDtypeStruct((rows, length, width // 2), BF16),
            jax.ShapeDtypeStruct((rows, length, width // 2), BF16),
            *[jax.ShapeDtypeStruct((2, width + PAIR // 2, width), BF16)] * 4,
            jax.ShapeDtypeStruct((8, width), F32),
        ],
        compiler_params=pltpu.CompilerParams(vmem_limit_bytes=VMEM_LIMIT),
        cost_estimate=pl.CostEstimate(flops=15 * 10**9, bytes_accessed=30 * 2**20, transcendentals=0),
    )(tokens, ctx_own, ctx_oth, nb, ids, cot, *weights, *received, edges, gains)


def attend_back(
    head, qkv_ref, p_ref, gctx_ref, ctx_ref, ds_ref, dq_ref, t_ref, dk_ref, dv_ref, with_memory
):
    length = ctx_ref.shape[1]
    grad = only_head(gctx_ref[0], head)
    delta = jnp.sum(grad.astype(F32) * ctx_ref[0].astype(F32), -1, keepdims=True)
    keys = only_head(qkv_ref[0, 0, pl.ds(length, 2 * length), :], head)
    lanes = pl.ds(pl.multiple_of(head * HEAD, HEAD), HEAD)
    low = 0 if with_memory else length
    for first in range(0, length, QROWS):
        rows = pl.ds(first, QROWS)
        high = length + first + QROWS
        here = pl.ds(low, high - low)
        probs = p_ref[0, 0, 0, rows, here].astype(F32)
        values = qkv_ref[0, 0, pl.ds(3 * length + low, high - low), :]
        grad_probs = dot(grad[first : first + QROWS], values, 1, 1)
        ds = (probs * (grad_probs - delta[first : first + QROWS])).astype(BF16)
        ds_ref[rows, here] = ds
        dq_ref[rows, :] += dot(ds, keys[low:high])
    for out_ref, left, right in (
        (dk_ref, t_ref[0, lanes, :], ds_ref),
        (dv_ref, t_ref[1, lanes, :], p_ref.at[0, 0, 0]),
    ):
        if not with_memory:
            out_ref[lanes, :length] = jnp.zeros((HEAD, length), BF16)
        for first in range(0, length, QROWS):
            start = low if first == 0 else length + first
            here = pl.ds(start, length + first + QROWS - start)
            out_ref[lanes, here] = dot(
                left[:, first:], right[pl.ds(first, length - first), here]
            ).astype(BF16)


def backward_body(
    starts_ref,
    qkv_ref,
    p_ref,
    gctx_ref,
    ctx_ref,
    kv_far,
    pack_ref,
    grads_ref,
    dw_ref,
    gain_ref,
    ds_ref,
    dq_ref,
    t_ref,
    dk_ref,
    dv_ref,
    acc_ref,
    kv_ref,
    sem,
):
    length = ctx_ref.shape[1]
    row = pl.program_id(1)
    head = pl.program_id(2)
    start = starts_ref[lax.axis_index("mp") * pl.num_programs(1) + row]
    fetch = pltpu.make_async_copy(kv_far.at[row], kv_ref, sem)
    args = (qkv_ref, p_ref, gctx_ref, ctx_ref, ds_ref, dq_ref, t_ref, dk_ref, dv_ref)

    @pl.when(head == 0)
    def _():
        fetch.start()
        dq_ref[...] = jnp.zeros_like(dq_ref)
        t_ref[0] = qkv_ref[0, 0, pl.ds(0, length), :].T
        t_ref[1] = gctx_ref[0].T

    @pl.when(start == 0)
    def _():
        attend_back(head, *args, True)

    @pl.when(start != 0)
    def _():
        attend_back(head, *args, False)

    @pl.when(head == 1)
    def _():
        dq_t = (dq_ref[...] * HEAD ** (-0.5)).astype(BF16).T
        grads_ref[0, 0, pl.ds(0, PAIR), :] = dq_t
        grads_ref[0, 0, pl.ds(PAIR, PAIR), :] = dk_ref[:, length:]
        grads_ref[0, 0, pl.ds(2 * PAIR, PAIR), :] = dv_ref[:, length:]
        fetch.wait()
        for i, add in enumerate(
            (
                dot(dq_t, kv_ref[pl.ds(length, length), :]),
                dot(dk_ref[...], kv_ref[...]),
                dot(dv_ref[...], kv_ref[...]),
            )
        ):
            acc_ref[i] = jnp.where(row == 0, add, acc_ref[i] + add)

    @pl.when((head == 1) & (row == pl.num_programs(1) - 1))
    def _():
        part = None
        for i in range(3):
            total = acc_ref[i]
            dw_ref[0, i] = total.astype(BF16)
            weight = pack_ref[:, pl.ds(i * PAIR, PAIR)].T.astype(F32)
            add = jnp.sum(total * weight, 0, keepdims=True)
            part = add if part is None else part + add
        gain_ref[0] = jnp.broadcast_to(part, gain_ref.shape[1:])


def attention_backward(starts, saved, gctx, kv, shift, many):
    pack, qkv, p, ctx = saved
    rows, _, _, length, _ = p.shape
    width = kv.shape[-1]

    def pair(n):
        return lax.rem(core_index() + shift + n, 2)

    return pl.pallas_call(
        backward_body,
        grid=(many, rows, 2),
        in_specs=[
            pl.BlockSpec(memory_space=pltpu.SMEM),
            pl.BlockSpec((1, 1, 5 * length, PAIR), lambda n, r, h: (r, pair(n), 0, 0)),
            pl.BlockSpec((1, 1, 1, length, 2 * length), lambda n, r, h: (r, pair(n), h, 0, 0)),
            pl.BlockSpec((1, length, PAIR), lambda n, r, h: (r, 0, pair(n))),
            pl.BlockSpec((1, length, PAIR), lambda n, r, h: (r, 0, pair(n))),
            pl.BlockSpec(memory_space=pl.ANY),
            pl.BlockSpec((width, 3 * PAIR), lambda n, r, h: (0, pair(n))),
        ],
        out_specs=[
            pl.BlockSpec((1, 1, 3 * PAIR, length), lambda n, r, h: (n, r, 0, 0)),
            pl.BlockSpec((1, 3, PAIR, width), lambda n, r, h: (n, 0, 0, 0)),
            pl.BlockSpec((1, 8, width), lambda n, r, h: (n, 0, 0)),
        ],
        scratch_shapes=[
            pltpu.VMEM((length, 2 * length), BF16),
            pltpu.VMEM((length, PAIR), F32),
            pltpu.VMEM((2, PAIR, length), BF16),
            pltpu.VMEM((PAIR, 2 * length), BF16),
            pltpu.VMEM((PAIR, 2 * length), BF16),
            pltpu.VMEM((3, PAIR, width), F32),
            pltpu.VMEM((2 * length, width), BF16),
            pltpu.SemaphoreType.DMA,
        ],
        out_shape=[
            jax.ShapeDtypeStruct((many, rows, 3 * PAIR, length), BF16),
            jax.ShapeDtypeStruct((many, 3, PAIR, width), BF16),
            jax.ShapeDtypeStruct((many, 8, width), F32),
        ],
        compiler_params=pltpu.CompilerParams(vmem_limit_bytes=BACKWARD_VMEM),
        cost_estimate=pl.CostEstimate(
            flops=4 * 10**9 * many, bytes_accessed=8 * 2**20 * many, transcendentals=0
        ),
    )(starts, qkv, p, gctx, ctx, kv, pack)


def input_body(
    tok_ref,
    grad_hidden_ref,
    gain_ref,
    oth_ref,
    own_first_ref,
    own_last_ref,
    oth_pack_ref,
    own_pack_ref,
    out_ref,
):
    core = core_index()
    total = None
    for block, pack, which in (
        (oth_ref[0, 0], oth_pack_ref, 1 - core),
        (oth_ref[1, 0], oth_pack_ref, core),
        (own_first_ref[0, 0], own_pack_ref, 1 - core),
        (own_last_ref[0, 0], own_pack_ref, core),
    ):
        here = pl.ds(pl.multiple_of(which * 3 * PAIR, 3 * PAIR), 3 * PAIR)
        add = dot(block, pack[:, here], 0, 1)
        total = add if total is None else total + add
    normal, rstd = normalize(tok_ref[0].astype(F32))
    grad = total * gain_ref[...]
    out_ref[0] = (
        grad_hidden_ref[0]
        + rstd
        * (
            grad
            - jnp.mean(grad, -1, keepdims=True)
            - normal * jnp.mean(grad * normal, -1, keepdims=True)
        )
    ).astype(BF16)


def input_grad(tokens, grad_hidden, gain, grads, packs):
    rows, length, width = tokens.shape
    row = pl.BlockSpec((1, length, width), lambda r: (r, 0, 0))

    def whole(array):
        return pl.BlockSpec(array.shape, lambda r: (0, 0))

    return pl.pallas_call(
        input_body,
        grid=(rows,),
        in_specs=[
            row,
            row,
            whole(gain),
            *[pl.BlockSpec((g.shape[0], 1) + g.shape[2:], lambda r: (0, r, 0, 0)) for g in grads],
            *[whole(p) for p in packs],
        ],
        out_specs=row,
        out_shape=jax.ShapeDtypeStruct(tokens.shape, BF16),
        compiler_params=pltpu.CompilerParams(vmem_limit_bytes=VMEM_LIMIT),
        cost_estimate=pl.CostEstimate(flops=2 * 10**9, bytes_accessed=8 * 2**20, transcendentals=0),
    )(tokens, grad_hidden, gain, *grads, *packs)


def finish_body(
    ffn_mine,
    ffn_sibling,
    attn_mine,
    attn_sibling,
    small_ref,
    q_far,
    k_far,
    v_far,
    out_far,
    up_far,
    down_far,
    gain_attn_ref,
    gain_ffn_ref,
    gate_ref,
    mean_ref,
    hist_ref,
    q_ref,
    k_ref,
    v_ref,
    out_ref,
    up_ref,
    down_ref,
    sems,
    tokens,
):
    core = core_index()
    width = up_far.shape[0]
    rows = attn_mine.shape[1]
    moves = []

    def pair(mine, sibling):
        return (
            jnp.where(core == 0, mine, sibling).astype(F32),
            jnp.where(core == 0, sibling, mine).astype(F32),
        )

    def move(near, far):
        moves.append(pltpu.make_async_copy(near, far, sems.at[len(moves)]))
        moves[-1].start()

    size = ffn_mine.shape[1] // 2
    pieces = [(x, pl.ds(y * size, size)) for y in range(2) for x in range(2)]
    halves = zip(*(pair(ffn_mine[x, y, :], ffn_sibling[x, y, :]) for x, y in pieces))
    for which, parts in enumerate(halves):
        rows_of = jnp.concatenate(parts, 0)
        to = pl.ds(which * width, width)
        up_ref[:, to] = rows_of[:width]
        down_ref[to, :] = rows_of[width : 2 * width]
        out_ref[pl.ds(which * PAIR, PAIR), :] = rows_of[2 * width :]
        move(down_ref.at[to, :], down_far.at[to, :])
    move(up_ref, up_far)
    move(out_ref, out_far)
    for i, (near, far) in enumerate(((q_ref, q_far), (k_ref, k_far), (v_ref, v_far))):
        first, last = pair(attn_mine[i], attn_sibling[pl.ds(i * rows, rows), :])
        near[...] = jnp.concatenate([first, last], 0).T
        move(near, far)
    count = small_ref.shape[0]
    below = attn_sibling[pl.ds(3 * rows, -(-3 * count // 16) * 16), :].astype(F32)
    small = small_ref[...]
    for i in range(3):
        small = small + below[i * count : (i + 1) * count]
    gain_ffn_ref[...] = small[0:1]
    mean_ref[...] = small[1:2, 0:1] / tokens
    gate_ref[...] = small[2:3]
    hist_ref[...] = small[3:4, :BINS] * (BINS / (tokens * NEIGH))
    gain_attn_ref[...] = small[4:5]
    for one in moves:
        one.wait()


def finish(ffn, attn, small, tokens):
    width = ffn[0].shape[-1]
    quarter = attn[0].shape[1]
    shapes = [(width, 2 * quarter)] * 3
    shapes += [(2 * quarter, width), (width, 2 * width), (2 * width, width)]
    rows = [(1, width)] * 3 + [(1, 1), (1, BINS)]

    def whole(array):
        return pl.BlockSpec(array.shape, lambda i: (0,) * array.ndim)

    return pl.pallas_call(
        functools.partial(finish_body, tokens=tokens),
        grid=(1,),
        in_specs=[whole(a) for a in (*ffn, *attn, small)],
        out_specs=[pl.BlockSpec(memory_space=pl.ANY)] * 6
        + [pl.BlockSpec(s, lambda i: (0, 0)) for s in rows],
        scratch_shapes=[pltpu.VMEM(s, F32) for s in shapes] + [pltpu.SemaphoreType.DMA((8,))],
        out_shape=[jax.ShapeDtypeStruct(s, F32) for s in shapes + rows],
        compiler_params=pltpu.CompilerParams(vmem_limit_bytes=FINISH_VMEM),
    )(*ffn, *attn, small)


def swap(array, axis, bit):
    size = lax.axis_size(axis)
    return lax.ppermute(array, axis, [(i, i ^ bit) for i in range(size)])


def bit_of(axis, bit):
    return (lax.axis_index(axis) // bit) % 2


def part_of(array, which, dim):
    half = array.shape[dim] // 2
    return lax.dynamic_slice_in_dim(array, which * half, half, dim)


def add_low(left, right):
    return (left.astype(F32) + right.astype(F32)).astype(BF16)


def join(mine, other, bit, dim):
    return jnp.where(
        bit_of("dp", bit) == 0,
        lax.concatenate([mine, other], dim),
        lax.concatenate([other, mine], dim),
    )


def swap_diagonal(array, first, last):
    size = lax.axis_size("dp")
    return lax.ppermute(array, "dp", [(i, i ^ first ^ last) for i in range(size)])


def join_four(mine, by_first, by_last, by_both, first, last):
    return join(
        join(mine, by_last, last, 0)[None], join(by_first, by_both, last, 0)[None], first, 0
    )


def after(value, *others):
    return lax.optimization_barrier((value, *others))[0]


class Chain:
    def __init__(self, array, dim):
        self.pieces = (array,)
        self.dim = dim

    def total(self, cut=lambda piece: piece):
        pieces = [cut(piece) for piece in self.pieces]
        if len(pieces) == 1:
            return pieces[0]
        return sum(piece.astype(F32) for piece in pieces).astype(BF16)

    def pass_on(self, sent, kept, bit, *others):
        self.sent = after(sent, *others)
        self.kept = kept
        self.come = swap(self.sent, "dp", bit)
        return self.sent

    def halve(self, bit, *others):
        mine = bit_of("dp", bit)
        self.sent = after(self.total(lambda p: part_of(p, 1 - mine, self.dim)), *others)
        self.kept = self.total(lambda p: part_of(p, mine, self.dim))
        self.come = swap(self.sent, "dp", bit)
        return self.sent

    def give(self, index, *others):
        self.sent = after(self.total(lambda p: p[index]), *others)
        self.kept = self.total(lambda p: p[1 - index])
        self.dim -= 1
        self.come = swap(self.sent, "mp", 1)
        return self.sent

    def send(self, bit, *others):
        self.sent = self.kept = after(self.total(), *others)
        self.come = swap(self.sent, "dp", bit)
        return self.sent

    def add(self, *others):
        self.come = after(self.come, *others)
        self.pieces = (self.kept, self.come)

    def join(self, bit, *others):
        self.pieces = (join(self.sent, after(self.come, *others), bit, self.dim),)


class Ride:
    def __init__(self, rows):
        self.rows = rows

    def below(self, array):
        left = self.rows
        parts = [array.reshape(-1, array.shape[-1])]
        for _ in range(3):
            part = lax.reduce_precision(left, 8, 7)
            parts.append(part.astype(BF16))
            left = left - part
        spare = -3 * left.shape[0] % 16
        parts.append(jnp.zeros((spare, left.shape[1]), BF16))
        return lax.concatenate(parts, 0)

    def add(self, block, like):
        size = like.size // like.shape[-1]
        count = self.rows.shape[0]
        for i in range(3):
            at = size + i * count
            self.rows = self.rows + block[at : at + count].astype(F32)
        return block[:size].reshape(like.shape)


def shards(
    tokens,
    memory,
    neighbours,
    neighbour_ids,
    doc_starts,
    bin_edges,
    w_query,
    w_key,
    w_value,
    w_out,
    w_up,
    w_down,
    gain_attn,
    gain_ffn,
    w_gate,
    cotangent,
):
    rows, length, width = tokens.shape
    count = rows * length
    dp = lax.axis_size("dp")
    core = bit_of("dp", 1)
    attn_gain = gain_attn.reshape(1, width)
    gains = jnp.stack([gain_ffn, w_gate])
    qkv = (w_query, w_key, w_value)
    far = []
    bit = 2
    while bit < dp:
        far.append(bit)
        bit *= 2

    qkv_sent = lax.concatenate([part_of(w, core, 0) for w in qkv], 1)
    up_part = part_of(w_up, core, 0)
    ffn_sent = lax.concatenate(
        [up_part[:, :width], up_part[:, width:], part_of(w_down, core, 0), part_of(w_out, core, 0)],
        0,
    )
    qkv_mine = swap(qkv_sent, "mp", 1)
    ffn_mine = swap(after(ffn_sent, qkv_sent), "mp", 1)
    kv, *own = attention_forward(
        doc_starts, after(tokens, qkv_sent, ffn_sent), memory, attn_gain, None, qkv
    )
    qkv_mine = after(qkv_mine, kv)
    qkv_got = (qkv_mine, swap(qkv_mine, "dp", 1))
    oth = attention_forward(doc_starts, tokens, memory, attn_gain, kv, qkv_got)
    ffn_mine = after(ffn_mine, oth[3])
    ffn_got = (ffn_mine, swap(ffn_mine, "dp", 1))
    ids = jnp.swapaxes(neighbour_ids, 1, 2)
    edges = bin_edges.reshape(1, BINS + 1)
    (
        result,
        grad_hidden,
        gctx_own,
        gctx_oth,
        sent_up,
        sent_down,
        kept_up,
        kept_down,
        sums,
    ) = middle_layer(
        tokens,
        own[3],
        oth[3],
        neighbours,
        ids,
        cotangent,
        (w_up, w_down, w_out),
        ffn_got,
        edges,
        gains,
    )
    up = Chain(None, 1)
    down = Chain(None, 1)
    up.pass_on(sent_up, kept_up, 1)
    down.pass_on(sent_down, kept_down, 1)
    up.add()
    down.add()
    sent = up.give(1)
    sent = down.halve(far[0], sent)
    g_oth, da, gain_oth = attention_backward(
        doc_starts, oth, after(gctx_oth, sent), kv, 1, 2
    )
    up.add(da)
    down.add(da)
    sent = up.halve(far[0])
    sent = down.give(1, sent)
    attn = Chain(None, 1)
    sent = attn.pass_on(da[0], da[1], 1, sent)
    g_own_first, da_first, gain_first = attention_backward(
        doc_starts, own, after(gctx_own, sent), kv, 1, 1
    )
    da_first = da_first[0]
    attn.add(da_first)
    up.add(da_first)
    down.add(da_first)
    both = Chain(None, 0)
    both.pieces = tuple(lax.concatenate([u, d], 0) for u, d in zip(up.pieces, down.pieces))
    attn_sent = attn.total()
    attn_come = swap(attn_sent, "mp", 1)
    sent = both.halve(far[1], attn_sent)
    first_sent = after(da_first, sent)
    first_come = swap(first_sent, "dp", 1)
    g_own_last, da_last, gain_last = attention_backward(
        doc_starts, own, after(gctx_own, first_sent), kv, 0, 1
    )
    da_last = da_last[0]
    attn_come, first_come = lax.optimization_barrier((attn_come, first_come, da_last))[:2]
    attn = Chain(None, 1)
    attn.pieces = (da_last, first_come, attn_come)
    both.add(da_last)
    gain_part = sum(g[:, 0].sum(0) for g in (gain_oth, gain_first, gain_last))[None] / attn_gain
    small = lax.concatenate([sums[:4], gain_part], 0)
    first_bit, last_bit = far[:2]

    def quarter(piece, by_first, by_last):
        at = 2 * (bit_of("dp", first_bit) ^ by_first) + (bit_of("dp", last_bit) ^ by_last)
        size = piece.shape[1] // 4
        return lax.dynamic_slice_in_dim(piece, at * size, size, 1)

    sent = both.send(far[2])
    sent_x = after(attn.total(lambda p: quarter(p, 1, 0)), sent)
    sent_z = attn.total(lambda p: quarter(p, 0, 1))
    sent_d = attn.total(lambda p: quarter(p, 1, 1))
    kept = attn.total(lambda p: quarter(p, 0, 0))
    come_x = swap(sent_x, "dp", first_bit)
    come_z = swap(sent_z, "dp", last_bit)
    come_d = swap_diagonal(sent_d, first_bit, last_bit)
    small_sent = after(small, sent_x, sent_z, sent_d)
    small_come = swap(small_sent, "mp", 1)
    grad_input = input_grad(
        tokens,
        after(grad_hidden, small_sent),
        attn_gain,
        (g_oth, g_own_first, g_own_last),
        (oth[0], own[0]),
    )
    come_x, come_z, come_d, small_come = lax.optimization_barrier(
        (come_x, come_z, come_d, small_come, grad_input)
    )[:4]
    ride = Ride(small_sent + small_come)
    total = sum(part.astype(F32) for part in (kept, come_x, come_z, come_d)).astype(BF16)
    ffn_x = ffn_z = None
    for bit in far[2:]:
        sent = ride.below(total)
        come = swap(sent, "dp", bit)
        if bit == far[2]:
            ffn_sent = add_low(both.sent, after(both.come, sent))
            for far_bit in far[3:]:
                ffn_sent = add_low(ffn_sent, swap(ffn_sent, "dp", far_bit))
            ffn_x = swap(ffn_sent, "dp", first_bit)
            ffn_z = swap(ffn_sent, "dp", last_bit)
            ffn_d = swap_diagonal(ffn_sent, first_bit, last_bit)
            come = after(come, ffn_sent)
        total = add_low(total, ride.add(come, total))
    sent = ride.below(total)
    come_x = swap(sent, "dp", first_bit)
    come_z = swap(sent, "dp", last_bit)
    come_d = swap_diagonal(sent, first_bit, last_bit)
    come_x, come_z, come_d, ffn_x, ffn_z, ffn_d = lax.optimization_barrier(
        (come_x, come_z, come_d, ffn_x, ffn_z, ffn_d)
    )
    flat = total.reshape(-1, width)
    parts = [ride.add(come, flat) for come in (come_x, come_z, come_d)]
    shape = total.shape
    total = join_four(
        flat.reshape(shape).swapaxes(0, 1),
        *[part.reshape(shape).swapaxes(0, 1) for part in parts],
        far[0],
        far[1],
    )
    total = total.reshape(-1, *shape[:1], width).swapaxes(0, 1)
    sent = ride.below(total)
    come = swap(sent, "dp", 1)
    ffn_total = after(join_four(ffn_sent, ffn_x, ffn_z, ffn_d, far[0], far[1]), sent)
    ffn_come = swap(ffn_total, "dp", 1)
    grads = finish(
        (ffn_total, ffn_come),
        (total, come),
        ride.rows,
        count * dp * lax.axis_size("mp"),
    )
    gain_attn_sum, gain_ffn_sum, gate_sum, mean, histogram = grads[6:]
    return (
        result,
        grad_input,
        *grads[:6],
        gain_attn_sum.reshape(width),
        gain_ffn_sum.reshape(width),
        gate_sum.reshape(width),
        mean.reshape(()),
        histogram.reshape(BINS),
    )


def solution(mesh):
    in_specs = (
        P(("dp", "mp"), None, None),
        P("dp", None, None),
        P(("dp", "mp"), None, None, None),
        P(("dp", "mp"), None, None),
        P("dp"),
        P(),
        P(None, "mp"),
        P(None, "mp"),
        P(None, "mp"),
        P("mp", None),
        P(None, "mp"),
        P("mp", None),
        P(),
        P(),
        P(),
        P(("dp", "mp"), None, None),
    )
    out_specs = (
        P(("dp", "mp"), None, None),
        P(("dp", "mp"), None, None),
        P(None, "mp"),
        P(None, "mp"),
        P(None, "mp"),
        P("mp", None),
        P(None, "mp"),
        P("mp", None),
        P(),
        P(),
        P(),
        P(),
        P(),
    )
    return jax.shard_map(shards, mesh=mesh, in_specs=in_specs, out_specs=out_specs, check_vma=False)
```

```python
import functools

import jax
import jax.numpy as jnp
from jax import lax
from jax.experimental import pallas as pl
from jax.experimental.pallas import tpu as pltpu
from jax.sharding import PartitionSpec as P

HEAD = 64
NEIGH = 4
BINS = 128
PAIR = 2 * HEAD
QROWS = 256
TILE = 256
GROUP = 64

EPS = 1e-05
BF16 = jnp.bfloat16
F32 = jnp.float32
VMEM_LIMIT = 56 * 1024 * 1024
FORWARD_VMEM = 52 * 1024 * 1024
BACKWARD_VMEM = 48 * 1024 * 1024
FINISH_VMEM = 24 * 1024 * 1024


def dot(left, right, left_dim=1, right_dim=0):
    return lax.dot_general(
        left, right, (((left_dim,), (right_dim,)), ((), ())), preferred_element_type=F32
    )


def normalize(values):
    centre = values - jnp.mean(values, -1, keepdims=True)
    spread = jnp.mean(centre * centre, -1, keepdims=True)
    rstd = lax.rsqrt(spread + EPS)
    return centre * rstd, rstd


def core_index():
    return lax.rem(lax.axis_index("dp"), 2)


def head_lanes(rows, head):
    lane = lax.broadcasted_iota(jnp.int32, (rows, PAIR), 1)
    return (lane >= head * HEAD) & (lane < (head + 1) * HEAD)


def only_head(block, head):
    return jnp.where(head_lanes(block.shape[0], head), block, jnp.zeros_like(block))


def attend(qkv_ref, p_ref, ctx_ref, length, with_memory):
    values = [only_head(qkv_ref[0, 0, pl.ds(3 * length, 2 * length), :], head) for head in range(2)]
    low = 0 if with_memory else length
    for first in range(0, length, QROWS):
        rows = pl.ds(first, QROWS)
        high = length + first + QROWS
        total = None
        for head in range(2):
            query = only_head(qkv_ref[0, 0, rows, :], head)
            scores = dot(query, qkv_ref[0, 0, pl.ds(length + low, high - low), :], 1, 1)
            seg = scores[:, length - low :]
            at = lax.broadcasted_iota(jnp.int32, seg.shape, 0) + first
            key = lax.broadcasted_iota(jnp.int32, seg.shape, 1)
            seg = jnp.where(key <= at, seg, -1e30)
            top = jnp.max(seg, -1, keepdims=True)
            if with_memory:
                mem = scores[:, :length]
                top = jnp.maximum(top, jnp.max(mem, -1, keepdims=True))
                mem = jnp.exp(mem - top)
            probs = jnp.exp(seg - top)
            mass = jnp.sum(probs, -1, keepdims=True)
            if with_memory:
                mass = mass + jnp.sum(mem, -1, keepdims=True)
            part = 1.0 / mass
            probs = (probs * part).astype(BF16)
            if with_memory:
                probs = jnp.concatenate([(mem * part).astype(BF16), probs], 1)
            p_ref[0, 0, head, rows, pl.ds(low, high - low)] = probs
            add = dot(probs, values[head][low:high])
            total = add if total is None else total + add
        ctx_ref[0, rows, :] = total.astype(BF16)


def forward_body(starts_ref, kv_ref, pack_ref, qkv_ref, p_ref, ctx_ref):
    length = kv_ref.shape[1] // 2
    pair = pl.program_id(1)
    kv = kv_ref[0]
    here = pl.multiple_of(3 * pair * PAIR, PAIR)
    query = dot(kv[length:], pack_ref[:, pl.ds(here, PAIR)]).astype(BF16)
    qkv_ref[0, 0, pl.ds(0, length), :] = (query.astype(F32) * HEAD ** (-0.5)).astype(BF16)
    both = dot(kv, pack_ref[:, pl.ds(here + PAIR, 2 * PAIR)]).astype(BF16)
    qkv_ref[0, 0, pl.ds(length, 2 * length), :] = both[:, :PAIR]
    qkv_ref[0, 0, pl.ds(3 * length, 2 * length), :] = both[:, PAIR:]
    start = starts_ref[lax.axis_index("mp") * pl.num_programs(0) + pl.program_id(0)]

    @pl.when(start == 0)
    def _():
        attend(qkv_ref, p_ref, ctx_ref, length, True)

    @pl.when(start != 0)
    def _():
        attend(qkv_ref, p_ref, ctx_ref, length, False)


def first_forward(
    starts_ref, tok_ref, mem_ref, gain_ref, wq_ref, wk_ref, wv_ref, kv_ref, pack_ref, *outs
):
    length = tok_ref.shape[1]

    @pl.when((pl.program_id(0) == 0) & (pl.program_id(1) == 0))
    def _():
        for i, weight in enumerate((wq_ref, wk_ref, wv_ref)):
            for p in range(2):
                pack_ref[:, pl.ds((3 * p + i) * PAIR, PAIR)] = weight[:, pl.ds(p * PAIR, PAIR)]

    @pl.when(pl.program_id(1) == 0)
    def _():
        gain = gain_ref[...]
        kv_ref[0, pl.ds(0, length), :] = (normalize(mem_ref[0].astype(F32))[0] * gain).astype(BF16)
        kv_ref[0, pl.ds(length, length), :] = (
            normalize(tok_ref[0].astype(F32))[0] * gain
        ).astype(BF16)

    forward_body(starts_ref, kv_ref, pack_ref, *outs)


def second_forward(starts_ref, kv_ref, mine_ref, sibling_ref, pack_ref, *outs):
    rows = mine_ref.shape[0]
    core = core_index()

    @pl.when((pl.program_id(0) == 0) & (pl.program_id(1) == 0))
    def _():
        for block, which in ((mine_ref, core), (sibling_ref, 1 - core)):
            to = pl.ds(pl.multiple_of(which * rows, rows), rows)
            for i in range(3):
                for p in range(2):
                    pack_ref[to, pl.ds((3 * p + i) * PAIR, PAIR)] = block[
                        :, pl.ds((2 * i + p) * PAIR, PAIR)
                    ]

    forward_body(starts_ref, kv_ref, pack_ref, *outs)


def attention_forward(starts, tokens, memory, gain, kv, weights):
    rows, length, width = tokens.shape
    pairs = 2
    pack = (width, 3 * pairs * PAIR)
    outs = [
        jax.ShapeDtypeStruct(pack, BF16),
        jax.ShapeDtypeStruct((rows, pairs, 5 * length, PAIR), BF16),
        jax.ShapeDtypeStruct((rows, pairs, 2, length, 2 * length), BF16),
        jax.ShapeDtypeStruct((rows, length, pairs * PAIR), BF16),
    ]
    out_specs = [
        pl.BlockSpec(pack, lambda r, p: (0, 0)),
        pl.BlockSpec((1, 1, 5 * length, PAIR), lambda r, p: (r, p, 0, 0)),
        pl.BlockSpec((1, 1, 2, length, 2 * length), lambda r, p: (r, p, 0, 0, 0)),
        pl.BlockSpec((1, length, PAIR), lambda r, p: (r, 0, p)),
    ]
    kv_spec = pl.BlockSpec((1, 2 * length, width), lambda r, p: (r, 0, 0))
    in_specs = [pl.BlockSpec(memory_space=pltpu.SMEM)]
    if kv is None:
        body = first_forward
        ins = [tokens, memory, gain]
        in_specs += [
            pl.BlockSpec((1, length, width), lambda r, p: (r, 0, 0)),
            pl.BlockSpec((1, length, width), lambda r, p: (lax.axis_index("mp") * rows + r, 0, 0)),
            pl.BlockSpec((1, width), lambda r, p: (0, 0)),
        ]
        outs = [jax.ShapeDtypeStruct((rows, 2 * length, width), BF16)] + outs
        out_specs = [kv_spec] + out_specs
    else:
        body = second_forward
        ins = [kv]
        in_specs += [kv_spec]
    in_specs += [pl.BlockSpec(w.shape, lambda r, p: (0, 0)) for w in weights]
    return pl.pallas_call(
        body,
        grid=(rows, pairs),
        in_specs=in_specs,
        out_specs=out_specs,
        out_shape=outs,
        compiler_params=pltpu.CompilerParams(vmem_limit_bytes=FORWARD_VMEM),
        cost_estimate=pl.CostEstimate(flops=6 * 10**9, bytes_accessed=16 * 2**20, transcendentals=0),
    )(starts, *ins, *weights)


def gelu_parts(pre):
    c0 = 0.7978845608028654
    c1 = c0 * 0.044715
    square = pre * pre
    part = 0.5 * jnp.tanh(pre * (c1 * square + c0)) + 0.5
    act = pre * part
    return act, part + act * (1.0 - part) * ((6.0 * c1) * square + 2.0 * c0)


def weighted(weights, values):
    return sum(w * v for w, v in zip(weights[1:], values[1:])) + weights[0] * values[0]


def middle_body(
    tok_ref,
    ctx_own_ref,
    ctx_oth_ref,
    nb_ref,
    ids_ref,
    cot_ref,
    up_far,
    down_far,
    out_far,
    mine_far,
    sibling_far,
    edges_ref,
    gain_ref,
    wgate_ref,
    result_ref,
    grad_hidden_ref,
    gctx_own_ref,
    gctx_oth_ref,
    sent_up_far,
    sent_down_far,
    kept_up_far,
    kept_down_far,
    sums_ref,
    e_ref,
    hist_ref,
    edge_ref,
    pick_ref,
    up_ref,
    down_ref,
    out_ref,
    oth_ref,
    stage_ref,
    ffn_in_ref,
    act_ref,
    gpre_ref,
    cots_ref,
    low_ref,
    ctx_ref,
    in_sems,
    out_sems,
):
    step = pl.program_id(0)
    here = pl.ds(pl.multiple_of(step * TILE, TILE), TILE)
    width = tok_ref.shape[-1]
    hidden_units = down_ref.shape[0]
    half = width // 2
    chunks = hidden_units // width
    scale = width ** (-0.5)
    core = core_index()
    copies = [
        pltpu.make_async_copy(far, near, in_sems.at[i])
        for i, (far, near) in enumerate(
            (
                (out_far, out_ref),
                (mine_far, oth_ref.at[core]),
                (sibling_far, oth_ref.at[1 - core]),
                (up_far, up_ref),
                (down_far, down_ref),
            )
        )
    ]

    @pl.when(step == 0)
    def _():
        for copy in copies:
            copy.start()
        sums_ref[...] = jnp.zeros_like(sums_ref)
        hist_ref[...] = jnp.zeros_like(hist_ref)
        row = lax.broadcasted_iota(jnp.int32, pick_ref.shape, 0)
        column = lax.broadcasted_iota(jnp.int32, pick_ref.shape, 1)
        from_row = NEIGH * (row % GROUP) + row // GROUP
        pick_ref[...] = (column == from_row).astype(F32).astype(BF16)
        edges = edges_ref[...].astype(F32)
        for i in range(2):
            edge_ref[i] = jnp.broadcast_to(edges[:, i : i + BINS], (BINS, BINS)).T
        for copy in copies[:3]:
            copy.wait()

    def other_out():
        at = pl.ds(2 * width, half // 2)
        return jnp.concatenate([oth_ref[0, at, :], oth_ref[1, at, :]], 0)

    wgate = wgate_ref[...]
    gain = gain_ref[...]

    def front():
        ctx_ref[here, pl.ds(0, half)] = ctx_own_ref[0]
        ctx_ref[here, pl.ds(half, half)] = ctx_oth_ref[0]
        cots_ref[here, :] = cot_ref[0]
        hidden = (
            tok_ref[0].astype(F32)
            + dot(ctx_own_ref[0], out_ref[...])
            + dot(ctx_oth_ref[0], other_out())
        )
        for first in range(0, TILE, GROUP):
            mixed_rows = nb_ref[0, pl.ds(first, GROUP)].reshape(NEIGH * GROUP, width)
            planes = dot(pick_ref[...], mixed_rows)
            for k in range(NEIGH):
                e_ref[k, pl.ds(first, GROUP), :] = planes[k * GROUP : (k + 1) * GROUP]
        affinity = [
            jnp.sum(e_ref[k] * hidden, -1, keepdims=True) * scale for k in range(NEIGH)
        ]
        top = jnp.maximum(
            jnp.maximum(affinity[0], affinity[1]), jnp.maximum(affinity[2], affinity[3])
        )
        raised = [jnp.exp(a - top) for a in affinity]
        inverse = 1.0 / (raised[0] + raised[1] + raised[2] + raised[3])
        weights = [a * inverse for a in raised]
        gate = jax.nn.sigmoid(jnp.sum(hidden * wgate, -1, keepdims=True))
        recalled = weighted(weights, [e_ref[k] for k in range(NEIGH)])
        mixed = hidden + gate * recalled
        normal, rstd = normalize(mixed)
        ffn_in_ref[here, :] = (normal * gain).astype(BF16)
        return hidden, weights, gate, mixed, normal, rstd

    def other_up():
        rows = [
            jnp.concatenate([oth_ref[h, pl.ds(c * half, half), :] for c in range(chunks)], 1)
            for h in range(2)
        ]
        return jnp.concatenate(rows, 0)

    def other_down():
        return jnp.concatenate([oth_ref[c, pl.ds(width, width), :] for c in range(chunks)], 0)

    def feed():
        ffn_in = ffn_in_ref[here, :]
        cot = cot_ref[0]
        for side in range(2):
            for c in range(chunks):
                if side == 0:
                    up = up_ref[:, pl.ds(c * width, width)]
                    down = down_ref[pl.ds(c * width, width), :]
                else:
                    part = pl.ds(c * half, half)
                    up = jnp.concatenate([oth_ref[0, part, :], oth_ref[1, part, :]], 0)
                    down = oth_ref[c, pl.ds(width, width), :]
                at = pl.ds((side * chunks + c) * width, width)
                act, slope = gelu_parts(dot(ffn_in, up))
                act_ref[here, at] = act.astype(BF16)
                gpre_ref[here, at] = (dot(cot, down, 1, 1) * slope).astype(BF16)
        own = pl.ds(0, hidden_units)
        oth = pl.ds(hidden_units, hidden_units)
        down_sum = dot(act_ref[here, own], down_ref[...]) + dot(act_ref[here, oth], other_down())
        grad_sum = dot(gpre_ref[here, own], up_ref[...], 1, 1) + dot(
            gpre_ref[here, oth], other_up(), 1, 1
        )
        return down_sum, grad_sum

    def back(kept, sums):
        hidden, weights, gate, mixed, normal, rstd = kept
        down_sum, grad_sum = sums
        result_ref[0] = (mixed + down_sum).astype(BF16)
        gain_part = jnp.sum(grad_sum * normal, 0, keepdims=True)
        grad_normal = grad_sum * gain
        grad_mixed = cot_ref[0].astype(F32) + rstd * (
            grad_normal
            - jnp.mean(grad_normal, -1, keepdims=True)
            - normal * jnp.mean(grad_normal * normal, -1, keepdims=True)
        )
        pulls = [
            jnp.sum(grad_mixed * e_ref[k], -1, keepdims=True) for k in range(NEIGH)
        ]
        pulled = weighted(weights, pulls)
        gate_grad = gate * (1.0 - gate) * pulled
        grad_hidden = grad_mixed + gate_grad * wgate
        for k in range(NEIGH):
            grad_hidden = (
                grad_hidden + (scale * gate * weights[k] * (pulls[k] - pulled)) * e_ref[k]
            )
        grad_hidden_ref[0] = grad_hidden
        low = grad_hidden.astype(BF16)
        low_ref[here, :] = low
        gctx_own_ref[0] = dot(low, out_ref[...], 1, 1).astype(BF16)
        gctx_oth_ref[0] = dot(low, other_out(), 1, 1).astype(BF16)
        gate_wide = jnp.broadcast_to(gate, (TILE, BINS)).T
        low_edge = jnp.concatenate([edge_ref[0]] * (TILE // BINS), 1)
        high_edge = jnp.concatenate([edge_ref[1]] * (TILE // BINS), 1)
        mass = jnp.zeros_like(gate_wide)
        for k in range(NEIGH):
            ids = ids_ref[0, pl.ds(k, 1), :].astype(F32)
            mass = mass + jnp.where((ids >= low_edge) & (ids < high_edge), gate_wide, 0.0)
        gate_sum = jnp.sum(jnp.broadcast_to(gate, (TILE, width)), 0, keepdims=True)
        sums_ref[pl.ds(0, 1), :] += gain_part
        sums_ref[pl.ds(1, 1), :] += gate_sum
        sums_ref[pl.ds(2, 1), :] += jnp.sum(gate_grad * hidden, 0, keepdims=True)
        hist_ref[...] += mass

    kept = front()

    @pl.when(step == 0)
    def _():
        for copy in copies[3:]:
            copy.wait()

    back(kept, feed())

    @pl.when(step == pl.num_programs(0) - 1)
    def _():
        sums_ref[pl.ds(3, 1), pl.ds(0, BINS)] = jnp.sum(hist_ref[...].T, 0, keepdims=True)
        cut = sent_up_far.shape[1]
        moves = []
        for fars, which in (
            ((sent_up_far, sent_down_far), 1 - core),
            ((kept_up_far, kept_down_far), core),
        ):
            for side in range(2):
                at = pl.ds(pl.multiple_of((side * chunks + which) * width, width), width)
                here = pl.ds(pl.multiple_of((2 * side + which) * PAIR, PAIR), PAIR)
                slot = len(moves) // 3
                first = 0
                for left, right in (
                    (ffn_in_ref[...], gpre_ref[:, at]),
                    (act_ref[:, at], cots_ref[...]),
                    (ctx_ref[:, here], low_ref[...]),
                ):
                    piece = dot(left, right, 0, 0).astype(BF16)
                    stage_ref[slot, pl.ds(first, piece.shape[0]), :] = piece
                    first += piece.shape[0]
                part = cut // 2
                own = lax.rem(lax.div(lax.axis_index("dp"), 2), 2) * part
                for start, size, far, to in (
                    (0, cut, fars[0], 0),
                    (cut, part, fars[1], part - own),
                    (cut + part, part, fars[1], own),
                ):
                    move = pltpu.make_async_copy(
                        stage_ref.at[slot, pl.ds(start, size), :],
                        far.at[side, pl.ds(pl.multiple_of(to, part), size), :],
                        out_sems.at[len(moves)],
                    )
                    move.start()
                    moves.append(move)
        for move in moves:
            move.wait()


def middle_layer(tokens, ctx_own, ctx_oth, nb, ids, cot, weights, received, edges, gain, wgate):
    rows, length, width = tokens.shape
    hidden_units = weights[1].shape[0]
    steps = length // TILE
    tiles = rows * steps
    count = rows * length
    assert hidden_units == 2 * width

    def place_of(i):
        return i // steps, i % steps

    def tiled(last):
        return pl.BlockSpec((1, TILE, last), lambda i: (*place_of(i), 0))

    def whole(shape):
        return pl.BlockSpec(shape, lambda i: (0,) * len(shape))

    far = pl.BlockSpec(memory_space=pl.ANY)
    return pl.pallas_call(
        middle_body,
        grid=(tiles,),
            in_specs=[
                tiled(width),
                tiled(width // 2),
                tiled(width // 2),
                pl.BlockSpec((1, TILE, NEIGH, width), lambda i: (*place_of(i), 0, 0)),
                pl.BlockSpec(
                    (1, NEIGH, TILE), lambda i: (place_of(i)[0], 0, place_of(i)[1])
                ),
                tiled(width),
                *[far] * 5,
                whole((1, BINS + 1)),
                whole((1, width)),
                whole((1, width)),
            ],
            out_specs=[
                tiled(width),
                tiled(width),
                tiled(width // 2),
                tiled(width // 2),
                far,
                far,
                far,
                far,
                whole((8, width)),
            ],
            scratch_shapes=[
                pltpu.VMEM((NEIGH, TILE, width), F32),
                pltpu.VMEM((BINS, TILE), F32),
                pltpu.VMEM((2, BINS, BINS), F32),
                pltpu.VMEM((NEIGH * GROUP, NEIGH * GROUP), BF16),
                *[pltpu.VMEM(w.shape, BF16) for w in weights],
                pltpu.VMEM((2, *received[0].shape), BF16),
                pltpu.VMEM((4, 2 * width + PAIR, width), BF16),
                pltpu.VMEM((count, width), BF16),
                pltpu.VMEM((count, 2 * hidden_units), BF16),
                pltpu.VMEM((count, 2 * hidden_units), BF16),
                pltpu.VMEM((count, width), BF16),
                pltpu.VMEM((count, width), BF16),
                pltpu.VMEM((count, width), BF16),
                pltpu.SemaphoreType.DMA((5,)),
                pltpu.SemaphoreType.DMA((12,)),
            ],
        out_shape=[
            jax.ShapeDtypeStruct((rows, length, width), BF16),
            jax.ShapeDtypeStruct((rows, length, width), F32),
            jax.ShapeDtypeStruct((rows, length, width // 2), BF16),
            jax.ShapeDtypeStruct((rows, length, width // 2), BF16),
            *[jax.ShapeDtypeStruct((2, width + PAIR // 2, width), BF16)] * 4,
            jax.ShapeDtypeStruct((8, width), F32),
        ],
        compiler_params=pltpu.CompilerParams(vmem_limit_bytes=VMEM_LIMIT),
        cost_estimate=pl.CostEstimate(flops=15 * 10**9, bytes_accessed=30 * 2**20, transcendentals=0),
    )(tokens, ctx_own, ctx_oth, nb, ids, cot, *weights, *received, edges, gain, wgate)


def attend_back(
    head, qkv_ref, p_ref, gctx_ref, ctx_ref, ds_ref, dq_ref, t_ref, dk_ref, dv_ref, with_memory
):
    length = ctx_ref.shape[1]
    grad = only_head(gctx_ref[0], head)
    delta = jnp.sum(grad.astype(F32) * ctx_ref[0].astype(F32), -1, keepdims=True)
    keys = only_head(qkv_ref[0, 0, pl.ds(length, 2 * length), :], head)
    lanes = pl.ds(pl.multiple_of(head * HEAD, HEAD), HEAD)
    low = 0 if with_memory else length
    for first in range(0, length, QROWS):
        rows = pl.ds(first, QROWS)
        high = length + first + QROWS
        here = pl.ds(low, high - low)
        probs = p_ref[0, 0, 0, rows, here].astype(F32)
        values = qkv_ref[0, 0, pl.ds(3 * length + low, high - low), :]
        grad_probs = dot(grad[first : first + QROWS], values, 1, 1)
        ds = (probs * (grad_probs - delta[first : first + QROWS])).astype(BF16)
        ds_ref[rows, here] = ds
        dq_ref[rows, :] += dot(ds, keys[low:high])
    for out_ref, left, right in (
        (dk_ref, t_ref[0, lanes, :], ds_ref),
        (dv_ref, t_ref[1, lanes, :], p_ref.at[0, 0, 0]),
    ):
        if not with_memory:
            out_ref[lanes, :length] = jnp.zeros((HEAD, length), BF16)
        for first in range(0, length, QROWS):
            start = low if first == 0 else length + first
            here = pl.ds(start, length + first + QROWS - start)
            out_ref[lanes, here] = dot(
                left[:, first:], right[pl.ds(first, length - first), here]
            ).astype(BF16)


def backward_body(
    starts_ref,
    qkv_ref,
    p_ref,
    gctx_ref,
    ctx_ref,
    kv_far,
    pack_ref,
    grads_ref,
    dw_ref,
    gain_ref,
    ds_ref,
    dq_ref,
    t_ref,
    dk_ref,
    dv_ref,
    acc_ref,
    kv_ref,
    sem,
):
    length = ctx_ref.shape[1]
    row = pl.program_id(1)
    head = pl.program_id(2)
    start = starts_ref[lax.axis_index("mp") * pl.num_programs(1) + row]
    fetch = pltpu.make_async_copy(kv_far.at[row], kv_ref, sem)
    args = (qkv_ref, p_ref, gctx_ref, ctx_ref, ds_ref, dq_ref, t_ref, dk_ref, dv_ref)

    @pl.when(head == 0)
    def _():
        fetch.start()
        dq_ref[...] = jnp.zeros_like(dq_ref)
        t_ref[0] = qkv_ref[0, 0, pl.ds(0, length), :].T
        t_ref[1] = gctx_ref[0].T

    @pl.when(start == 0)
    def _():
        attend_back(head, *args, True)

    @pl.when(start != 0)
    def _():
        attend_back(head, *args, False)

    @pl.when(head == 1)
    def _():
        dq_t = (dq_ref[...] * HEAD ** (-0.5)).astype(BF16).T
        grads_ref[0, 0, pl.ds(0, PAIR), :] = dq_t
        grads_ref[0, 0, pl.ds(PAIR, PAIR), :] = dk_ref[:, length:]
        grads_ref[0, 0, pl.ds(2 * PAIR, PAIR), :] = dv_ref[:, length:]
        fetch.wait()
        for i, add in enumerate(
            (
                dot(dq_t, kv_ref[pl.ds(length, length), :]),
                dot(dk_ref[...], kv_ref[...]),
                dot(dv_ref[...], kv_ref[...]),
            )
        ):
            acc_ref[i] = jnp.where(row == 0, add, acc_ref[i] + add)

    @pl.when((head == 1) & (row == pl.num_programs(1) - 1))
    def _():
        part = None
        for i in range(3):
            total = acc_ref[i]
            dw_ref[0, i] = total.astype(BF16)
            weight = pack_ref[:, pl.ds(i * PAIR, PAIR)].T.astype(F32)
            add = jnp.sum(total * weight, 0, keepdims=True)
            part = add if part is None else part + add
        gain_ref[0] = jnp.broadcast_to(part, gain_ref.shape[1:])


def attention_backward(starts, saved, gctx, kv, shift, many):
    pack, qkv, p, ctx = saved
    rows, _, _, length, _ = p.shape
    width = kv.shape[-1]

    def pair(n):
        return lax.rem(core_index() + shift + n, 2)

    return pl.pallas_call(
        backward_body,
        grid=(many, rows, 2),
        in_specs=[
            pl.BlockSpec(memory_space=pltpu.SMEM),
            pl.BlockSpec((1, 1, 5 * length, PAIR), lambda n, r, h: (r, pair(n), 0, 0)),
            pl.BlockSpec((1, 1, 1, length, 2 * length), lambda n, r, h: (r, pair(n), h, 0, 0)),
            pl.BlockSpec((1, length, PAIR), lambda n, r, h: (r, 0, pair(n))),
            pl.BlockSpec((1, length, PAIR), lambda n, r, h: (r, 0, pair(n))),
            pl.BlockSpec(memory_space=pl.ANY),
            pl.BlockSpec((width, 3 * PAIR), lambda n, r, h: (0, pair(n))),
        ],
        out_specs=[
            pl.BlockSpec((1, 1, 3 * PAIR, length), lambda n, r, h: (n, r, 0, 0)),
            pl.BlockSpec((1, 3, PAIR, width), lambda n, r, h: (n, 0, 0, 0)),
            pl.BlockSpec((1, 8, width), lambda n, r, h: (n, 0, 0)),
        ],
        scratch_shapes=[
            pltpu.VMEM((length, 2 * length), BF16),
            pltpu.VMEM((length, PAIR), F32),
            pltpu.VMEM((2, PAIR, length), BF16),
            pltpu.VMEM((PAIR, 2 * length), BF16),
            pltpu.VMEM((PAIR, 2 * length), BF16),
            pltpu.VMEM((3, PAIR, width), F32),
            pltpu.VMEM((2 * length, width), BF16),
            pltpu.SemaphoreType.DMA,
        ],
        out_shape=[
            jax.ShapeDtypeStruct((many, rows, 3 * PAIR, length), BF16),
            jax.ShapeDtypeStruct((many, 3, PAIR, width), BF16),
            jax.ShapeDtypeStruct((many, 8, width), F32),
        ],
        compiler_params=pltpu.CompilerParams(vmem_limit_bytes=BACKWARD_VMEM),
        cost_estimate=pl.CostEstimate(
            flops=4 * 10**9 * many, bytes_accessed=8 * 2**20 * many, transcendentals=0
        ),
    )(starts, qkv, p, gctx, ctx, kv, pack)


def input_body(
    tok_ref,
    grad_hidden_ref,
    gain_ref,
    oth_ref,
    own_first_ref,
    own_last_ref,
    oth_pack_ref,
    own_pack_ref,
    out_ref,
):
    core = core_index()
    total = None
    for block, pack, which in (
        (oth_ref[0, 0], oth_pack_ref, 1 - core),
        (oth_ref[1, 0], oth_pack_ref, core),
        (own_first_ref[0, 0], own_pack_ref, 1 - core),
        (own_last_ref[0, 0], own_pack_ref, core),
    ):
        here = pl.ds(pl.multiple_of(which * 3 * PAIR, 3 * PAIR), 3 * PAIR)
        add = dot(block, pack[:, here], 0, 1)
        total = add if total is None else total + add
    normal, rstd = normalize(tok_ref[0].astype(F32))
    grad = total * gain_ref[...]
    out_ref[0] = (
        grad_hidden_ref[0]
        + rstd
        * (
            grad
            - jnp.mean(grad, -1, keepdims=True)
            - normal * jnp.mean(grad * normal, -1, keepdims=True)
        )
    ).astype(BF16)


def input_grad(tokens, grad_hidden, gain, grads, packs):
    rows, length, width = tokens.shape
    row = pl.BlockSpec((1, length, width), lambda r: (r, 0, 0))

    def whole(array):
        return pl.BlockSpec(array.shape, lambda r: (0, 0))

    return pl.pallas_call(
        input_body,
        grid=(rows,),
        in_specs=[
            row,
            row,
            whole(gain),
            *[pl.BlockSpec((g.shape[0], 1) + g.shape[2:], lambda r: (0, r, 0, 0)) for g in grads],
            *[whole(p) for p in packs],
        ],
        out_specs=row,
        out_shape=jax.ShapeDtypeStruct(tokens.shape, BF16),
        compiler_params=pltpu.CompilerParams(vmem_limit_bytes=VMEM_LIMIT),
        cost_estimate=pl.CostEstimate(flops=2 * 10**9, bytes_accessed=8 * 2**20, transcendentals=0),
    )(tokens, grad_hidden, gain, *grads, *packs)


def finish_body(
    ffn_mine,
    ffn_sibling,
    attn_mine,
    attn_sibling,
    small_ref,
    q_far,
    k_far,
    v_far,
    out_far,
    up_far,
    down_far,
    gain_attn_ref,
    gain_ffn_ref,
    gate_ref,
    mean_ref,
    hist_ref,
    q_ref,
    k_ref,
    v_ref,
    out_ref,
    up_ref,
    down_ref,
    sems,
    tokens,
):
    core = core_index()
    width = up_far.shape[0]
    rows = attn_mine.shape[1]
    moves = []

    def pair(mine, sibling):
        return (
            jnp.where(core == 0, mine, sibling).astype(F32),
            jnp.where(core == 0, sibling, mine).astype(F32),
        )

    def move(near, far):
        moves.append(pltpu.make_async_copy(near, far, sems.at[len(moves)]))
        moves[-1].start()

    size = ffn_mine.shape[1] // 2
    pieces = [(x, pl.ds(y * size, size)) for y in range(2) for x in range(2)]
    halves = zip(*(pair(ffn_mine[x, y, :], ffn_sibling[x, y, :]) for x, y in pieces))
    for which, parts in enumerate(halves):
        rows_of = jnp.concatenate(parts, 0)
        to = pl.ds(which * width, width)
        up_ref[:, to] = rows_of[:width]
        down_ref[to, :] = rows_of[width : 2 * width]
        out_ref[pl.ds(which * PAIR, PAIR), :] = rows_of[2 * width :]
        move(down_ref.at[to, :], down_far.at[to, :])
    move(up_ref, up_far)
    move(out_ref, out_far)
    for i, (near, far) in enumerate(((q_ref, q_far), (k_ref, k_far), (v_ref, v_far))):
        first, last = pair(attn_mine[i], attn_sibling[pl.ds(i * rows, rows), :])
        near[...] = jnp.concatenate([first, last], 0).T
        move(near, far)
    count = small_ref.shape[0]
    below = attn_sibling[pl.ds(3 * rows, -(-3 * count // 16) * 16), :].astype(F32)
    small = small_ref[...]
    for i in range(3):
        small = small + below[i * count : (i + 1) * count]
    gain_ffn_ref[...] = small[0:1]
    mean_ref[...] = small[1:2, 0:1] / tokens
    gate_ref[...] = small[2:3]
    hist_ref[...] = small[3:4, :BINS] * (BINS / (tokens * NEIGH))
    gain_attn_ref[...] = small[4:5]
    for one in moves:
        one.wait()


def finish(ffn, attn, small, tokens):
    width = ffn[0].shape[-1]
    quarter = attn[0].shape[1]
    shapes = [(width, 2 * quarter)] * 3
    shapes += [(2 * quarter, width), (width, 2 * width), (2 * width, width)]
    rows = [(1, width)] * 3 + [(1, 1), (1, BINS)]

    def whole(array):
        return pl.BlockSpec(array.shape, lambda i: (0,) * array.ndim)

    return pl.pallas_call(
        functools.partial(finish_body, tokens=tokens),
        grid=(1,),
        in_specs=[whole(a) for a in (*ffn, *attn, small)],
        out_specs=[pl.BlockSpec(memory_space=pl.ANY)] * 6
        + [pl.BlockSpec(s, lambda i: (0, 0)) for s in rows],
        scratch_shapes=[pltpu.VMEM(s, F32) for s in shapes] + [pltpu.SemaphoreType.DMA((8,))],
        out_shape=[jax.ShapeDtypeStruct(s, F32) for s in shapes + rows],
        compiler_params=pltpu.CompilerParams(vmem_limit_bytes=FINISH_VMEM),
    )(*ffn, *attn, small)


def swap(array, axis, bit):
    size = lax.axis_size(axis)
    return lax.ppermute(array, axis, [(i, i ^ bit) for i in range(size)])


def bit_of(axis, bit):
    return (lax.axis_index(axis) // bit) % 2


def part_of(array, which, dim):
    half = array.shape[dim] // 2
    return lax.dynamic_slice_in_dim(array, which * half, half, dim)


def add_low(left, right):
    return (left.astype(F32) + right.astype(F32)).astype(BF16)


def join(mine, other, bit, dim):
    return jnp.where(
        bit_of("dp", bit) == 0,
        lax.concatenate([mine, other], dim),
        lax.concatenate([other, mine], dim),
    )


def swap_diagonal(array, first, last):
    size = lax.axis_size("dp")
    return lax.ppermute(array, "dp", [(i, i ^ first ^ last) for i in range(size)])


def join_four(mine, by_first, by_last, by_both, first, last):
    return join(
        join(mine, by_last, last, 0)[None], join(by_first, by_both, last, 0)[None], first, 0
    )


def after(value, *others):
    return lax.optimization_barrier((value, *others))[0]


class Chain:
    def __init__(self, array, dim):
        self.pieces = (array,)
        self.dim = dim

    def total(self, cut=lambda piece: piece):
        pieces = [cut(piece) for piece in self.pieces]
        if len(pieces) == 1:
            return pieces[0]
        return sum(piece.astype(F32) for piece in pieces).astype(BF16)

    def pass_on(self, sent, kept, bit, *others):
        self.sent = after(sent, *others)
        self.kept = kept
        self.come = swap(self.sent, "dp", bit)
        return self.sent

    def halve(self, bit, *others):
        mine = bit_of("dp", bit)
        self.sent = after(self.total(lambda p: part_of(p, 1 - mine, self.dim)), *others)
        self.kept = self.total(lambda p: part_of(p, mine, self.dim))
        self.come = swap(self.sent, "dp", bit)
        return self.sent

    def first_half(self, bit, *others):
        half = self.pieces[0].shape[self.dim] // 2
        self.sent = after(
            self.total(lambda p: lax.slice_in_dim(p, 0, half, axis=self.dim)), *others
        )
        self.kept = self.total(lambda p: lax.slice_in_dim(p, half, 2 * half, axis=self.dim))
        self.come = swap(self.sent, "dp", bit)
        return self.sent

    def give(self, index, *others):
        self.sent = after(self.total(lambda p: p[index]), *others)
        self.kept = self.total(lambda p: p[1 - index])
        self.dim -= 1
        self.come = swap(self.sent, "mp", 1)
        return self.sent

    def send(self, bit, *others):
        self.sent = self.kept = after(self.total(), *others)
        self.come = swap(self.sent, "dp", bit)
        return self.sent

    def add(self, *others):
        self.come = after(self.come, *others)
        self.pieces = (self.kept, self.come)

    def join(self, bit, *others):
        self.pieces = (join(self.sent, after(self.come, *others), bit, self.dim),)


class Ride:
    def __init__(self, rows):
        self.rows = rows

    def below(self, array):
        left = self.rows
        parts = [array.reshape(-1, array.shape[-1])]
        for _ in range(3):
            part = lax.reduce_precision(left, 8, 7)
            parts.append(part.astype(BF16))
            left = left - part
        spare = -3 * left.shape[0] % 16
        parts.append(jnp.zeros((spare, left.shape[1]), BF16))
        return lax.concatenate(parts, 0)

    def add(self, block, like):
        size = like.size // like.shape[-1]
        count = self.rows.shape[0]
        for i in range(3):
            at = size + i * count
            self.rows = self.rows + block[at : at + count].astype(F32)
        return block[:size].reshape(like.shape)


def shards(
    tokens,
    memory,
    neighbours,
    neighbour_ids,
    doc_starts,
    bin_edges,
    w_query,
    w_key,
    w_value,
    w_out,
    w_up,
    w_down,
    gain_attn,
    gain_ffn,
    w_gate,
    cotangent,
):
    rows, length, width = tokens.shape
    count = rows * length
    dp = lax.axis_size("dp")
    core = bit_of("dp", 1)
    attn_gain = gain_attn.reshape(1, width)
    qkv = (w_query, w_key, w_value)
    far = []
    bit = 2
    while bit < dp:
        far.append(bit)
        bit *= 2

    qkv_sent = lax.concatenate([part_of(w, core, 0) for w in qkv], 1)
    up_part = part_of(w_up, core, 0)
    ffn_sent = lax.concatenate(
        [up_part[:, :width], up_part[:, width:], part_of(w_down, core, 0), part_of(w_out, core, 0)],
        0,
    )
    qkv_mine = swap(qkv_sent, "mp", 1)
    ffn_mine = swap(after(ffn_sent, qkv_sent), "mp", 1)
    kv, *own = attention_forward(
        doc_starts, after(tokens, qkv_sent, ffn_sent), memory, attn_gain, None, qkv
    )
    qkv_mine = after(qkv_mine, kv)
    qkv_got = (qkv_mine, swap(qkv_mine, "dp", 1))
    oth = attention_forward(doc_starts, tokens, memory, attn_gain, kv, qkv_got)
    ffn_mine = after(ffn_mine, oth[3])
    ffn_got = (ffn_mine, swap(ffn_mine, "dp", 1))
    ids = jnp.swapaxes(neighbour_ids, 1, 2)
    edges = bin_edges.reshape(1, BINS + 1)
    (
        result,
        grad_hidden,
        gctx_own,
        gctx_oth,
        sent_up,
        sent_down,
        kept_up,
        kept_down,
        sums,
    ) = middle_layer(
        tokens,
        own[3],
        oth[3],
        neighbours,
        ids,
        cotangent,
        (w_up, w_down, w_out),
        ffn_got,
        edges,
        gain_ffn.reshape(1, width),
        w_gate.reshape(1, width),
    )
    up = Chain(None, 1)
    down = Chain(None, 1)
    up.pass_on(sent_up, kept_up, 1)
    down.pass_on(sent_down, kept_down, 1)
    up.add()
    down.add()
    sent = up.give(1)
    sent = down.first_half(far[0], sent)
    g_oth, da, gain_oth = attention_backward(
        doc_starts, oth, after(gctx_oth, sent), kv, 1, 2
    )
    up.add(da)
    down.add(da)
    sent = up.halve(far[0])
    sent = down.give(1, sent)
    attn = Chain(None, 1)
    sent = attn.pass_on(da[0], da[1], 1, sent)
    g_own_first, da_first, gain_first = attention_backward(
        doc_starts, own, after(gctx_own, sent), kv, 1, 1
    )
    da_first = da_first[0]
    attn.add(da_first)
    up.add(da_first)
    down.add(da_first)
    both = Chain(None, 0)
    both.pieces = tuple(lax.concatenate([u, d], 0) for u, d in zip(up.pieces, down.pieces))
    attn_sent = attn.total()
    attn_come = swap(attn_sent, "mp", 1)
    sent = both.halve(far[1], attn_sent)
    first_sent = after(da_first, sent)
    first_come = swap(first_sent, "dp", 1)
    g_own_last, da_last, gain_last = attention_backward(
        doc_starts, own, after(gctx_own, first_sent), kv, 0, 1
    )
    da_last = da_last[0]
    attn_come, first_come = lax.optimization_barrier((attn_come, first_come, da_last))[:2]
    attn = Chain(None, 1)
    attn.pieces = (da_last, first_come, attn_come)
    both.add(da_last)
    gain_part = sum(g[:, 0].sum(0) for g in (gain_oth, gain_first, gain_last))[None] / attn_gain
    small = lax.concatenate([sums[:4], gain_part], 0)
    first_bit, last_bit = far[:2]

    def quarter(piece, by_first, by_last):
        at = 2 * (bit_of("dp", first_bit) ^ by_first) + (bit_of("dp", last_bit) ^ by_last)
        size = piece.shape[1] // 4
        return lax.dynamic_slice_in_dim(piece, at * size, size, 1)

    sent = both.send(far[2])
    sent_x = after(attn.total(lambda p: quarter(p, 1, 0)), sent)
    sent_z = attn.total(lambda p: quarter(p, 0, 1))
    sent_d = attn.total(lambda p: quarter(p, 1, 1))
    kept = attn.total(lambda p: quarter(p, 0, 0))
    come_x = swap(sent_x, "dp", first_bit)
    come_z = swap(sent_z, "dp", last_bit)
    come_d = swap_diagonal(sent_d, first_bit, last_bit)
    small_sent = after(small, sent_x, sent_z, sent_d)
    small_come = swap(small_sent, "mp", 1)
    grad_input = input_grad(
        tokens,
        after(grad_hidden, small_sent),
        attn_gain,
        (g_oth, g_own_first, g_own_last),
        (oth[0], own[0]),
    )
    come_x, come_z, come_d, small_come = lax.optimization_barrier(
        (come_x, come_z, come_d, small_come, grad_input)
    )[:4]
    ride = Ride(small_sent + small_come)
    total = sum(part.astype(F32) for part in (kept, come_x, come_z, come_d)).astype(BF16)
    ffn_x = ffn_z = None
    for bit in far[2:]:
        sent = ride.below(total)
        come = swap(sent, "dp", bit)
        if bit == far[2]:
            ffn_sent = add_low(both.sent, after(both.come, sent))
            for far_bit in far[3:]:
                ffn_sent = add_low(ffn_sent, swap(ffn_sent, "dp", far_bit))
            ffn_x = swap(ffn_sent, "dp", first_bit)
            ffn_z = swap(ffn_sent, "dp", last_bit)
            ffn_d = swap_diagonal(ffn_sent, first_bit, last_bit)
            come = after(come, ffn_sent)
        total = add_low(total, ride.add(come, total))
    sent = ride.below(total)
    come_x = swap(sent, "dp", first_bit)
    come_z = swap(sent, "dp", last_bit)
    come_d = swap_diagonal(sent, first_bit, last_bit)
    come_x, come_z, come_d, ffn_x, ffn_z, ffn_d = lax.optimization_barrier(
        (come_x, come_z, come_d, ffn_x, ffn_z, ffn_d)
    )
    flat = total.reshape(-1, width)
    parts = [ride.add(come, flat) for come in (come_x, come_z, come_d)]
    shape = total.shape
    total = join_four(
        flat.reshape(shape).swapaxes(0, 1),
        *[part.reshape(shape).swapaxes(0, 1) for part in parts],
        far[0],
        far[1],
    )
    total = total.reshape(-1, *shape[:1], width).swapaxes(0, 1)
    sent = ride.below(total)
    come = swap(sent, "dp", 1)
    ffn_total = after(join_four(ffn_sent, ffn_x, ffn_z, ffn_d, far[0], far[1]), sent)
    ffn_come = swap(ffn_total, "dp", 1)
    grads = finish(
        (ffn_total, ffn_come),
        (total, come),
        ride.rows,
        count * dp * lax.axis_size("mp"),
    )
    gain_attn_sum, gain_ffn_sum, gate_sum, mean, histogram = grads[6:]
    return (
        result,
        grad_input,
        *grads[:6],
        gain_attn_sum.reshape(width),
        gain_ffn_sum.reshape(width),
        gate_sum.reshape(width),
        mean.reshape(()),
        histogram.reshape(BINS),
    )


def solution(mesh):
    in_specs = (
        P(("dp", "mp"), None, None),
        P("dp", None, None),
        P(("dp", "mp"), None, None, None),
        P(("dp", "mp"), None, None),
        P("dp"),
        P(),
        P(None, "mp"),
        P(None, "mp"),
        P(None, "mp"),
        P("mp", None),
        P(None, "mp"),
        P("mp", None),
        P(),
        P(),
        P(),
        P(("dp", "mp"), None, None),
    )
    out_specs = (
        P(("dp", "mp"), None, None),
        P(("dp", "mp"), None, None),
        P(None, "mp"),
        P(None, "mp"),
        P(None, "mp"),
        P("mp", None),
        P(None, "mp"),
        P("mp", None),
        P(),
        P(),
        P(),
        P(),
        P(),
    )
    return jax.shard_map(shards, mesh=mesh, in_specs=in_specs, out_specs=out_specs, check_vma=False)
```

```python
import functools

import jax
import jax.numpy as jnp
from jax import lax
from jax.experimental import pallas as pl
from jax.experimental.pallas import tpu as pltpu
from jax.sharding import PartitionSpec as P

HEAD = 64
NEIGH = 4
BINS = 128
PAIR = 2 * HEAD
QROWS = 256
TILE = 256
GROUP = 64

EPS = 1e-05
BF16 = jnp.bfloat16
F32 = jnp.float32
VMEM_LIMIT = 56 * 1024 * 1024
FORWARD_VMEM = 52 * 1024 * 1024
BACKWARD_VMEM = 48 * 1024 * 1024
INPUT_VMEM = 40 * 1024 * 1024
FINISH_VMEM = 24 * 1024 * 1024


def dot(left, right, left_dim=1, right_dim=0):
    return lax.dot_general(
        left, right, (((left_dim,), (right_dim,)), ((), ())), preferred_element_type=F32
    )


def normalize(values):
    centre = values - jnp.mean(values, -1, keepdims=True)
    spread = jnp.mean(centre * centre, -1, keepdims=True)
    rstd = lax.rsqrt(spread + EPS)
    return centre * rstd, rstd


def core_index():
    return lax.rem(lax.axis_index("dp"), 2)


def head_lanes(rows, head):
    lane = lax.broadcasted_iota(jnp.int32, (rows, PAIR), 1)
    return (lane >= head * HEAD) & (lane < (head + 1) * HEAD)


def only_head(block, head):
    return jnp.where(head_lanes(block.shape[0], head), block, jnp.zeros_like(block))


def attend(qkv_ref, p_ref, ctx_ref, length, with_memory):
    values = [only_head(qkv_ref[0, 0, pl.ds(3 * length, 2 * length), :], head) for head in range(2)]
    low = 0 if with_memory else length
    for first in range(0, length, QROWS):
        rows = pl.ds(first, QROWS)
        high = length + first + QROWS
        total = None
        for head in range(2):
            query = only_head(qkv_ref[0, 0, rows, :], head)
            scores = dot(query, qkv_ref[0, 0, pl.ds(length + low, high - low), :], 1, 1)
            seg = scores[:, length - low :]
            at = lax.broadcasted_iota(jnp.int32, seg.shape, 0) + first
            key = lax.broadcasted_iota(jnp.int32, seg.shape, 1)
            seg = jnp.where(key <= at, seg, -1e30)
            top = jnp.max(seg, -1, keepdims=True)
            if with_memory:
                mem = scores[:, :length]
                top = jnp.maximum(top, jnp.max(mem, -1, keepdims=True))
                mem = jnp.exp(mem - top)
            probs = jnp.exp(seg - top)
            mass = jnp.sum(probs, -1, keepdims=True)
            if with_memory:
                mass = mass + jnp.sum(mem, -1, keepdims=True)
            part = 1.0 / mass
            probs = (probs * part).astype(BF16)
            if with_memory:
                probs = jnp.concatenate([(mem * part).astype(BF16), probs], 1)
            p_ref[0, 0, head, rows, pl.ds(low, high - low)] = probs
            add = dot(probs, values[head][low:high])
            total = add if total is None else total + add
        ctx_ref[0, rows, :] = total.astype(BF16)


def forward_body(starts_ref, kv_ref, pack_ref, qkv_ref, p_ref, ctx_ref):
    length = kv_ref.shape[1] // 2
    pair = pl.program_id(1)
    kv = kv_ref[0]
    here = pl.multiple_of(3 * pair * PAIR, PAIR)
    query = dot(kv[length:], pack_ref[:, pl.ds(here, PAIR)]).astype(BF16)
    qkv_ref[0, 0, pl.ds(0, length), :] = (query.astype(F32) * HEAD ** (-0.5)).astype(BF16)
    both = dot(kv, pack_ref[:, pl.ds(here + PAIR, 2 * PAIR)]).astype(BF16)
    qkv_ref[0, 0, pl.ds(length, 2 * length), :] = both[:, :PAIR]
    qkv_ref[0, 0, pl.ds(3 * length, 2 * length), :] = both[:, PAIR:]
    start = starts_ref[lax.axis_index("mp") * pl.num_programs(0) + pl.program_id(0)]

    @pl.when(start == 0)
    def _():
        attend(qkv_ref, p_ref, ctx_ref, length, True)

    @pl.when(start != 0)
    def _():
        attend(qkv_ref, p_ref, ctx_ref, length, False)


def first_forward(
    starts_ref, tok_ref, mem_ref, gain_ref, wq_ref, wk_ref, wv_ref, kv_ref, pack_ref, *outs
):
    length = tok_ref.shape[1]

    @pl.when((pl.program_id(0) == 0) & (pl.program_id(1) == 0))
    def _():
        for i, weight in enumerate((wq_ref, wk_ref, wv_ref)):
            for p in range(2):
                pack_ref[:, pl.ds((3 * p + i) * PAIR, PAIR)] = weight[:, pl.ds(p * PAIR, PAIR)]

    @pl.when(pl.program_id(1) == 0)
    def _():
        gain = gain_ref[...]
        kv_ref[0, pl.ds(0, length), :] = (normalize(mem_ref[0].astype(F32))[0] * gain).astype(BF16)
        kv_ref[0, pl.ds(length, length), :] = (
            normalize(tok_ref[0].astype(F32))[0] * gain
        ).astype(BF16)

    forward_body(starts_ref, kv_ref, pack_ref, *outs)


def second_forward(starts_ref, kv_ref, mine_ref, sibling_ref, pack_ref, *outs):
    rows = mine_ref.shape[0]
    core = core_index()

    @pl.when((pl.program_id(0) == 0) & (pl.program_id(1) == 0))
    def _():
        for block, which in ((mine_ref, core), (sibling_ref, 1 - core)):
            to = pl.ds(pl.multiple_of(which * rows, rows), rows)
            for i in range(3):
                for p in range(2):
                    pack_ref[to, pl.ds((3 * p + i) * PAIR, PAIR)] = block[
                        :, pl.ds((2 * i + p) * PAIR, PAIR)
                    ]

    forward_body(starts_ref, kv_ref, pack_ref, *outs)


def attention_forward(starts, tokens, memory, gain, kv, weights):
    rows, length, width = tokens.shape
    pairs = 2
    pack = (width, 3 * pairs * PAIR)
    outs = [
        jax.ShapeDtypeStruct(pack, BF16),
        jax.ShapeDtypeStruct((rows, pairs, 5 * length, PAIR), BF16),
        jax.ShapeDtypeStruct((rows, pairs, 2, length, 2 * length), BF16),
        jax.ShapeDtypeStruct((rows, length, pairs * PAIR), BF16),
    ]
    out_specs = [
        pl.BlockSpec(pack, lambda r, p: (0, 0)),
        pl.BlockSpec((1, 1, 5 * length, PAIR), lambda r, p: (r, p, 0, 0)),
        pl.BlockSpec((1, 1, 2, length, 2 * length), lambda r, p: (r, p, 0, 0, 0)),
        pl.BlockSpec((1, length, PAIR), lambda r, p: (r, 0, p)),
    ]
    kv_spec = pl.BlockSpec((1, 2 * length, width), lambda r, p: (r, 0, 0))
    in_specs = [pl.BlockSpec(memory_space=pltpu.SMEM)]
    if kv is None:
        body = first_forward
        ins = [tokens, memory, gain]
        in_specs += [
            pl.BlockSpec((1, length, width), lambda r, p: (r, 0, 0)),
            pl.BlockSpec((1, length, width), lambda r, p: (lax.axis_index("mp") * rows + r, 0, 0)),
            pl.BlockSpec((1, width), lambda r, p: (0, 0)),
        ]
        outs = [jax.ShapeDtypeStruct((rows, 2 * length, width), BF16)] + outs
        out_specs = [kv_spec] + out_specs
    else:
        body = second_forward
        ins = [kv]
        in_specs += [kv_spec]
    in_specs += [pl.BlockSpec(w.shape, lambda r, p: (0, 0)) for w in weights]
    return pl.pallas_call(
        body,
        grid=(rows, pairs),
        in_specs=in_specs,
        out_specs=out_specs,
        out_shape=outs,
        compiler_params=pltpu.CompilerParams(vmem_limit_bytes=FORWARD_VMEM),
        cost_estimate=pl.CostEstimate(flops=6 * 10**9, bytes_accessed=16 * 2**20, transcendentals=0),
    )(starts, *ins, *weights)


def gelu_parts(pre):
    c0 = 0.7978845608028654
    c1 = c0 * 0.044715
    square = pre * pre
    part = 0.5 * jnp.tanh(pre * (c1 * square + c0)) + 0.5
    act = pre * part
    return act, part + act * (1.0 - part) * ((6.0 * c1) * square + 2.0 * c0)


def weighted(weights, values):
    return sum(w * v for w, v in zip(weights[1:], values[1:])) + weights[0] * values[0]


def middle_body(
    tok_ref,
    ctx_own_ref,
    ctx_oth_ref,
    nb_ref,
    ids_ref,
    cot_ref,
    up_far,
    down_far,
    out_far,
    mine_far,
    sibling_far,
    edges_ref,
    gain_ref,
    wgate_ref,
    result_ref,
    grad_hidden_ref,
    gctx_own_ref,
    gctx_oth_ref,
    sent_up_far,
    sent_down_far,
    kept_up_far,
    kept_down_far,
    sums_ref,
    e_ref,
    hist_ref,
    edge_ref,
    pick_ref,
    up_ref,
    down_ref,
    out_ref,
    oth_ref,
    stage_ref,
    ffn_in_ref,
    act_ref,
    gpre_ref,
    cots_ref,
    low_ref,
    ctx_ref,
    in_sems,
    out_sems,
):
    step = pl.program_id(0)
    here = pl.ds(pl.multiple_of(step * TILE, TILE), TILE)
    width = tok_ref.shape[-1]
    hidden_units = down_ref.shape[0]
    half = width // 2
    chunks = hidden_units // width
    scale = width ** (-0.5)
    core = core_index()
    copies = [
        pltpu.make_async_copy(far, near, in_sems.at[i])
        for i, (far, near) in enumerate(
            (
                (out_far, out_ref),
                (mine_far, oth_ref.at[core]),
                (sibling_far, oth_ref.at[1 - core]),
                (up_far, up_ref),
                (down_far, down_ref),
            )
        )
    ]

    @pl.when(step == 0)
    def _():
        for copy in copies:
            copy.start()
        sums_ref[...] = jnp.zeros_like(sums_ref)
        hist_ref[...] = jnp.zeros_like(hist_ref)
        row = lax.broadcasted_iota(jnp.int32, pick_ref.shape, 0)
        column = lax.broadcasted_iota(jnp.int32, pick_ref.shape, 1)
        from_row = NEIGH * (row % GROUP) + row // GROUP
        pick_ref[...] = (column == from_row).astype(F32).astype(BF16)
        edges = edges_ref[...].astype(F32)
        for i in range(2):
            edge_ref[i] = jnp.broadcast_to(edges[:, i : i + BINS], (BINS, BINS)).T
        for copy in copies[:3]:
            copy.wait()

    def other_out():
        at = pl.ds(2 * width, half // 2)
        return jnp.concatenate([oth_ref[0, at, :], oth_ref[1, at, :]], 0)

    wgate = wgate_ref[...]
    gain = gain_ref[...]

    def front():
        ctx_ref[here, pl.ds(0, half)] = ctx_own_ref[0]
        ctx_ref[here, pl.ds(half, half)] = ctx_oth_ref[0]
        cots_ref[here, :] = cot_ref[0]
        hidden = (
            tok_ref[0].astype(F32)
            + dot(ctx_own_ref[0], out_ref[...])
            + dot(ctx_oth_ref[0], other_out())
        )
        for first in range(0, TILE, GROUP):
            mixed_rows = nb_ref[0, pl.ds(first, GROUP)].reshape(NEIGH * GROUP, width)
            planes = dot(pick_ref[...], mixed_rows)
            for k in range(NEIGH):
                e_ref[k, pl.ds(first, GROUP), :] = planes[k * GROUP : (k + 1) * GROUP]
        affinity = [
            jnp.sum(e_ref[k] * hidden, -1, keepdims=True) * scale for k in range(NEIGH)
        ]
        top = jnp.maximum(
            jnp.maximum(affinity[0], affinity[1]), jnp.maximum(affinity[2], affinity[3])
        )
        raised = [jnp.exp(a - top) for a in affinity]
        inverse = 1.0 / (raised[0] + raised[1] + raised[2] + raised[3])
        weights = [a * inverse for a in raised]
        gate = jax.nn.sigmoid(jnp.sum(hidden * wgate, -1, keepdims=True))
        recalled = weighted(weights, [e_ref[k] for k in range(NEIGH)])
        mixed = hidden + gate * recalled
        normal, rstd = normalize(mixed)
        ffn_in_ref[here, :] = (normal * gain).astype(BF16)
        return hidden, weights, gate, mixed, normal, rstd

    def other_up():
        rows = [
            jnp.concatenate([oth_ref[h, pl.ds(c * half, half), :] for c in range(chunks)], 1)
            for h in range(2)
        ]
        return jnp.concatenate(rows, 0)

    def other_down():
        return jnp.concatenate([oth_ref[c, pl.ds(width, width), :] for c in range(chunks)], 0)

    def feed():
        ffn_in = ffn_in_ref[here, :]
        cot = cot_ref[0]
        for side in range(2):
            for c in range(chunks):
                if side == 0:
                    up = up_ref[:, pl.ds(c * width, width)]
                    down = down_ref[pl.ds(c * width, width), :]
                else:
                    part = pl.ds(c * half, half)
                    up = jnp.concatenate([oth_ref[0, part, :], oth_ref[1, part, :]], 0)
                    down = oth_ref[c, pl.ds(width, width), :]
                at = pl.ds((side * chunks + c) * width, width)
                act, slope = gelu_parts(dot(ffn_in, up))
                act_ref[here, at] = act.astype(BF16)
                gpre_ref[here, at] = (dot(cot, down, 1, 1) * slope).astype(BF16)
        own = pl.ds(0, hidden_units)
        oth = pl.ds(hidden_units, hidden_units)
        down_sum = dot(act_ref[here, own], down_ref[...]) + dot(act_ref[here, oth], other_down())
        grad_sum = dot(gpre_ref[here, own], up_ref[...], 1, 1) + dot(
            gpre_ref[here, oth], other_up(), 1, 1
        )
        return down_sum, grad_sum

    def back(kept, sums):
        hidden, weights, gate, mixed, normal, rstd = kept
        down_sum, grad_sum = sums
        result_ref[0] = (mixed + down_sum).astype(BF16)
        gain_part = jnp.sum(grad_sum * normal, 0, keepdims=True)
        grad_normal = grad_sum * gain
        grad_mixed = cot_ref[0].astype(F32) + rstd * (
            grad_normal
            - jnp.mean(grad_normal, -1, keepdims=True)
            - normal * jnp.mean(grad_normal * normal, -1, keepdims=True)
        )
        pulls = [
            jnp.sum(grad_mixed * e_ref[k], -1, keepdims=True) for k in range(NEIGH)
        ]
        pulled = weighted(weights, pulls)
        gate_grad = gate * (1.0 - gate) * pulled
        grad_hidden = grad_mixed + gate_grad * wgate
        for k in range(NEIGH):
            grad_hidden = (
                grad_hidden + (scale * gate * weights[k] * (pulls[k] - pulled)) * e_ref[k]
            )
        grad_hidden_ref[0] = grad_hidden
        low = grad_hidden.astype(BF16)
        low_ref[here, :] = low
        gctx_own_ref[0] = dot(low, out_ref[...], 1, 1).astype(BF16)
        gctx_oth_ref[0] = dot(low, other_out(), 1, 1).astype(BF16)
        gate_wide = jnp.broadcast_to(gate, (TILE, BINS)).T
        low_edge = jnp.concatenate([edge_ref[0]] * (TILE // BINS), 1)
        high_edge = jnp.concatenate([edge_ref[1]] * (TILE // BINS), 1)
        mass = jnp.zeros_like(gate_wide)
        for k in range(NEIGH):
            ids = ids_ref[0, pl.ds(k, 1), :].astype(F32)
            mass = mass + jnp.where((ids >= low_edge) & (ids < high_edge), gate_wide, 0.0)
        gate_sum = jnp.sum(jnp.broadcast_to(gate, (TILE, width)), 0, keepdims=True)
        sums_ref[pl.ds(0, 1), :] += gain_part
        sums_ref[pl.ds(1, 1), :] += gate_sum
        sums_ref[pl.ds(2, 1), :] += jnp.sum(gate_grad * hidden, 0, keepdims=True)
        hist_ref[...] += mass

    kept = front()

    @pl.when(step == 0)
    def _():
        for copy in copies[3:]:
            copy.wait()

    back(kept, feed())

    @pl.when(step == pl.num_programs(0) - 1)
    def _():
        sums_ref[pl.ds(3, 1), pl.ds(0, BINS)] = jnp.sum(hist_ref[...].T, 0, keepdims=True)
        cut = sent_up_far.shape[1]
        moves = []
        for fars, which in (
            ((sent_up_far, sent_down_far), 1 - core),
            ((kept_up_far, kept_down_far), core),
        ):
            for side in range(2):
                at = pl.ds(pl.multiple_of((side * chunks + which) * width, width), width)
                here = pl.ds(pl.multiple_of((2 * side + which) * PAIR, PAIR), PAIR)
                slot = len(moves) // 3
                first = 0
                for left, right in (
                    (ffn_in_ref[...], gpre_ref[:, at]),
                    (act_ref[:, at], cots_ref[...]),
                    (ctx_ref[:, here], low_ref[...]),
                ):
                    piece = dot(left, right, 0, 0).astype(BF16)
                    stage_ref[slot, pl.ds(first, piece.shape[0]), :] = piece
                    first += piece.shape[0]
                part = cut // 2
                own = lax.rem(lax.div(lax.axis_index("dp"), 2), 2) * part
                for start, size, far, to in (
                    (0, cut, fars[0], 0),
                    (cut, part, fars[1], part - own),
                    (cut + part, part, fars[1], own),
                ):
                    move = pltpu.make_async_copy(
                        stage_ref.at[slot, pl.ds(start, size), :],
                        far.at[side, pl.ds(pl.multiple_of(to, part), size), :],
                        out_sems.at[len(moves)],
                    )
                    move.start()
                    moves.append(move)
        for move in moves:
            move.wait()


def middle_layer(tokens, ctx_own, ctx_oth, nb, ids, cot, weights, received, edges, gain, wgate):
    rows, length, width = tokens.shape
    hidden_units = weights[1].shape[0]
    steps = length // TILE
    tiles = rows * steps
    count = rows * length
    assert hidden_units == 2 * width

    def place_of(i):
        return i // steps, i % steps

    def tiled(last):
        return pl.BlockSpec((1, TILE, last), lambda i: (*place_of(i), 0))

    def whole(shape):
        return pl.BlockSpec(shape, lambda i: (0,) * len(shape))

    far = pl.BlockSpec(memory_space=pl.ANY)
    return pl.pallas_call(
        middle_body,
        grid=(tiles,),
            in_specs=[
                tiled(width),
                tiled(width // 2),
                tiled(width // 2),
                pl.BlockSpec((1, TILE, NEIGH, width), lambda i: (*place_of(i), 0, 0)),
                pl.BlockSpec(
                    (1, NEIGH, TILE), lambda i: (place_of(i)[0], 0, place_of(i)[1])
                ),
                tiled(width),
                *[far] * 5,
                whole((1, BINS + 1)),
                whole((1, width)),
                whole((1, width)),
            ],
            out_specs=[
                tiled(width),
                tiled(width),
                tiled(width // 2),
                tiled(width // 2),
                far,
                far,
                far,
                far,
                whole((8, width)),
            ],
            scratch_shapes=[
                pltpu.VMEM((NEIGH, TILE, width), F32),
                pltpu.VMEM((BINS, TILE), F32),
                pltpu.VMEM((2, BINS, BINS), F32),
                pltpu.VMEM((NEIGH * GROUP, NEIGH * GROUP), BF16),
                *[pltpu.VMEM(w.shape, BF16) for w in weights],
                pltpu.VMEM((2, *received[0].shape), BF16),
                pltpu.VMEM((4, 2 * width + PAIR, width), BF16),
                pltpu.VMEM((count, width), BF16),
                pltpu.VMEM((count, 2 * hidden_units), BF16),
                pltpu.VMEM((count, 2 * hidden_units), BF16),
                pltpu.VMEM((count, width), BF16),
                pltpu.VMEM((count, width), BF16),
                pltpu.VMEM((count, width), BF16),
                pltpu.SemaphoreType.DMA((5,)),
                pltpu.SemaphoreType.DMA((12,)),
            ],
        out_shape=[
            jax.ShapeDtypeStruct((rows, length, width), BF16),
            jax.ShapeDtypeStruct((rows, length, width), F32),
            jax.ShapeDtypeStruct((rows, length, width // 2), BF16),
            jax.ShapeDtypeStruct((rows, length, width // 2), BF16),
            *[jax.ShapeDtypeStruct((2, width + PAIR // 2, width), BF16)] * 4,
            jax.ShapeDtypeStruct((8, width), F32),
        ],
        compiler_params=pltpu.CompilerParams(vmem_limit_bytes=VMEM_LIMIT),
        cost_estimate=pl.CostEstimate(flops=15 * 10**9, bytes_accessed=30 * 2**20, transcendentals=0),
    )(tokens, ctx_own, ctx_oth, nb, ids, cot, *weights, *received, edges, gain, wgate)


def attend_back(
    head, qkv_ref, p_ref, gctx_ref, ctx_ref, ds_ref, dq_ref, t_ref, dk_ref, dv_ref, with_memory
):
    length = ctx_ref.shape[1]
    grad = only_head(gctx_ref[0], head)
    delta = jnp.sum(grad.astype(F32) * ctx_ref[0].astype(F32), -1, keepdims=True)
    keys = only_head(qkv_ref[0, 0, pl.ds(length, 2 * length), :], head)
    lanes = pl.ds(pl.multiple_of(head * HEAD, HEAD), HEAD)
    low = 0 if with_memory else length
    for first in range(0, length, QROWS):
        rows = pl.ds(first, QROWS)
        high = length + first + QROWS
        here = pl.ds(low, high - low)
        probs = p_ref[0, 0, 0, rows, here].astype(F32)
        values = qkv_ref[0, 0, pl.ds(3 * length + low, high - low), :]
        grad_probs = dot(grad[first : first + QROWS], values, 1, 1)
        ds = (probs * (grad_probs - delta[first : first + QROWS])).astype(BF16)
        ds_ref[rows, here] = ds
        dq_ref[rows, :] += dot(ds, keys[low:high])
    for out_ref, left, right in (
        (dk_ref, t_ref[0, lanes, :], ds_ref),
        (dv_ref, t_ref[1, lanes, :], p_ref.at[0, 0, 0]),
    ):
        if not with_memory:
            out_ref[lanes, :length] = jnp.zeros((HEAD, length), BF16)
        for first in range(0, length, QROWS):
            start = low if first == 0 else length + first
            here = pl.ds(start, length + first + QROWS - start)
            out_ref[lanes, here] = dot(
                left[:, first:], right[pl.ds(first, length - first), here]
            ).astype(BF16)


def backward_body(
    starts_ref,
    qkv_ref,
    p_ref,
    gctx_ref,
    ctx_ref,
    kv_far,
    pack_ref,
    grads_ref,
    dw_ref,
    gain_ref,
    ds_ref,
    dq_ref,
    t_ref,
    dk_ref,
    dv_ref,
    acc_ref,
    kv_ref,
    sem,
):
    length = ctx_ref.shape[1]
    row = pl.program_id(1)
    head = pl.program_id(2)
    start = starts_ref[lax.axis_index("mp") * pl.num_programs(1) + row]
    fetch = pltpu.make_async_copy(kv_far.at[row], kv_ref, sem)
    args = (qkv_ref, p_ref, gctx_ref, ctx_ref, ds_ref, dq_ref, t_ref, dk_ref, dv_ref)

    @pl.when(head == 0)
    def _():
        fetch.start()
        dq_ref[...] = jnp.zeros_like(dq_ref)
        t_ref[0] = qkv_ref[0, 0, pl.ds(0, length), :].T
        t_ref[1] = gctx_ref[0].T

    @pl.when(start == 0)
    def _():
        attend_back(head, *args, True)

    @pl.when(start != 0)
    def _():
        attend_back(head, *args, False)

    @pl.when(head == 1)
    def _():
        dq_t = (dq_ref[...] * HEAD ** (-0.5)).astype(BF16).T
        grads_ref[0, 0, pl.ds(0, PAIR), :] = dq_t
        grads_ref[0, 0, pl.ds(PAIR, PAIR), :] = dk_ref[:, length:]
        grads_ref[0, 0, pl.ds(2 * PAIR, PAIR), :] = dv_ref[:, length:]
        fetch.wait()
        for i, add in enumerate(
            (
                dot(dq_t, kv_ref[pl.ds(length, length), :]),
                dot(dk_ref[...], kv_ref[...]),
                dot(dv_ref[...], kv_ref[...]),
            )
        ):
            acc_ref[i] = jnp.where(row == 0, add, acc_ref[i] + add)

    @pl.when((head == 1) & (row == pl.num_programs(1) - 1))
    def _():
        part = None
        for i in range(3):
            total = acc_ref[i]
            dw_ref[0, i] = total.astype(BF16)
            weight = pack_ref[:, pl.ds(i * PAIR, PAIR)].T.astype(F32)
            add = jnp.sum(total * weight, 0, keepdims=True)
            part = add if part is None else part + add
        gain_ref[0] = jnp.broadcast_to(part, gain_ref.shape[1:])


def attention_backward(starts, saved, gctx, kv, shift, many):
    pack, qkv, p, ctx = saved
    rows, _, _, length, _ = p.shape
    width = kv.shape[-1]

    def pair(n):
        return lax.rem(core_index() + shift + n, 2)

    return pl.pallas_call(
        backward_body,
        grid=(many, rows, 2),
        in_specs=[
            pl.BlockSpec(memory_space=pltpu.SMEM),
            pl.BlockSpec((1, 1, 5 * length, PAIR), lambda n, r, h: (r, pair(n), 0, 0)),
            pl.BlockSpec((1, 1, 1, length, 2 * length), lambda n, r, h: (r, pair(n), h, 0, 0)),
            pl.BlockSpec((1, length, PAIR), lambda n, r, h: (r, 0, pair(n))),
            pl.BlockSpec((1, length, PAIR), lambda n, r, h: (r, 0, pair(n))),
            pl.BlockSpec(memory_space=pl.ANY),
            pl.BlockSpec((width, 3 * PAIR), lambda n, r, h: (0, pair(n))),
        ],
        out_specs=[
            pl.BlockSpec((1, 1, 3 * PAIR, length), lambda n, r, h: (n, r, 0, 0)),
            pl.BlockSpec((1, 3, PAIR, width), lambda n, r, h: (n, 0, 0, 0)),
            pl.BlockSpec((1, 8, width), lambda n, r, h: (n, 0, 0)),
        ],
        scratch_shapes=[
            pltpu.VMEM((length, 2 * length), BF16),
            pltpu.VMEM((length, PAIR), F32),
            pltpu.VMEM((2, PAIR, length), BF16),
            pltpu.VMEM((PAIR, 2 * length), BF16),
            pltpu.VMEM((PAIR, 2 * length), BF16),
            pltpu.VMEM((3, PAIR, width), F32),
            pltpu.VMEM((2 * length, width), BF16),
            pltpu.SemaphoreType.DMA,
        ],
        out_shape=[
            jax.ShapeDtypeStruct((many, rows, 3 * PAIR, length), BF16),
            jax.ShapeDtypeStruct((many, 3, PAIR, width), BF16),
            jax.ShapeDtypeStruct((many, 8, width), F32),
        ],
        compiler_params=pltpu.CompilerParams(vmem_limit_bytes=BACKWARD_VMEM),
        cost_estimate=pl.CostEstimate(
            flops=4 * 10**9 * many, bytes_accessed=8 * 2**20 * many, transcendentals=0
        ),
    )(starts, qkv, p, gctx, ctx, kv, pack)


def input_body(
    tok_ref,
    grad_hidden_ref,
    gain_ref,
    oth_ref,
    own_first_ref,
    own_last_ref,
    oth_pack_ref,
    own_pack_ref,
    out_ref,
):
    core = core_index()
    total = None
    for block, pack, which in (
        (oth_ref[0, 0], oth_pack_ref, 1 - core),
        (oth_ref[1, 0], oth_pack_ref, core),
        (own_first_ref[0, 0], own_pack_ref, 1 - core),
        (own_last_ref[0, 0], own_pack_ref, core),
    ):
        here = pl.ds(pl.multiple_of(which * 3 * PAIR, 3 * PAIR), 3 * PAIR)
        add = dot(block, pack[:, here], 0, 1)
        total = add if total is None else total + add
    normal, rstd = normalize(tok_ref[0].astype(F32))
    grad = total * gain_ref[...]
    out_ref[0] = (
        grad_hidden_ref[0]
        + rstd
        * (
            grad
            - jnp.mean(grad, -1, keepdims=True)
            - normal * jnp.mean(grad * normal, -1, keepdims=True)
        )
    ).astype(BF16)


def input_grad(tokens, grad_hidden, gain, grads, packs):
    rows, length, width = tokens.shape
    row = pl.BlockSpec((1, length, width), lambda r: (r, 0, 0))

    def whole(array):
        return pl.BlockSpec(array.shape, lambda r: (0, 0))

    return pl.pallas_call(
        input_body,
        grid=(rows,),
        in_specs=[
            row,
            row,
            whole(gain),
            *[pl.BlockSpec((g.shape[0], 1) + g.shape[2:], lambda r: (0, r, 0, 0)) for g in grads],
            *[whole(p) for p in packs],
        ],
        out_specs=row,
        out_shape=jax.ShapeDtypeStruct(tokens.shape, BF16),
        compiler_params=pltpu.CompilerParams(vmem_limit_bytes=INPUT_VMEM),
        cost_estimate=pl.CostEstimate(flops=2 * 10**9, bytes_accessed=8 * 2**20, transcendentals=0),
    )(tokens, grad_hidden, gain, *grads, *packs)


def finish_body(
    ffn_mine,
    ffn_sibling,
    attn_mine,
    attn_sibling,
    small_ref,
    q_far,
    k_far,
    v_far,
    out_far,
    up_far,
    down_far,
    gain_attn_ref,
    gain_ffn_ref,
    gate_ref,
    mean_ref,
    hist_ref,
    q_ref,
    k_ref,
    v_ref,
    out_ref,
    up_ref,
    down_ref,
    sems,
    tokens,
):
    core = core_index()
    width = up_far.shape[0]
    rows = attn_mine.shape[1]
    moves = []

    def pair(mine, sibling):
        return (
            jnp.where(core == 0, mine, sibling).astype(F32),
            jnp.where(core == 0, sibling, mine).astype(F32),
        )

    def move(near, far):
        moves.append(pltpu.make_async_copy(near, far, sems.at[len(moves)]))
        moves[-1].start()

    size = ffn_mine.shape[1] // 2
    pieces = [(x, pl.ds(y * size, size)) for y in range(2) for x in range(2)]
    halves = zip(*(pair(ffn_mine[x, y, :], ffn_sibling[x, y, :]) for x, y in pieces))
    for which, parts in enumerate(halves):
        rows_of = jnp.concatenate(parts, 0)
        to = pl.ds(which * width, width)
        up_ref[:, to] = rows_of[:width]
        down_ref[to, :] = rows_of[width : 2 * width]
        out_ref[pl.ds(which * PAIR, PAIR), :] = rows_of[2 * width :]
        move(down_ref.at[to, :], down_far.at[to, :])
    move(up_ref, up_far)
    move(out_ref, out_far)
    for i, (near, far) in enumerate(((q_ref, q_far), (k_ref, k_far), (v_ref, v_far))):
        first, last = pair(attn_mine[i], attn_sibling[pl.ds(i * rows, rows), :])
        near[...] = jnp.concatenate([first, last], 0).T
        move(near, far)
    count = small_ref.shape[0]
    below = attn_sibling[pl.ds(3 * rows, -(-3 * count // 16) * 16), :].astype(F32)
    small = small_ref[...]
    for i in range(3):
        small = small + below[i * count : (i + 1) * count]
    gain_ffn_ref[...] = small[0:1]
    mean_ref[...] = small[1:2, 0:1] / tokens
    gate_ref[...] = small[2:3]
    hist_ref[...] = small[3:4, :BINS] * (BINS / (tokens * NEIGH))
    gain_attn_ref[...] = small[4:5]
    for one in moves:
        one.wait()


def finish(ffn, attn, small, tokens):
    width = ffn[0].shape[-1]
    quarter = attn[0].shape[1]
    shapes = [(width, 2 * quarter)] * 3
    shapes += [(2 * quarter, width), (width, 2 * width), (2 * width, width)]
    rows = [(1, width)] * 3 + [(1, 1), (1, BINS)]

    def whole(array):
        return pl.BlockSpec(array.shape, lambda i: (0,) * array.ndim)

    return pl.pallas_call(
        functools.partial(finish_body, tokens=tokens),
        grid=(1,),
        in_specs=[whole(a) for a in (*ffn, *attn, small)],
        out_specs=[pl.BlockSpec(memory_space=pl.ANY)] * 6
        + [pl.BlockSpec(s, lambda i: (0, 0)) for s in rows],
        scratch_shapes=[pltpu.VMEM(s, F32) for s in shapes] + [pltpu.SemaphoreType.DMA((8,))],
        out_shape=[jax.ShapeDtypeStruct(s, F32) for s in shapes + rows],
        compiler_params=pltpu.CompilerParams(vmem_limit_bytes=FINISH_VMEM),
    )(*ffn, *attn, small)


def swap(array, axis, bit):
    size = lax.axis_size(axis)
    return lax.ppermute(array, axis, [(i, i ^ bit) for i in range(size)])


def bit_of(axis, bit):
    return (lax.axis_index(axis) // bit) % 2


def part_of(array, which, dim):
    half = array.shape[dim] // 2
    return lax.dynamic_slice_in_dim(array, which * half, half, dim)


def add_low(left, right):
    return (left.astype(F32) + right.astype(F32)).astype(BF16)


def join(mine, other, bit, dim):
    return jnp.where(
        bit_of("dp", bit) == 0,
        lax.concatenate([mine, other], dim),
        lax.concatenate([other, mine], dim),
    )


def swap_diagonal(array, first, last):
    size = lax.axis_size("dp")
    return lax.ppermute(array, "dp", [(i, i ^ first ^ last) for i in range(size)])


def join_four(mine, by_first, by_last, by_both, first, last):
    return join(
        join(mine, by_last, last, 0)[None], join(by_first, by_both, last, 0)[None], first, 0
    )


def after(value, *others):
    return lax.optimization_barrier((value, *others))[0]


class Chain:
    def __init__(self, array, dim):
        self.pieces = (array,)
        self.dim = dim

    def total(self, cut=lambda piece: piece):
        pieces = [cut(piece) for piece in self.pieces]
        if len(pieces) == 1:
            return pieces[0]
        return sum(piece.astype(F32) for piece in pieces).astype(BF16)

    def pass_on(self, sent, kept, bit, *others):
        self.sent = after(sent, *others)
        self.kept = kept
        self.come = swap(self.sent, "dp", bit)
        return self.sent

    def halve(self, bit, *others):
        mine = bit_of("dp", bit)
        self.sent = after(self.total(lambda p: part_of(p, 1 - mine, self.dim)), *others)
        self.kept = self.total(lambda p: part_of(p, mine, self.dim))
        self.come = swap(self.sent, "dp", bit)
        return self.sent

    def first_half(self, bit, *others):
        half = self.pieces[0].shape[self.dim] // 2
        self.sent = after(
            self.total(lambda p: lax.slice_in_dim(p, 0, half, axis=self.dim)), *others
        )
        self.kept = self.total(lambda p: lax.slice_in_dim(p, half, 2 * half, axis=self.dim))
        self.come = swap(self.sent, "dp", bit)
        return self.sent

    def give(self, index, *others):
        self.sent = after(self.total(lambda p: p[index]), *others)
        self.kept = self.total(lambda p: p[1 - index])
        self.dim -= 1
        self.come = swap(self.sent, "mp", 1)
        return self.sent

    def send(self, bit, *others):
        self.sent = self.kept = after(self.total(), *others)
        self.come = swap(self.sent, "dp", bit)
        return self.sent

    def add(self, *others):
        self.come = after(self.come, *others)
        self.pieces = (self.kept, self.come)

    def join(self, bit, *others):
        self.pieces = (join(self.sent, after(self.come, *others), bit, self.dim),)


class Ride:
    def __init__(self, rows):
        self.rows = rows

    def below(self, array):
        left = self.rows
        parts = [array.reshape(-1, array.shape[-1])]
        for _ in range(3):
            part = lax.reduce_precision(left, 8, 7)
            parts.append(part.astype(BF16))
            left = left - part
        spare = -3 * left.shape[0] % 16
        parts.append(jnp.zeros((spare, left.shape[1]), BF16))
        return lax.concatenate(parts, 0)

    def add(self, block, like):
        size = like.size // like.shape[-1]
        count = self.rows.shape[0]
        for i in range(3):
            at = size + i * count
            self.rows = self.rows + block[at : at + count].astype(F32)
        return block[:size].reshape(like.shape)


def shards(
    tokens,
    memory,
    neighbours,
    neighbour_ids,
    doc_starts,
    bin_edges,
    w_query,
    w_key,
    w_value,
    w_out,
    w_up,
    w_down,
    gain_attn,
    gain_ffn,
    w_gate,
    cotangent,
):
    rows, length, width = tokens.shape
    count = rows * length
    dp = lax.axis_size("dp")
    core = bit_of("dp", 1)
    attn_gain = gain_attn.reshape(1, width)
    qkv = (w_query, w_key, w_value)
    far = []
    bit = 2
    while bit < dp:
        far.append(bit)
        bit *= 2

    qkv_sent = lax.concatenate([part_of(w, core, 0) for w in qkv], 1)
    up_part = part_of(w_up, core, 0)
    ffn_sent = lax.concatenate(
        [up_part[:, :width], up_part[:, width:], part_of(w_down, core, 0), part_of(w_out, core, 0)],
        0,
    )
    qkv_mine = swap(qkv_sent, "mp", 1)
    ffn_mine = swap(after(ffn_sent, qkv_sent), "mp", 1)
    kv, *own = attention_forward(
        doc_starts, after(tokens, qkv_sent, ffn_sent), memory, attn_gain, None, qkv
    )
    qkv_mine = after(qkv_mine, kv)
    qkv_got = (qkv_mine, swap(qkv_mine, "dp", 1))
    oth = attention_forward(doc_starts, tokens, memory, attn_gain, kv, qkv_got)
    ffn_mine = after(ffn_mine, oth[3])
    ffn_got = (ffn_mine, swap(ffn_mine, "dp", 1))
    ids = jnp.swapaxes(neighbour_ids, 1, 2)
    edges = bin_edges.reshape(1, BINS + 1)
    (
        result,
        grad_hidden,
        gctx_own,
        gctx_oth,
        sent_up,
        sent_down,
        kept_up,
        kept_down,
        sums,
    ) = middle_layer(
        tokens,
        own[3],
        oth[3],
        neighbours,
        ids,
        cotangent,
        (w_up, w_down, w_out),
        ffn_got,
        edges,
        gain_ffn.reshape(1, width),
        w_gate.reshape(1, width),
    )
    up = Chain(None, 1)
    down = Chain(None, 1)
    up.pass_on(sent_up, kept_up, 1)
    down.pass_on(sent_down, kept_down, 1)
    up.add()
    down.add()
    sent = up.give(1)
    sent = down.first_half(far[0], sent)
    g_oth, da, gain_oth = attention_backward(
        doc_starts, oth, after(gctx_oth, sent), kv, 1, 2
    )
    up.add(da)
    down.add(da)
    sent = up.halve(far[0])
    sent = down.give(1, sent)
    attn = Chain(None, 1)
    sent = attn.pass_on(da[0], da[1], 1, sent)
    g_own_first, da_first, gain_first = attention_backward(
        doc_starts, own, after(gctx_own, sent), kv, 1, 1
    )
    da_first = da_first[0]
    attn.add(da_first)
    up.add(da_first)
    down.add(da_first)
    both = Chain(None, 0)
    both.pieces = tuple(lax.concatenate([u, d], 0) for u, d in zip(up.pieces, down.pieces))
    attn_sent = attn.total()
    attn_come = swap(attn_sent, "mp", 1)
    sent = both.halve(far[1], attn_sent)
    first_sent = after(da_first, sent)
    first_come = swap(first_sent, "dp", 1)
    g_own_last, da_last, gain_last = attention_backward(
        doc_starts, own, after(gctx_own, first_sent), kv, 0, 1
    )
    da_last = da_last[0]
    attn_come, first_come = lax.optimization_barrier((attn_come, first_come, da_last))[:2]
    attn = Chain(None, 1)
    attn.pieces = (da_last, first_come, attn_come)
    both.add(da_last)
    gain_part = sum(g[:, 0].sum(0) for g in (gain_oth, gain_first, gain_last))[None] / attn_gain
    small = lax.concatenate([sums[:4], gain_part], 0)
    first_bit, last_bit = far[:2]

    def quarter(piece, by_first, by_last):
        at = 2 * (bit_of("dp", first_bit) ^ by_first) + (bit_of("dp", last_bit) ^ by_last)
        size = piece.shape[1] // 4
        return lax.dynamic_slice_in_dim(piece, at * size, size, 1)

    sent = both.send(far[2])
    sent_x = after(attn.total(lambda p: quarter(p, 1, 0)), sent)
    sent_z = attn.total(lambda p: quarter(p, 0, 1))
    sent_d = attn.total(lambda p: quarter(p, 1, 1))
    kept = attn.total(lambda p: quarter(p, 0, 0))
    come_x = swap(sent_x, "dp", first_bit)
    come_z = swap(sent_z, "dp", last_bit)
    come_d = swap_diagonal(sent_d, first_bit, last_bit)
    small_sent = after(small, sent_x, sent_z, sent_d)
    small_come = swap(small_sent, "mp", 1)
    grad_input = input_grad(
        tokens,
        after(grad_hidden, small_sent),
        attn_gain,
        (g_oth, g_own_first, g_own_last),
        (oth[0], own[0]),
    )
    come_x, come_z, come_d, small_come = lax.optimization_barrier(
        (come_x, come_z, come_d, small_come, grad_input)
    )[:4]
    ride = Ride(small_sent + small_come)
    total = sum(part.astype(F32) for part in (kept, come_x, come_z, come_d)).astype(BF16)
    ffn_x = ffn_z = None
    for bit in far[2:]:
        sent = ride.below(total)
        come = swap(sent, "dp", bit)
        if bit == far[2]:
            ffn_sent = add_low(both.sent, after(both.come, sent))
            for far_bit in far[3:]:
                ffn_sent = add_low(ffn_sent, swap(ffn_sent, "dp", far_bit))
            ffn_x = swap(ffn_sent, "dp", first_bit)
            ffn_z = swap(ffn_sent, "dp", last_bit)
            ffn_d = swap_diagonal(ffn_sent, first_bit, last_bit)
            come = after(come, ffn_sent)
        total = add_low(total, ride.add(come, total))
    sent = ride.below(total)
    come_x = swap(sent, "dp", first_bit)
    come_z = swap(sent, "dp", last_bit)
    come_d = swap_diagonal(sent, first_bit, last_bit)
    come_x, come_z, come_d, ffn_x, ffn_z, ffn_d = lax.optimization_barrier(
        (come_x, come_z, come_d, ffn_x, ffn_z, ffn_d)
    )
    flat = total.reshape(-1, width)
    parts = [ride.add(come, flat) for come in (come_x, come_z, come_d)]
    shape = total.shape
    total = join_four(
        flat.reshape(shape).swapaxes(0, 1),
        *[part.reshape(shape).swapaxes(0, 1) for part in parts],
        far[0],
        far[1],
    )
    total = total.reshape(-1, *shape[:1], width).swapaxes(0, 1)
    sent = ride.below(total)
    come = swap(sent, "dp", 1)
    ffn_total = after(join_four(ffn_sent, ffn_x, ffn_z, ffn_d, far[0], far[1]), sent)
    ffn_come = swap(ffn_total, "dp", 1)
    grads = finish(
        (ffn_total, ffn_come),
        (total, come),
        ride.rows,
        count * dp * lax.axis_size("mp"),
    )
    gain_attn_sum, gain_ffn_sum, gate_sum, mean, histogram = grads[6:]
    return (
        result,
        grad_input,
        *grads[:6],
        gain_attn_sum.reshape(width),
        gain_ffn_sum.reshape(width),
        gate_sum.reshape(width),
        mean.reshape(()),
        histogram.reshape(BINS),
    )


def solution(mesh):
    in_specs = (
        P(("dp", "mp"), None, None),
        P("dp", None, None),
        P(("dp", "mp"), None, None, None),
        P(("dp", "mp"), None, None),
        P("dp"),
        P(),
        P(None, "mp"),
        P(None, "mp"),
        P(None, "mp"),
        P("mp", None),
        P(None, "mp"),
        P("mp", None),
        P(),
        P(),
        P(),
        P(("dp", "mp"), None, None),
    )
    out_specs = (
        P(("dp", "mp"), None, None),
        P(("dp", "mp"), None, None),
        P(None, "mp"),
        P(None, "mp"),
        P(None, "mp"),
        P("mp", None),
        P(None, "mp"),
        P("mp", None),
        P(),
        P(),
        P(),
        P(),
        P(),
    )
    return jax.shard_map(shards, mesh=mesh, in_specs=in_specs, out_specs=out_specs, check_vma=False)
```

```python
import functools

import jax
import jax.numpy as jnp
from jax import lax
from jax.experimental import pallas as pl
from jax.experimental.pallas import tpu as pltpu
from jax.sharding import PartitionSpec as P

HEAD = 64
NEIGH = 4
BINS = 128
PAIR = 2 * HEAD
QROWS = 256
TILE = 256
GROUP = 64

EPS = 1e-05
BF16 = jnp.bfloat16
F32 = jnp.float32
VMEM_LIMIT = 56 * 1024 * 1024
FORWARD_VMEM = 52 * 1024 * 1024
BACKWARD_VMEM = 48 * 1024 * 1024
INPUT_VMEM = 40 * 1024 * 1024
FINISH_VMEM = 24 * 1024 * 1024


def dot(left, right, left_dim=1, right_dim=0):
    return lax.dot_general(
        left, right, (((left_dim,), (right_dim,)), ((), ())), preferred_element_type=F32
    )


def normalize(values):
    centre = values - jnp.mean(values, -1, keepdims=True)
    spread = jnp.mean(centre * centre, -1, keepdims=True)
    rstd = lax.rsqrt(spread + EPS)
    return centre * rstd, rstd


def core_index():
    return lax.rem(lax.axis_index("dp"), 2)


def head_lanes(rows, head):
    lane = lax.broadcasted_iota(jnp.int32, (rows, PAIR), 1)
    return (lane >= head * HEAD) & (lane < (head + 1) * HEAD)


def only_head(block, head):
    return jnp.where(head_lanes(block.shape[0], head), block, jnp.zeros_like(block))


def attend(qkv_ref, p_ref, ctx_ref, length, with_memory):
    values = [only_head(qkv_ref[0, 0, pl.ds(3 * length, 2 * length), :], head) for head in range(2)]
    low = 0 if with_memory else length
    for first in range(0, length, QROWS):
        rows = pl.ds(first, QROWS)
        high = length + first + QROWS
        total = None
        for head in range(2):
            query = only_head(qkv_ref[0, 0, rows, :], head)
            scores = dot(query, qkv_ref[0, 0, pl.ds(length + low, high - low), :], 1, 1)
            seg = scores[:, length - low :]
            at = lax.broadcasted_iota(jnp.int32, seg.shape, 0) + first
            key = lax.broadcasted_iota(jnp.int32, seg.shape, 1)
            seg = jnp.where(key <= at, seg, -1e30)
            top = jnp.max(seg, -1, keepdims=True)
            if with_memory:
                mem = scores[:, :length]
                top = jnp.maximum(top, jnp.max(mem, -1, keepdims=True))
                mem = jnp.exp(mem - top)
            probs = jnp.exp(seg - top)
            mass = jnp.sum(probs, -1, keepdims=True)
            if with_memory:
                mass = mass + jnp.sum(mem, -1, keepdims=True)
            part = 1.0 / mass
            probs = (probs * part).astype(BF16)
            if with_memory:
                probs = jnp.concatenate([(mem * part).astype(BF16), probs], 1)
            p_ref[0, 0, head, rows, pl.ds(low, high - low)] = probs
            add = dot(probs, values[head][low:high])
            total = add if total is None else total + add
        ctx_ref[0, rows, :] = total.astype(BF16)


def forward_body(starts_ref, kv_ref, pack_ref, qkv_ref, p_ref, ctx_ref):
    length = kv_ref.shape[1] // 2
    pair = pl.program_id(1)
    kv = kv_ref[0]
    here = pl.multiple_of(3 * pair * PAIR, PAIR)
    query = dot(kv[length:], pack_ref[:, pl.ds(here, PAIR)]).astype(BF16)
    qkv_ref[0, 0, pl.ds(0, length), :] = (query.astype(F32) * HEAD ** (-0.5)).astype(BF16)
    both = dot(kv, pack_ref[:, pl.ds(here + PAIR, 2 * PAIR)]).astype(BF16)
    qkv_ref[0, 0, pl.ds(length, 2 * length), :] = both[:, :PAIR]
    qkv_ref[0, 0, pl.ds(3 * length, 2 * length), :] = both[:, PAIR:]
    start = starts_ref[lax.axis_index("mp") * pl.num_programs(0) + pl.program_id(0)]

    @pl.when(start == 0)
    def _():
        attend(qkv_ref, p_ref, ctx_ref, length, True)

    @pl.when(start != 0)
    def _():
        attend(qkv_ref, p_ref, ctx_ref, length, False)


def first_forward(
    starts_ref, tok_ref, mem_ref, gain_ref, wq_ref, wk_ref, wv_ref, kv_ref, pack_ref, *outs
):
    length = tok_ref.shape[1]

    @pl.when((pl.program_id(0) == 0) & (pl.program_id(1) == 0))
    def _():
        for i, weight in enumerate((wq_ref, wk_ref, wv_ref)):
            for p in range(2):
                pack_ref[:, pl.ds((3 * p + i) * PAIR, PAIR)] = weight[:, pl.ds(p * PAIR, PAIR)]

    @pl.when(pl.program_id(1) == 0)
    def _():
        gain = gain_ref[...]
        kv_ref[0, pl.ds(0, length), :] = (normalize(mem_ref[0].astype(F32))[0] * gain).astype(BF16)
        kv_ref[0, pl.ds(length, length), :] = (
            normalize(tok_ref[0].astype(F32))[0] * gain
        ).astype(BF16)

    forward_body(starts_ref, kv_ref, pack_ref, *outs)


def second_forward(starts_ref, kv_ref, mine_ref, sibling_ref, pack_ref, *outs):
    rows = mine_ref.shape[0]
    core = core_index()

    @pl.when((pl.program_id(0) == 0) & (pl.program_id(1) == 0))
    def _():
        for block, which in ((mine_ref, core), (sibling_ref, 1 - core)):
            to = pl.ds(pl.multiple_of(which * rows, rows), rows)
            for i in range(3):
                for p in range(2):
                    pack_ref[to, pl.ds((3 * p + i) * PAIR, PAIR)] = block[
                        :, pl.ds((2 * i + p) * PAIR, PAIR)
                    ]

    forward_body(starts_ref, kv_ref, pack_ref, *outs)


def attention_forward(starts, tokens, memory, gain, kv, weights):
    rows, length, width = tokens.shape
    pairs = 2
    pack = (width, 3 * pairs * PAIR)
    outs = [
        jax.ShapeDtypeStruct(pack, BF16),
        jax.ShapeDtypeStruct((rows, pairs, 5 * length, PAIR), BF16),
        jax.ShapeDtypeStruct((rows, pairs, 2, length, 2 * length), BF16),
        jax.ShapeDtypeStruct((rows, length, pairs * PAIR), BF16),
    ]
    out_specs = [
        pl.BlockSpec(pack, lambda r, p: (0, 0)),
        pl.BlockSpec((1, 1, 5 * length, PAIR), lambda r, p: (r, p, 0, 0)),
        pl.BlockSpec((1, 1, 2, length, 2 * length), lambda r, p: (r, p, 0, 0, 0)),
        pl.BlockSpec((1, length, PAIR), lambda r, p: (r, 0, p)),
    ]
    kv_spec = pl.BlockSpec((1, 2 * length, width), lambda r, p: (r, 0, 0))
    in_specs = [pl.BlockSpec(memory_space=pltpu.SMEM)]
    if kv is None:
        body = first_forward
        ins = [tokens, memory, gain]
        in_specs += [
            pl.BlockSpec((1, length, width), lambda r, p: (r, 0, 0)),
            pl.BlockSpec((1, length, width), lambda r, p: (lax.axis_index("mp") * rows + r, 0, 0)),
            pl.BlockSpec((1, width), lambda r, p: (0, 0)),
        ]
        outs = [jax.ShapeDtypeStruct((rows, 2 * length, width), BF16)] + outs
        out_specs = [kv_spec] + out_specs
    else:
        body = second_forward
        ins = [kv]
        in_specs += [kv_spec]
    in_specs += [pl.BlockSpec(w.shape, lambda r, p: (0, 0)) for w in weights]
    return pl.pallas_call(
        body,
        grid=(rows, pairs),
        in_specs=in_specs,
        out_specs=out_specs,
        out_shape=outs,
        compiler_params=pltpu.CompilerParams(vmem_limit_bytes=FORWARD_VMEM),
        cost_estimate=pl.CostEstimate(flops=6 * 10**9, bytes_accessed=16 * 2**20, transcendentals=0),
    )(starts, *ins, *weights)


def gelu_parts(pre):
    c0 = 0.7978845608028654
    c1 = c0 * 0.044715
    square = pre * pre
    part = 0.5 * jnp.tanh(pre * (c1 * square + c0)) + 0.5
    act = pre * part
    return act, part + act * (1.0 - part) * ((6.0 * c1) * square + 2.0 * c0)


def weighted(weights, values):
    return sum(w * v for w, v in zip(weights[1:], values[1:])) + weights[0] * values[0]


def middle_body(
    tok_ref,
    ctx_own_ref,
    ctx_oth_ref,
    nb_ref,
    ids_ref,
    cot_ref,
    up_far,
    down_far,
    out_far,
    mine_far,
    sibling_far,
    edges_ref,
    gain_ref,
    wgate_ref,
    result_ref,
    grad_hidden_ref,
    gctx_own_ref,
    gctx_oth_ref,
    sent_up_far,
    sent_down_far,
    kept_up_far,
    kept_down_far,
    sums_ref,
    e_ref,
    hist_ref,
    edge_ref,
    pick_ref,
    up_ref,
    down_ref,
    out_ref,
    oth_ref,
    stage_ref,
    ffn_in_ref,
    act_ref,
    gpre_ref,
    cots_ref,
    low_ref,
    ctx_ref,
    in_sems,
    out_sems,
):
    step = pl.program_id(0)
    here = pl.ds(pl.multiple_of(step * TILE, TILE), TILE)
    width = tok_ref.shape[-1]
    hidden_units = down_ref.shape[0]
    half = width // 2
    chunks = hidden_units // width
    scale = width ** (-0.5)
    core = core_index()
    copies = [
        pltpu.make_async_copy(far, near, in_sems.at[i])
        for i, (far, near) in enumerate(
            (
                (out_far, out_ref),
                (mine_far, oth_ref.at[core]),
                (sibling_far, oth_ref.at[1 - core]),
                (up_far, up_ref),
                (down_far, down_ref),
            )
        )
    ]

    @pl.when(step == 0)
    def _():
        for copy in copies:
            copy.start()
        sums_ref[...] = jnp.zeros_like(sums_ref)
        hist_ref[...] = jnp.zeros_like(hist_ref)
        row = lax.broadcasted_iota(jnp.int32, pick_ref.shape, 0)
        column = lax.broadcasted_iota(jnp.int32, pick_ref.shape, 1)
        from_row = NEIGH * (row % GROUP) + row // GROUP
        pick_ref[...] = (column == from_row).astype(F32).astype(BF16)
        edges = edges_ref[...].astype(F32)
        for i in range(2):
            edge_ref[i] = jnp.broadcast_to(edges[:, i : i + BINS], (BINS, BINS)).T
        for copy in copies[:3]:
            copy.wait()

    def other_out():
        at = pl.ds(2 * width, half // 2)
        return jnp.concatenate([oth_ref[0, at, :], oth_ref[1, at, :]], 0)

    wgate = wgate_ref[...]
    gain = gain_ref[...]

    def front():
        ctx_ref[here, pl.ds(0, half)] = ctx_own_ref[0]
        ctx_ref[here, pl.ds(half, half)] = ctx_oth_ref[0]
        cots_ref[here, :] = cot_ref[0]
        hidden = (
            tok_ref[0].astype(F32)
            + dot(ctx_own_ref[0], out_ref[...])
            + dot(ctx_oth_ref[0], other_out())
        )
        for first in range(0, TILE, GROUP):
            mixed_rows = nb_ref[0, pl.ds(first, GROUP)].reshape(NEIGH * GROUP, width)
            planes = dot(pick_ref[...], mixed_rows)
            for k in range(NEIGH):
                e_ref[k, pl.ds(first, GROUP), :] = planes[k * GROUP : (k + 1) * GROUP]
        affinity = [
            jnp.sum(e_ref[k] * hidden, -1, keepdims=True) * scale for k in range(NEIGH)
        ]
        top = jnp.maximum(
            jnp.maximum(affinity[0], affinity[1]), jnp.maximum(affinity[2], affinity[3])
        )
        raised = [jnp.exp(a - top) for a in affinity]
        inverse = 1.0 / (raised[0] + raised[1] + raised[2] + raised[3])
        weights = [a * inverse for a in raised]
        gate = jax.nn.sigmoid(jnp.sum(hidden * wgate, -1, keepdims=True))
        recalled = weighted(weights, [e_ref[k] for k in range(NEIGH)])
        mixed = hidden + gate * recalled
        normal, rstd = normalize(mixed)
        ffn_in_ref[here, :] = (normal * gain).astype(BF16)
        return hidden, weights, gate, mixed, normal, rstd

    def other_up():
        rows = [
            jnp.concatenate([oth_ref[h, pl.ds(c * half, half), :] for c in range(chunks)], 1)
            for h in range(2)
        ]
        return jnp.concatenate(rows, 0)

    def other_down():
        return jnp.concatenate([oth_ref[c, pl.ds(width, width), :] for c in range(chunks)], 0)

    def feed():
        ffn_in = ffn_in_ref[here, :]
        cot = cot_ref[0]
        for side in range(2):
            for c in range(chunks):
                if side == 0:
                    up = up_ref[:, pl.ds(c * width, width)]
                    down = down_ref[pl.ds(c * width, width), :]
                else:
                    part = pl.ds(c * half, half)
                    up = jnp.concatenate([oth_ref[0, part, :], oth_ref[1, part, :]], 0)
                    down = oth_ref[c, pl.ds(width, width), :]
                at = pl.ds((side * chunks + c) * width, width)
                act, slope = gelu_parts(dot(ffn_in, up))
                act_ref[here, at] = act.astype(BF16)
                gpre_ref[here, at] = (dot(cot, down, 1, 1) * slope).astype(BF16)
        own = pl.ds(0, hidden_units)
        oth = pl.ds(hidden_units, hidden_units)
        down_sum = dot(act_ref[here, own], down_ref[...]) + dot(act_ref[here, oth], other_down())
        grad_sum = dot(gpre_ref[here, own], up_ref[...], 1, 1) + dot(
            gpre_ref[here, oth], other_up(), 1, 1
        )
        return down_sum, grad_sum

    def back(kept, sums):
        hidden, weights, gate, mixed, normal, rstd = kept
        down_sum, grad_sum = sums
        result_ref[0] = (mixed + down_sum).astype(BF16)
        gain_part = jnp.sum(grad_sum * normal, 0, keepdims=True)
        grad_normal = grad_sum * gain
        grad_mixed = cot_ref[0].astype(F32) + rstd * (
            grad_normal
            - jnp.mean(grad_normal, -1, keepdims=True)
            - normal * jnp.mean(grad_normal * normal, -1, keepdims=True)
        )
        pulls = [
            jnp.sum(grad_mixed * e_ref[k], -1, keepdims=True) for k in range(NEIGH)
        ]
        pulled = weighted(weights, pulls)
        gate_grad = gate * (1.0 - gate) * pulled
        grad_hidden = grad_mixed + gate_grad * wgate
        for k in range(NEIGH):
            grad_hidden = (
                grad_hidden + (scale * gate * weights[k] * (pulls[k] - pulled)) * e_ref[k]
            )
        grad_hidden_ref[0] = grad_hidden
        low = grad_hidden.astype(BF16)
        low_ref[here, :] = low
        gctx_own_ref[0] = dot(low, out_ref[...], 1, 1).astype(BF16)
        gctx_oth_ref[0] = dot(low, other_out(), 1, 1).astype(BF16)
        gate_wide = jnp.broadcast_to(gate, (TILE, BINS)).T
        low_edge = jnp.concatenate([edge_ref[0]] * (TILE // BINS), 1)
        high_edge = jnp.concatenate([edge_ref[1]] * (TILE // BINS), 1)
        mass = jnp.zeros_like(gate_wide)
        for k in range(NEIGH):
            ids = ids_ref[0, pl.ds(k, 1), :].astype(F32)
            mass = mass + jnp.where((ids >= low_edge) & (ids < high_edge), gate_wide, 0.0)
        gate_sum = jnp.sum(jnp.broadcast_to(gate, (TILE, width)), 0, keepdims=True)
        sums_ref[pl.ds(0, 1), :] += gain_part
        sums_ref[pl.ds(1, 1), :] += gate_sum
        sums_ref[pl.ds(2, 1), :] += jnp.sum(gate_grad * hidden, 0, keepdims=True)
        hist_ref[...] += mass

    kept = front()

    @pl.when(step == 0)
    def _():
        for copy in copies[3:]:
            copy.wait()

    back(kept, feed())

    @pl.when(step == pl.num_programs(0) - 1)
    def _():
        sums_ref[pl.ds(3, 1), pl.ds(0, BINS)] = jnp.sum(hist_ref[...].T, 0, keepdims=True)
        cut = sent_up_far.shape[1]
        moves = []
        for fars, which in (
            ((sent_up_far, sent_down_far), 1 - core),
            ((kept_up_far, kept_down_far), core),
        ):
            for side in range(2):
                at = pl.ds(pl.multiple_of((side * chunks + which) * width, width), width)
                here = pl.ds(pl.multiple_of((2 * side + which) * PAIR, PAIR), PAIR)
                slot = len(moves) // 3
                first = 0
                for left, right in (
                    (ffn_in_ref[...], gpre_ref[:, at]),
                    (act_ref[:, at], cots_ref[...]),
                    (ctx_ref[:, here], low_ref[...]),
                ):
                    piece = dot(left, right, 0, 0).astype(BF16)
                    stage_ref[slot, pl.ds(first, piece.shape[0]), :] = piece
                    first += piece.shape[0]
                part = cut // 2
                own = lax.rem(lax.div(lax.axis_index("dp"), 2), 2) * part
                for start, size, far, to in (
                    (0, cut, fars[0], 0),
                    (cut, part, fars[1], part - own),
                    (cut + part, part, fars[1], own),
                ):
                    move = pltpu.make_async_copy(
                        stage_ref.at[slot, pl.ds(start, size), :],
                        far.at[side, pl.ds(pl.multiple_of(to, part), size), :],
                        out_sems.at[len(moves)],
                    )
                    move.start()
                    moves.append(move)
        for move in moves:
            move.wait()


def middle_layer(tokens, ctx_own, ctx_oth, nb, ids, cot, weights, received, edges, gain, wgate):
    rows, length, width = tokens.shape
    hidden_units = weights[1].shape[0]
    steps = length // TILE
    tiles = rows * steps
    count = rows * length
    assert hidden_units == 2 * width

    def place_of(i):
        return i // steps, i % steps

    def tiled(last):
        return pl.BlockSpec((1, TILE, last), lambda i: (*place_of(i), 0))

    def whole(shape):
        return pl.BlockSpec(shape, lambda i: (0,) * len(shape))

    far = pl.BlockSpec(memory_space=pl.ANY)
    return pl.pallas_call(
        middle_body,
        grid=(tiles,),
            in_specs=[
                tiled(width),
                tiled(width // 2),
                tiled(width // 2),
                pl.BlockSpec((1, TILE, NEIGH, width), lambda i: (*place_of(i), 0, 0)),
                pl.BlockSpec(
                    (1, NEIGH, TILE), lambda i: (place_of(i)[0], 0, place_of(i)[1])
                ),
                tiled(width),
                *[far] * 5,
                whole((1, BINS + 1)),
                whole((1, width)),
                whole((1, width)),
            ],
            out_specs=[
                tiled(width),
                tiled(width),
                tiled(width // 2),
                tiled(width // 2),
                far,
                far,
                far,
                far,
                whole((8, width)),
            ],
            scratch_shapes=[
                pltpu.VMEM((NEIGH, TILE, width), F32),
                pltpu.VMEM((BINS, TILE), F32),
                pltpu.VMEM((2, BINS, BINS), F32),
                pltpu.VMEM((NEIGH * GROUP, NEIGH * GROUP), BF16),
                *[pltpu.VMEM(w.shape, BF16) for w in weights],
                pltpu.VMEM((2, *received[0].shape), BF16),
                pltpu.VMEM((4, 2 * width + PAIR, width), BF16),
                pltpu.VMEM((count, width), BF16),
                pltpu.VMEM((count, 2 * hidden_units), BF16),
                pltpu.VMEM((count, 2 * hidden_units), BF16),
                pltpu.VMEM((count, width), BF16),
                pltpu.VMEM((count, width), BF16),
                pltpu.VMEM((count, width), BF16),
                pltpu.SemaphoreType.DMA((5,)),
                pltpu.SemaphoreType.DMA((12,)),
            ],
        out_shape=[
            jax.ShapeDtypeStruct((rows, length, width), BF16),
            jax.ShapeDtypeStruct((rows, length, width), F32),
            jax.ShapeDtypeStruct((rows, length, width // 2), BF16),
            jax.ShapeDtypeStruct((rows, length, width // 2), BF16),
            *[jax.ShapeDtypeStruct((2, width + PAIR // 2, width), BF16)] * 4,
            jax.ShapeDtypeStruct((8, width), F32),
        ],
        compiler_params=pltpu.CompilerParams(vmem_limit_bytes=VMEM_LIMIT),
        cost_estimate=pl.CostEstimate(flops=15 * 10**9, bytes_accessed=30 * 2**20, transcendentals=0),
    )(tokens, ctx_own, ctx_oth, nb, ids, cot, *weights, *received, edges, gain, wgate)


def attend_back(
    head, qkv_ref, p_ref, gctx_ref, ctx_ref, ds_ref, dq_ref, t_ref, dk_ref, dv_ref, with_memory
):
    length = ctx_ref.shape[1]
    grad = only_head(gctx_ref[0], head)
    delta = jnp.sum(grad.astype(F32) * ctx_ref[0].astype(F32), -1, keepdims=True)
    keys = only_head(qkv_ref[0, 0, pl.ds(length, 2 * length), :], head)
    lanes = pl.ds(pl.multiple_of(head * HEAD, HEAD), HEAD)
    low = 0 if with_memory else length
    for first in range(0, length, QROWS):
        rows = pl.ds(first, QROWS)
        high = length + first + QROWS
        here = pl.ds(low, high - low)
        probs = p_ref[0, 0, 0, rows, here].astype(F32)
        values = qkv_ref[0, 0, pl.ds(3 * length + low, high - low), :]
        grad_probs = dot(grad[first : first + QROWS], values, 1, 1)
        ds = (probs * (grad_probs - delta[first : first + QROWS])).astype(BF16)
        ds_ref[rows, here] = ds
        dq_ref[rows, :] += dot(ds, keys[low:high])
    for out_ref, left, right in (
        (dk_ref, t_ref[0, lanes, :], ds_ref),
        (dv_ref, t_ref[1, lanes, :], p_ref.at[0, 0, 0]),
    ):
        if not with_memory:
            out_ref[lanes, :length] = jnp.zeros((HEAD, length), BF16)
        for first in range(0, length, QROWS):
            start = low if first == 0 else length + first
            here = pl.ds(start, length + first + QROWS - start)
            out_ref[lanes, here] = dot(
                left[:, first:], right[pl.ds(first, length - first), here]
            ).astype(BF16)


def backward_body(
    starts_ref,
    qkv_ref,
    p_ref,
    gctx_ref,
    ctx_ref,
    kv_far,
    pack_ref,
    grads_ref,
    dw_ref,
    gain_ref,
    ds_ref,
    dq_ref,
    t_ref,
    dk_ref,
    dv_ref,
    acc_ref,
    kv_ref,
    sem,
):
    length = ctx_ref.shape[1]
    row = pl.program_id(1)
    head = pl.program_id(2)
    start = starts_ref[lax.axis_index("mp") * pl.num_programs(1) + row]
    fetch = pltpu.make_async_copy(kv_far.at[row], kv_ref, sem)
    args = (qkv_ref, p_ref, gctx_ref, ctx_ref, ds_ref, dq_ref, t_ref, dk_ref, dv_ref)

    @pl.when(head == 0)
    def _():
        fetch.start()
        dq_ref[...] = jnp.zeros_like(dq_ref)
        t_ref[0] = qkv_ref[0, 0, pl.ds(0, length), :].T
        t_ref[1] = gctx_ref[0].T

    @pl.when(start == 0)
    def _():
        attend_back(head, *args, True)

    @pl.when(start != 0)
    def _():
        attend_back(head, *args, False)

    @pl.when(head == 1)
    def _():
        dq_t = (dq_ref[...] * HEAD ** (-0.5)).astype(BF16).T
        grads_ref[0, 0, pl.ds(0, PAIR), :] = dq_t
        grads_ref[0, 0, pl.ds(PAIR, PAIR), :] = dk_ref[:, length:]
        grads_ref[0, 0, pl.ds(2 * PAIR, PAIR), :] = dv_ref[:, length:]
        fetch.wait()
        for i, add in enumerate(
            (
                dot(dq_t, kv_ref[pl.ds(length, length), :]),
                dot(dk_ref[...], kv_ref[...]),
                dot(dv_ref[...], kv_ref[...]),
            )
        ):
            acc_ref[i] = jnp.where(row == 0, add, acc_ref[i] + add)

    @pl.when((head == 1) & (row == pl.num_programs(1) - 1))
    def _():
        part = None
        for i in range(3):
            total = acc_ref[i]
            dw_ref[0, i] = total.astype(BF16)
            weight = pack_ref[:, pl.ds(i * PAIR, PAIR)].T.astype(F32)
            add = jnp.sum(total * weight, 0, keepdims=True)
            part = add if part is None else part + add
        gain_ref[0] = jnp.broadcast_to(part, gain_ref.shape[1:])


def attention_backward(starts, saved, gctx, kv, shift, many):
    pack, qkv, p, ctx = saved
    rows, _, _, length, _ = p.shape
    width = kv.shape[-1]

    def pair(n):
        return lax.rem(core_index() + shift + n, 2)

    return pl.pallas_call(
        backward_body,
        grid=(many, rows, 2),
        in_specs=[
            pl.BlockSpec(memory_space=pltpu.SMEM),
            pl.BlockSpec((1, 1, 5 * length, PAIR), lambda n, r, h: (r, pair(n), 0, 0)),
            pl.BlockSpec((1, 1, 1, length, 2 * length), lambda n, r, h: (r, pair(n), h, 0, 0)),
            pl.BlockSpec((1, length, PAIR), lambda n, r, h: (r, 0, pair(n))),
            pl.BlockSpec((1, length, PAIR), lambda n, r, h: (r, 0, pair(n))),
            pl.BlockSpec(memory_space=pl.ANY),
            pl.BlockSpec((width, 3 * PAIR), lambda n, r, h: (0, pair(n))),
        ],
        out_specs=[
            pl.BlockSpec((1, 1, 3 * PAIR, length), lambda n, r, h: (n, r, 0, 0)),
            pl.BlockSpec((1, 3, PAIR, width), lambda n, r, h: (n, 0, 0, 0)),
            pl.BlockSpec((1, 8, width), lambda n, r, h: (n, 0, 0)),
        ],
        scratch_shapes=[
            pltpu.VMEM((length, 2 * length), BF16),
            pltpu.VMEM((length, PAIR), F32),
            pltpu.VMEM((2, PAIR, length), BF16),
            pltpu.VMEM((PAIR, 2 * length), BF16),
            pltpu.VMEM((PAIR, 2 * length), BF16),
            pltpu.VMEM((3, PAIR, width), F32),
            pltpu.VMEM((2 * length, width), BF16),
            pltpu.SemaphoreType.DMA,
        ],
        out_shape=[
            jax.ShapeDtypeStruct((many, rows, 3 * PAIR, length), BF16),
            jax.ShapeDtypeStruct((many, 3, PAIR, width), BF16),
            jax.ShapeDtypeStruct((many, 8, width), F32),
        ],
        compiler_params=pltpu.CompilerParams(vmem_limit_bytes=BACKWARD_VMEM),
        cost_estimate=pl.CostEstimate(
            flops=4 * 10**9 * many, bytes_accessed=8 * 2**20 * many, transcendentals=0
        ),
    )(starts, qkv, p, gctx, ctx, kv, pack)


def input_body(
    tok_ref,
    grad_hidden_ref,
    gain_ref,
    oth_ref,
    own_first_ref,
    own_last_ref,
    oth_pack_ref,
    own_pack_ref,
    out_ref,
):
    core = core_index()
    total = None
    for block, pack, which in (
        (oth_ref[0, 0], oth_pack_ref, 1 - core),
        (oth_ref[1, 0], oth_pack_ref, core),
        (own_first_ref[0, 0], own_pack_ref, 1 - core),
        (own_last_ref[0, 0], own_pack_ref, core),
    ):
        here = pl.ds(pl.multiple_of(which * 3 * PAIR, 3 * PAIR), 3 * PAIR)
        add = dot(block, pack[:, here], 0, 1)
        total = add if total is None else total + add
    normal, rstd = normalize(tok_ref[0].astype(F32))
    grad = total * gain_ref[...]
    out_ref[0] = (
        grad_hidden_ref[0]
        + rstd
        * (
            grad
            - jnp.mean(grad, -1, keepdims=True)
            - normal * jnp.mean(grad * normal, -1, keepdims=True)
        )
    ).astype(BF16)


def input_grad(tokens, grad_hidden, gain, grads, packs):
    rows, length, width = tokens.shape
    row = pl.BlockSpec((1, length, width), lambda r: (r, 0, 0))

    def whole(array):
        return pl.BlockSpec(array.shape, lambda r: (0, 0))

    return pl.pallas_call(
        input_body,
        grid=(rows,),
        in_specs=[
            row,
            row,
            whole(gain),
            *[pl.BlockSpec((g.shape[0], 1) + g.shape[2:], lambda r: (0, r, 0, 0)) for g in grads],
            *[whole(p) for p in packs],
        ],
        out_specs=row,
        out_shape=jax.ShapeDtypeStruct(tokens.shape, BF16),
        compiler_params=pltpu.CompilerParams(vmem_limit_bytes=INPUT_VMEM),
        cost_estimate=pl.CostEstimate(flops=2 * 10**9, bytes_accessed=8 * 2**20, transcendentals=0),
    )(tokens, grad_hidden, gain, *grads, *packs)


def finish_body(
    ffn_mine,
    ffn_sibling,
    attn_mine,
    attn_sibling,
    small_ref,
    q_far,
    k_far,
    v_far,
    out_far,
    up_far,
    down_far,
    gain_attn_ref,
    gain_ffn_ref,
    gate_ref,
    mean_ref,
    hist_ref,
    q_ref,
    k_ref,
    v_ref,
    out_ref,
    up_ref,
    down_ref,
    sems,
    tokens,
):
    core = core_index()
    width = up_far.shape[0]
    rows = attn_mine.shape[1]
    moves = []

    def pair(mine, sibling):
        return (
            jnp.where(core == 0, mine, sibling).astype(F32),
            jnp.where(core == 0, sibling, mine).astype(F32),
        )

    def move(near, far):
        moves.append(pltpu.make_async_copy(near, far, sems.at[len(moves)]))
        moves[-1].start()

    size = ffn_mine.shape[1] // 2
    pieces = [(x, pl.ds(y * size, size)) for y in range(2) for x in range(2)]
    halves = zip(*(pair(ffn_mine[x, y, :], ffn_sibling[x, y, :]) for x, y in pieces))
    for which, parts in enumerate(halves):
        rows_of = jnp.concatenate(parts, 0)
        to = pl.ds(which * width, width)
        up_ref[:, to] = rows_of[:width]
        down_ref[to, :] = rows_of[width : 2 * width]
        out_ref[pl.ds(which * PAIR, PAIR), :] = rows_of[2 * width :]
        move(down_ref.at[to, :], down_far.at[to, :])
    move(up_ref, up_far)
    move(out_ref, out_far)
    for i, (near, far) in enumerate(((q_ref, q_far), (k_ref, k_far), (v_ref, v_far))):
        first, last = pair(attn_mine[i], attn_sibling[pl.ds(i * rows, rows), :])
        near[...] = jnp.concatenate([first, last], 0).T
        move(near, far)
    count = small_ref.shape[0]
    below = attn_sibling[pl.ds(3 * rows, -(-3 * count // 16) * 16), :].astype(F32)
    small = small_ref[...]
    for i in range(3):
        small = small + below[i * count : (i + 1) * count]
    gain_ffn_ref[...] = small[0:1]
    mean_ref[...] = small[1:2, 0:1] / tokens
    gate_ref[...] = small[2:3]
    hist_ref[...] = small[3:4, :BINS] * (BINS / (tokens * NEIGH))
    gain_attn_ref[...] = small[4:5]
    for one in moves:
        one.wait()


def finish(ffn, attn, small, tokens):
    width = ffn[0].shape[-1]
    quarter = attn[0].shape[1]
    shapes = [(width, 2 * quarter)] * 3
    shapes += [(2 * quarter, width), (width, 2 * width), (2 * width, width)]
    rows = [(1, width)] * 3 + [(1, 1), (1, BINS)]

    def whole(array):
        return pl.BlockSpec(array.shape, lambda i: (0,) * array.ndim)

    return pl.pallas_call(
        functools.partial(finish_body, tokens=tokens),
        grid=(1,),
        in_specs=[whole(a) for a in (*ffn, *attn, small)],
        out_specs=[pl.BlockSpec(memory_space=pl.ANY)] * 6
        + [pl.BlockSpec(s, lambda i: (0, 0)) for s in rows],
        scratch_shapes=[pltpu.VMEM(s, F32) for s in shapes] + [pltpu.SemaphoreType.DMA((8,))],
        out_shape=[jax.ShapeDtypeStruct(s, F32) for s in shapes + rows],
        compiler_params=pltpu.CompilerParams(vmem_limit_bytes=FINISH_VMEM),
    )(*ffn, *attn, small)


def swap(array, axis, bit):
    size = lax.axis_size(axis)
    return lax.ppermute(array, axis, [(i, i ^ bit) for i in range(size)])


def bit_of(axis, bit):
    return (lax.axis_index(axis) // bit) % 2


def part_of(array, which, dim):
    half = array.shape[dim] // 2
    return lax.dynamic_slice_in_dim(array, which * half, half, dim)


def add_low(left, right):
    return (left.astype(F32) + right.astype(F32)).astype(BF16)


def join(mine, other, bit, dim):
    return jnp.where(
        bit_of("dp", bit) == 0,
        lax.concatenate([mine, other], dim),
        lax.concatenate([other, mine], dim),
    )


def swap_diagonal(array, first, last):
    size = lax.axis_size("dp")
    return lax.ppermute(array, "dp", [(i, i ^ first ^ last) for i in range(size)])


def join_four(mine, by_first, by_last, by_both, first, last):
    return join(
        join(mine, by_last, last, 0)[None], join(by_first, by_both, last, 0)[None], first, 0
    )


def after(value, *others):
    return lax.optimization_barrier((value, *others))[0]


class Chain:
    def __init__(self, array, dim):
        self.pieces = (array,)
        self.dim = dim

    def total(self, cut=lambda piece: piece):
        pieces = [cut(piece) for piece in self.pieces]
        if len(pieces) == 1:
            return pieces[0]
        return sum(piece.astype(F32) for piece in pieces).astype(BF16)

    def pass_on(self, sent, kept, bit, *others):
        self.sent = after(sent, *others)
        self.kept = kept
        self.come = swap(self.sent, "dp", bit)
        return self.sent

    def halve(self, bit, *others):
        mine = bit_of("dp", bit)
        self.sent = after(self.total(lambda p: part_of(p, 1 - mine, self.dim)), *others)
        self.kept = self.total(lambda p: part_of(p, mine, self.dim))
        self.come = swap(self.sent, "dp", bit)
        return self.sent

    def first_half(self, bit, *others):
        half = self.pieces[0].shape[self.dim] // 2
        self.sent = after(
            self.total(lambda p: lax.slice_in_dim(p, 0, half, axis=self.dim)), *others
        )
        self.kept = self.total(lambda p: lax.slice_in_dim(p, half, 2 * half, axis=self.dim))
        self.come = swap(self.sent, "dp", bit)
        return self.sent

    def give(self, index, *others):
        self.sent = after(self.total(lambda p: p[index]), *others)
        self.kept = self.total(lambda p: p[1 - index])
        self.dim -= 1
        self.come = swap(self.sent, "mp", 1)
        return self.sent

    def send(self, bit, *others):
        self.sent = self.kept = after(self.total(), *others)
        self.come = swap(self.sent, "dp", bit)
        return self.sent

    def add(self, *others):
        self.come = after(self.come, *others)
        self.pieces = (self.kept, self.come)

    def join(self, bit, *others):
        self.pieces = (join(self.sent, after(self.come, *others), bit, self.dim),)


class Ride:
    def __init__(self, rows):
        self.rows = rows

    def below(self, array):
        left = self.rows
        parts = [array.reshape(-1, array.shape[-1])]
        for _ in range(3):
            part = lax.reduce_precision(left, 8, 7)
            parts.append(part.astype(BF16))
            left = left - part
        spare = -3 * left.shape[0] % 16
        parts.append(jnp.zeros((spare, left.shape[1]), BF16))
        return lax.concatenate(parts, 0)

    def add(self, block, like):
        size = like.size // like.shape[-1]
        count = self.rows.shape[0]
        for i in range(3):
            at = size + i * count
            self.rows = self.rows + block[at : at + count].astype(F32)
        return block[:size].reshape(like.shape)


def shards(
    tokens,
    memory,
    neighbours,
    neighbour_ids,
    doc_starts,
    bin_edges,
    w_query,
    w_key,
    w_value,
    w_out,
    w_up,
    w_down,
    gain_attn,
    gain_ffn,
    w_gate,
    cotangent,
):
    rows, length, width = tokens.shape
    count = rows * length
    dp = lax.axis_size("dp")
    core = bit_of("dp", 1)
    attn_gain = gain_attn.reshape(1, width)
    qkv = (w_query, w_key, w_value)
    far = []
    bit = 2
    while bit < dp:
        far.append(bit)
        bit *= 2

    qkv_sent = lax.concatenate([part_of(w, core, 0) for w in qkv], 1)
    up_part = part_of(w_up, core, 0)
    ffn_sent = lax.concatenate(
        [up_part[:, :width], up_part[:, width:], part_of(w_down, core, 0), part_of(w_out, core, 0)],
        0,
    )
    qkv_mine = swap(qkv_sent, "mp", 1)
    ffn_mine = swap(after(ffn_sent, qkv_sent), "mp", 1)
    kv, *own = attention_forward(
        doc_starts, after(tokens, qkv_sent, ffn_sent), memory, attn_gain, None, qkv
    )
    qkv_mine = after(qkv_mine, kv)
    qkv_got = (qkv_mine, swap(qkv_mine, "dp", 1))
    oth = attention_forward(doc_starts, tokens, memory, attn_gain, kv, qkv_got)
    ffn_mine = after(ffn_mine, oth[3])
    ffn_got = (ffn_mine, swap(ffn_mine, "dp", 1))
    ids = jnp.swapaxes(neighbour_ids, 1, 2)
    edges = bin_edges.reshape(1, BINS + 1)
    (
        result,
        grad_hidden,
        gctx_own,
        gctx_oth,
        sent_up,
        sent_down,
        kept_up,
        kept_down,
        sums,
    ) = middle_layer(
        tokens,
        own[3],
        oth[3],
        neighbours,
        ids,
        cotangent,
        (w_up, w_down, w_out),
        ffn_got,
        edges,
        gain_ffn.reshape(1, width),
        w_gate.reshape(1, width),
    )
    up = Chain(None, 1)
    down = Chain(None, 1)
    up.pass_on(sent_up, kept_up, 1)
    down.pass_on(sent_down, kept_down, 1)
    up.add()
    down.add()
    sent = up.give(1)
    sent = down.first_half(far[0], sent)
    g_oth, da, gain_oth = attention_backward(
        doc_starts, oth, after(gctx_oth, sent), kv, 1, 2
    )
    up.add(da)
    down.add(da)
    sent = up.halve(far[0])
    sent = down.give(1, sent)
    attn = Chain(None, 1)
    sent = attn.pass_on(da[0], da[1], 1, sent)
    g_own_first, da_first, gain_first = attention_backward(
        doc_starts, own, after(gctx_own, sent), kv, 1, 1
    )
    da_first = da_first[0]
    attn.add(da_first)
    up.add(da_first)
    down.add(da_first)
    both = Chain(None, 0)
    both.pieces = tuple(lax.concatenate([u, d], 0) for u, d in zip(up.pieces, down.pieces))
    attn_sent = attn.total()
    attn_come = swap(attn_sent, "mp", 1)
    sent = both.halve(far[1], attn_sent)
    first_sent = after(da_first, sent)
    first_come = swap(first_sent, "dp", 1)
    g_own_last, da_last, gain_last = attention_backward(
        doc_starts, own, after(gctx_own, first_sent), kv, 0, 1
    )
    da_last = da_last[0]
    attn_come, first_come = lax.optimization_barrier((attn_come, first_come, da_last))[:2]
    attn = Chain(None, 1)
    attn.pieces = (da_last, first_come, attn_come)
    both.add(da_last)
    gain_part = sum(g[:, 0].sum(0) for g in (gain_oth, gain_first, gain_last))[None] / attn_gain
    small = lax.concatenate([sums[:4], gain_part], 0)
    first_bit, last_bit = far[:2]

    def quarter(piece, by_first, by_last):
        at = 2 * (bit_of("dp", first_bit) ^ by_first) + (bit_of("dp", last_bit) ^ by_last)
        size = piece.shape[1] // 4
        return lax.dynamic_slice_in_dim(piece, at * size, size, 1)

    sent = both.send(far[2])
    sent_x = after(attn.total(lambda p: quarter(p, 1, 0)), sent)
    sent_z = attn.total(lambda p: quarter(p, 0, 1))
    sent_d = attn.total(lambda p: quarter(p, 1, 1))
    kept = attn.total(lambda p: quarter(p, 0, 0))
    come_d = swap_diagonal(sent_d, first_bit, last_bit)
    come_z = swap(sent_z, "dp", last_bit)
    come_x = swap(sent_x, "dp", first_bit)
    small_sent = after(small, sent_x, sent_z, sent_d)
    small_come = swap(small_sent, "mp", 1)
    grad_input = input_grad(
        tokens,
        after(grad_hidden, sent_x, sent_z, sent_d),
        attn_gain,
        (g_oth, g_own_first, g_own_last),
        (oth[0], own[0]),
    )
    come_x, come_z, come_d, small_come = lax.optimization_barrier(
        (come_x, come_z, come_d, small_come, grad_input)
    )[:4]
    ride = Ride(small_sent + small_come)
    total = sum(part.astype(F32) for part in (kept, come_x, come_z, come_d)).astype(BF16)
    ffn_x = ffn_z = None
    for bit in far[2:]:
        sent = ride.below(total)
        come = swap(sent, "dp", bit)
        if bit == far[2]:
            ffn_sent = add_low(both.sent, after(both.come, sent))
            for far_bit in far[3:]:
                ffn_sent = add_low(ffn_sent, swap(ffn_sent, "dp", far_bit))
            ffn_x = swap(ffn_sent, "dp", first_bit)
            ffn_z = swap(ffn_sent, "dp", last_bit)
            ffn_d = swap_diagonal(ffn_sent, first_bit, last_bit)
            come = after(come, ffn_sent)
        total = add_low(total, ride.add(come, total))
    sent = ride.below(total)
    come_x = swap(sent, "dp", first_bit)
    come_z = swap(sent, "dp", last_bit)
    come_d = swap_diagonal(sent, first_bit, last_bit)
    come_x, come_z, come_d, ffn_x, ffn_z, ffn_d = lax.optimization_barrier(
        (come_x, come_z, come_d, ffn_x, ffn_z, ffn_d)
    )
    flat = total.reshape(-1, width)
    parts = [ride.add(come, flat) for come in (come_x, come_z, come_d)]
    shape = total.shape
    total = join_four(
        flat.reshape(shape).swapaxes(0, 1),
        *[part.reshape(shape).swapaxes(0, 1) for part in parts],
        far[0],
        far[1],
    )
    total = total.reshape(-1, *shape[:1], width).swapaxes(0, 1)
    sent = ride.below(total)
    come = swap(sent, "dp", 1)
    ffn_total = after(join_four(ffn_sent, ffn_x, ffn_z, ffn_d, far[0], far[1]), sent)
    ffn_come = swap(ffn_total, "dp", 1)
    grads = finish(
        (ffn_total, ffn_come),
        (total, come),
        ride.rows,
        count * dp * lax.axis_size("mp"),
    )
    gain_attn_sum, gain_ffn_sum, gate_sum, mean, histogram = grads[6:]
    return (
        result,
        grad_input,
        *grads[:6],
        gain_attn_sum.reshape(width),
        gain_ffn_sum.reshape(width),
        gate_sum.reshape(width),
        mean.reshape(()),
        histogram.reshape(BINS),
    )


def solution(mesh):
    in_specs = (
        P(("dp", "mp"), None, None),
        P("dp", None, None),
        P(("dp", "mp"), None, None, None),
        P(("dp", "mp"), None, None),
        P("dp"),
        P(),
        P(None, "mp"),
        P(None, "mp"),
        P(None, "mp"),
        P("mp", None),
        P(None, "mp"),
        P("mp", None),
        P(),
        P(),
        P(),
        P(("dp", "mp"), None, None),
    )
    out_specs = (
        P(("dp", "mp"), None, None),
        P(("dp", "mp"), None, None),
        P(None, "mp"),
        P(None, "mp"),
        P(None, "mp"),
        P("mp", None),
        P(None, "mp"),
        P("mp", None),
        P(),
        P(),
        P(),
        P(),
        P(),
    )
    return jax.shard_map(shards, mesh=mesh, in_specs=in_specs, out_specs=out_specs, check_vma=False)
```
